32 devices in a mesh: grp: 4 (over x, core), batch: 2 (over y), mp: 4 (over z).
Axes of the slice: x: 2, y: 2, z: 4, core: 2. Of those that a mesh axis runs over, the one named last changes fastest.
Arguments:
- rows_in: bfloat16 [56, 512, 768], P(('grp', 'batch'), 'mp'), may hold values from -6 to 6
- segment_ids: int32 [56, 512], P(('grp', 'batch')), may hold values from 0 to 3, never falling along the last dimension, each value on 1 to 256 neighbouring positions
- pair_labels: int32 [56, 4], P(('grp', 'batch')), may hold values from 0 to 13
- pair_mask: int32 [56, 4], P(('grp', 'batch')), may hold values 0 or 1
- exit_flag: int32 [56], P(('grp', 'batch')), may hold values from 0 to 1, as said below
- target: int32 [56], P(('grp', 'batch')), may hold values from 0 to 1, as said below
- cot_out: bfloat16 [64, 512, 768], P(('grp', 'batch', 'mp')), may hold values from -6 to 6
- w_qkv: bfloat16 [3, 768, 768], P(None, None, 'mp'), may hold values from -0.21875 to 0.21875
- b_qv: float32 [2, 768], P(None, 'mp'), may hold values from -3 to 3
- w_out: bfloat16 [768, 768], P('mp'), may hold values from -0.625 to 0.625
- b_out: float32 [768], replicated, may hold values from -3 to 3
- ln_gain: float32 [2, 768], replicated, may hold values from 0.25 to 1.75
- ln_bias: float32 [2, 768], replicated, may hold values from -2 to 2
- w_up: bfloat16 [768, 3072], P(None, 'mp'), may hold values from -0.21875 to 0.21875
- b_up: float32 [3072], P('mp'), may hold values from -3 to 3
- w_down: bfloat16 [3072, 768], P('mp'), may hold values from -0.109375 to 0.109375
- b_down: float32 [768], replicated, may hold values from -3 to 3
- s_w1: bfloat16 [768, 128], replicated, may hold values from -0.21875 to 0.21875
- s_bias: float32 [2, 128], replicated, may hold values from -3 to 3
- s_query: float32 [128], replicated, may hold values from -8 to 8
- s_w2: bfloat16 [128, 128], replicated, may hold values from -0.5 to 0.5
- s_w3: bfloat16 [128, 14], replicated, may hold values from -0.5 to 0.5
- s_b3: float32 [14], replicated, may hold values from -3 to 3
Outputs:
- mixed_out: bfloat16 [64, 512, 768], P(('grp', 'batch', 'mp'))
- grad_rows: bfloat16 [56, 512, 768], P(('grp', 'batch'), 'mp')
- g_wqkv: float32 [3, 768, 768], P(None, 'batch', 'mp')
- g_bqv: float32 [2, 768], P(None, ('mp', 'batch'))
- g_wout: float32 [768, 768], P('mp', 'batch')
- g_bout: float32 [768], replicated
- g_lngain: float32 [2, 768], replicated
- g_lnbias: float32 [2, 768], replicated
- g_wup: float32 [768, 3072], P('batch', 'mp')
- g_bup: float32 [3072], P(('mp', 'batch'))
- g_wdown: float32 [3072, 768], P('mp', 'batch')
- g_bdown: float32 [768], replicated
- g_sw1: float32 [768, 128], replicated
- g_sbias: float32 [2, 128], replicated
- g_squery: float32 [128], replicated
- g_sw2: float32 [128, 128], replicated
- g_sw3: float32 [128, 14], replicated
- g_sb3: float32 [14], replicated
The draws below stay inside these ranges and needn't reach their ends.
Inputs may be any that keep to these rules, and one draw needn't show every extreme that they name: `exit_flag`: 1 marks a row that has exited at an earlier layer. A batch index within the row's own group. Of one device's alive rows at most 4 name the same target, and some device sends exactly 4 to one target; of one group's alive rows at most 8 name the same target, and in every group some target receives exactly 8. `segment_ids`: each of the 4 pairs of a row is one run of positions.
All inputs are finite; a program needn't handle non-finite values. No bound on the sum of `pair_mask` on one device may be relied on, other than what follows from the above.
Results may differ from the reference program's by a relative error of at most 0.028.
Values may be sent and summed in bfloat16 or wider, within the bound.
A program may use at most 192 MiB of HBM per device.

```python
import math
import jax
import jax.numpy as jnp
import numpy as np
from jax import lax

D = 768
HEADS = 12
HEAD_DIM = 64
FF = 3072
SW = 128
CLASSES = 14
SEQ = 512
PAIRS = 4
PAIR_MOST = 256
ROWS_DEV = 7
CAP = 8
ROWS_ALL = 56
SLOTS_ALL = 64
N_GRP = 4
N_BATCH = 2
N_MP = 4


def group_plan(group_key):
    load_key, order_key, hot_key, rank_key, spare_key = jax.random.split(group_key, 5)
    load_counts = jax.random.randint(load_key, (N_BATCH,), 2, ROWS_DEV)
    hottest = jax.random.randint(hot_key, (), 0, N_BATCH)
    load_counts = jnp.where(jnp.arange(N_BATCH) == hottest, CAP, load_counts)
    load_ends = jnp.cumsum(load_counts)
    alive_total = load_ends[N_BATCH - 1]
    dest_order = jax.random.permutation(order_key, N_BATCH)

    def one_rank(rank_seed):
        return jax.random.permutation(rank_seed, ROWS_DEV)
    row_ranks = jax.vmap(one_rank)(jax.random.split(rank_key, N_BATCH))
    position = row_ranks * N_BATCH + jnp.arange(N_BATCH)[:, None]
    alive_rows = position < alive_total
    window = jnp.sum((position[:, :, None] >= load_ends[None, None, :]).astype(jnp.int32), axis=2)
    window = jnp.minimum(window, N_BATCH - 1)
    spare_goal = jax.random.randint(spare_key, (N_BATCH, ROWS_DEV), 0, N_BATCH)
    goal_rows = jnp.where(alive_rows, dest_order[window], spare_goal)
    return (alive_rows.astype(jnp.int32), goal_rows.astype(jnp.int32))


def route_plan(key):
    group_keys = jax.random.split(key, N_GRP)
    alive_rows, goal_rows = jax.vmap(group_plan)(group_keys)
    return (alive_rows.reshape(-1), goal_rows.reshape(-1))


def draw_exit_flag(key, part):
    alive_rows, goal_rows = route_plan(key)
    return (1 - alive_rows).astype(jnp.int32)


def draw_target(key, part):
    alive_rows, goal_rows = route_plan(key)
    return goal_rows.astype(jnp.int32)


def with_ends(drawn, key, least, largest):
    spot = [jax.random.randint(jax.random.fold_in(key, axis), (), 0, length) for axis, length in enumerate(drawn.shape)]
    main_axis = drawn.shape.index(max(drawn.shape))
    next_to = spot[:main_axis] + [(spot[main_axis] + 1) % drawn.shape[main_axis]] + spot[main_axis + 1:]
    return drawn.at[tuple(spot)].set(least).at[tuple(next_to)].set(largest)


def steps_of(own_key, dims, pieces, low, high):
    def one(axis_at, shards_of):
        heights = jax.random.uniform(jax.random.fold_in(jax.random.fold_in(own_key, 6), axis_at), (shards_of,), jnp.float32, low / len(pieces), high / len(pieces))
        return jnp.repeat(jnp.exp(heights), dims[axis_at] // shards_of).reshape((-1,) + (1,) * (len(dims) - axis_at - 1))

    factor_of = one(*pieces[0])
    for cut in pieces[1:]:
        factor_of = factor_of * one(*cut)
    return factor_of


def split_up(number_of, total, bound, slope):
    weights = [(1 << 20) // math.isqrt(rank ** slope) + 1 for rank in range(2, number_of + 1)]
    surplus, given = total - bound - (number_of - 1), [1] * (number_of - 1)
    while surplus > 0:
        free = [i for i in range(number_of - 1) if given[i] < bound]
        mass, left = sum([weights[i] for i in free]), surplus
        for i in free:
            addition = min(bound - given[i], max(1, left * weights[i] // mass), surplus)
            given[i] = given[i] + addition
            surplus = surplus - addition
    return np.array([bound] + given)


def uneven(own_key, number_of, total, reach, skew):
    if number_of == 2:
        one = jax.random.randint(own_key, (), max(1, total - reach), min(reach, total - 1) + 1)
        return jnp.stack([one, total - one])
    lengths = jnp.asarray(split_up(number_of, total, reach, skew), jnp.int32)
    pairs = (number_of - 1) // 2
    giver, receiver = lengths[1:1 + 2 * pairs:2], lengths[2:2 + 2 * pairs:2]
    room = jnp.minimum(giver - 1, reach - receiver)
    passed = jax.random.randint(jax.random.fold_in(own_key, 1), (pairs,), 0, 1 << 20) % (room + 1)
    lengths = lengths.at[1:1 + 2 * pairs:2].set(giver - passed).at[2:2 + 2 * pairs:2].set(receiver + passed)
    return lengths[jax.random.permutation(jax.random.fold_in(own_key, 2), number_of)]


def gaussian(key, shape, deviation, most, shards=(), kind=jnp.bfloat16):
    drawn = jax.random.normal(key, shape, jnp.float32) * deviation
    if len(shards) > 0:
        drawn = steps_of(key, shape, shards, -0.22, 0.18) * drawn
    return jnp.clip(drawn, min=-most, max=most).astype(kind)


def setup_inputs(seed: int = 0) -> dict:
    key_of = jax.random.split(jax.random.key(seed), 24)
    return {
        "rows_in": gaussian(key_of[0], (ROWS_ALL, SEQ, D), 1.0, 6.0, ((0, 8), (1, 4))),
        "segment_ids": jax.vmap(lambda own: jnp.searchsorted(jnp.cumsum(uneven(own, PAIRS, SEQ, PAIR_MOST, 1)), jnp.arange(SEQ), side="right"))(jax.random.split(key_of[1], ROWS_ALL)).reshape((ROWS_ALL, SEQ)).astype(jnp.int32),
        "pair_labels": with_ends(jax.random.randint(key_of[2], (ROWS_ALL, PAIRS), 0, CLASSES), jax.random.fold_in(key_of[2], 1), 0, CLASSES - 1).astype(jnp.int32),
        "pair_mask": with_ends((jax.random.randint(key_of[3], (ROWS_ALL, PAIRS), 0, 4) < 3).astype(jnp.int32), jax.random.fold_in(key_of[3], 1), 0, 1),
        "exit_flag": draw_exit_flag(jax.random.fold_in(key_of[23], 71), 0),
        "target": draw_target(jax.random.fold_in(key_of[23], 71), 0),
        "cot_out": gaussian(key_of[6], (SLOTS_ALL, SEQ, D), 1.0, 6.0, ((0, 32),)),
        "w_qkv": gaussian(key_of[7], (3, D, D), D ** -0.5, 0.21875, ((2, 4),)),
        "b_qv": gaussian(key_of[8], (2, D), 0.5, 3.0, ((1, 4),), jnp.float32),
        "w_out": gaussian(key_of[9], (D, D), (D // 8) ** -0.5, 0.625, ((0, 4),)),
        "b_out": gaussian(key_of[10], (D,), 0.5, 3.0, (), jnp.float32),
        "ln_gain": jnp.clip(1.0 + 0.15 * jax.random.normal(key_of[11], (2, D), jnp.float32), 0.25, 1.75),
        "ln_bias": gaussian(key_of[12], (2, D), 0.3, 2.0, (), jnp.float32),
        "w_up": gaussian(key_of[13], (D, FF), D ** -0.5, 0.21875, ((1, 4),)),
        "b_up": gaussian(key_of[14], (FF,), 0.5, 3.0, ((0, 4),), jnp.float32),
        "w_down": gaussian(key_of[15], (FF, D), FF ** -0.5, 0.109375, ((0, 4),)),
        "b_down": gaussian(key_of[16], (D,), 0.5, 3.0, (), jnp.float32),
        "s_w1": gaussian(key_of[17], (D, SW), D ** -0.5, 0.21875),
        "s_bias": gaussian(key_of[18], (2, SW), 0.5, 3.0, (), jnp.float32),
        "s_query": gaussian(key_of[19], (SW,), 2.0, 8.0, (), jnp.float32),
        "s_w2": gaussian(key_of[20], (SW, SW), SW ** -0.5, 0.5),
        "s_w3": gaussian(key_of[21], (SW, CLASSES), SW ** -0.5, 0.5),
        "s_b3": gaussian(key_of[22], (CLASSES,), 0.5, 3.0, (), jnp.float32),
    }


@jax.custom_vjp
def low(v):
    return lax.optimization_barrier(v.astype(jnp.bfloat16)).astype(jnp.float32)

@jax.custom_vjp
def low_back(v):
    return v

def low_keep(v):
    return (low(v), None)

def low_pass(kept, grad):
    return (grad,)

def back_keep(v):
    return (v, None)

def back_low(kept, grad):
    return (low(grad),)
low.defvjp(low_keep, low_pass)
low_back.defvjp(back_keep, back_low)
EPS = 1e-12
NEG = -1000000000.0
PRECISE = lax.Precision.HIGHEST

def layer_norm(resid_in, gain_vec, shift_vec):
    center = resid_in - lax.optimization_barrier(jnp.mean(resid_in, axis=-1, keepdims=True))
    spread = lax.optimization_barrier(jnp.mean(center * center, axis=-1, keepdims=True))
    return center * lax.rsqrt(spread + EPS) * gain_vec + shift_vec

def gelu_exact(pre_value):
    return jax.nn.gelu(pre_value, approximate=False)

def student_head(hidden, query_vec, w_mid, b_mid, w_cls, b_cls, seg_ids, labels, weights):
    row_total = hidden.shape[0]
    seq_len = hidden.shape[1]
    feat_dim = hidden.shape[2]
    half_dim = feat_dim // 2
    pair_count = labels.shape[-1]
    class_count = b_cls.shape[0]
    head_parts = hidden.reshape(row_total, seq_len, 2, half_dim)
    scores = jnp.einsum('bseh,eh->bse', head_parts, query_vec.reshape(2, half_dim), precision=PRECISE) * half_dim ** (-0.5)
    member = seg_ids[:, None, :] == jnp.arange(pair_count, dtype=jnp.int32)[None, :, None]
    masked = jnp.where(member[:, :, :, None], scores[:, None, :, :], NEG)
    peak_val = lax.optimization_barrier(jnp.max(masked, axis=2, keepdims=True))
    exp_terms = jnp.exp(masked - peak_val)
    shares = exp_terms / lax.optimization_barrier(jnp.sum(exp_terms, axis=2, keepdims=True))
    pooled = jnp.einsum('bpse,bseh->bpeh', shares, head_parts, precision=PRECISE).reshape(row_total, pair_count, feat_dim)
    middle = jnp.tanh(jnp.einsum('bpw,wv->bpv', pooled, w_mid, precision=PRECISE) + b_mid)
    logits = jnp.einsum('bpv,vk->bpk', middle, w_cls, precision=PRECISE) + b_cls
    top_val = lax.optimization_barrier(jnp.max(logits, axis=-1, keepdims=True))
    log_total = top_val[..., 0] + jnp.log(lax.optimization_barrier(jnp.sum(jnp.exp(logits - top_val), axis=-1)))
    chosen = lax.optimization_barrier(jnp.sum(jnp.where(labels[..., None] == jnp.arange(class_count, dtype=jnp.int32), logits, 0.0), axis=-1))
    return jnp.sum(weights * (log_total - chosen))

def row_layer(x_row, seg_row, lab_row, wt_row, params):
    w_qkv, b_qv, w_out, b_out, ln_gain, ln_bias, w_up, b_up, w_down, b_down, s_w1, s_bias, s_query, s_w2, s_w3, s_b3 = params
    seq_len = x_row.shape[0]
    model_dim = x_row.shape[1]
    group_dim = model_dim // N_MP
    inner_dim = w_up.shape[1] // N_MP
    projected = jnp.einsum('sd,jde->jse', x_row, w_qkv, precision=PRECISE)
    queries = low(low_back(projected[0] + b_qv[0])).reshape(seq_len, HEADS, HEAD_DIM)
    key_rows = low(low_back(projected[1])).reshape(seq_len, HEADS, HEAD_DIM)
    values = low(low_back(projected[2] + b_qv[1])).reshape(seq_len, HEADS, HEAD_DIM)
    scores = low_back(jnp.einsum('qhe,khe->hqk', queries, key_rows, precision=PRECISE) * HEAD_DIM ** (-0.5))
    allowed = seg_row[:, None] == seg_row[None, :]
    masked = jnp.where(allowed[None], scores, NEG)
    top_val = lax.optimization_barrier(jnp.max(masked, axis=-1, keepdims=True))
    exp_terms = jnp.exp(masked - top_val)
    prob_low = low(exp_terms / lax.optimization_barrier(jnp.sum(exp_terms, axis=-1, keepdims=True)))
    context = jnp.einsum('hqk,khe->qhe', prob_low, values, precision=PRECISE).reshape(seq_len, N_MP, group_dim)
    context = low(low_back(context))
    out_parts = low(jnp.einsum('sme,med->msd', context, w_out.reshape(N_MP, group_dim, model_dim), precision=PRECISE))
    attn_out = low_back(lax.optimization_barrier(jnp.sum(out_parts, axis=0)) + b_out)
    hidden_one = layer_norm(x_row + attn_out, ln_gain[0], ln_bias[0])
    copies = low_back(jnp.broadcast_to(low(hidden_one), (N_MP, seq_len, model_dim)))
    up_groups = w_up.reshape(model_dim, N_MP, inner_dim).transpose(1, 0, 2)
    pre_act = low_back(jnp.einsum('msd,mdf->msf', copies, up_groups, precision=PRECISE) + b_up.reshape(N_MP, 1, inner_dim))
    active = low(gelu_exact(pre_act))
    down_parts = low(jnp.einsum('msf,mfd->msd', active, w_down.reshape(N_MP, inner_dim, model_dim), precision=PRECISE))
    ffn_out = low_back(lax.optimization_barrier(jnp.sum(down_parts, axis=0)) + b_down)
    hidden_two = layer_norm(hidden_one + ffn_out, ln_gain[1], ln_bias[1])
    student_in = low_back(jnp.dot(low(hidden_two), s_w1, precision=PRECISE) + s_bias[0])
    loss_value = student_head(student_in[None], s_query, s_w2, s_bias[1], s_w3, s_b3, seg_row[None], lab_row[None], wt_row[None])
    return (hidden_two, loss_value)

def reference(rows_in, segment_ids, pair_labels, pair_mask, exit_flag, target, cot_out, w_qkv, b_qv, w_out, b_out, ln_gain, ln_bias, w_up, b_up, w_down, b_down, s_w1, s_bias, s_query, s_w2, s_w3, s_b3):
    weights_in = (w_qkv, b_qv, w_out, b_out, ln_gain, ln_bias, w_up, b_up, w_down, b_down, s_w1, s_bias, s_query, s_w2, s_w3, s_b3)
    params = tuple((weight_arg.astype(jnp.float32) for weight_arg in weights_in))
    group_rows = N_BATCH * ROWS_DEV
    slot_total = N_GRP * N_BATCH * CAP
    alive_rows = (1 - exit_flag).reshape(N_GRP, group_rows)
    goal_rows = target.reshape(N_GRP, group_rows)
    same_goal = (goal_rows[:, :, None] == goal_rows[:, None, :]) & (alive_rows[:, :, None] > 0) & (alive_rows[:, None, :] > 0)
    row_order = jnp.arange(group_rows, dtype=jnp.int32)
    earlier = row_order[None, :] < row_order[:, None]
    slot_in = lax.optimization_barrier(jnp.sum((same_goal & earlier[None]).astype(jnp.int32), axis=2))
    where_to = (jnp.arange(N_GRP, dtype=jnp.int32)[:, None] * N_BATCH + goal_rows) * CAP + slot_in
    where_to = jnp.where(alive_rows > 0, where_to, slot_total).reshape(-1).astype(jnp.int32)

    def place(values):
        return jnp.zeros((slot_total,) + values.shape[1:], values.dtype).at[where_to].set(values, mode='drop')
    seg_rep = place(segment_ids)
    lab_rep = place(pair_labels)
    wt_rep = place(pair_mask.astype(jnp.float32))
    live_rep = place(jnp.ones((rows_in.shape[0],), jnp.float32))

    def forward(rows_value, param_list):
        repacked = low_back(place(rows_value))

        def one_row(packed):
            return row_layer(packed[0], packed[1], packed[2], packed[3], param_list)
        return lax.map(jax.checkpoint(one_row), (repacked, seg_rep, lab_rep, wt_rep))
    (hidden_two, losses), pullback = jax.vjp(forward, rows_in.astype(jnp.float32), params)
    grad_in, grad_params = pullback((cot_out.astype(jnp.float32) * live_rep[:, None, None], jnp.ones((slot_total,), jnp.float32)))
    mixed_out = (hidden_two * live_rep[:, None, None]).astype(jnp.bfloat16)
    g_wqkv, g_bqv, g_wout, g_bout, g_lngain, g_lnbias, g_wup, g_bup, g_wdown, g_bdown, g_sw1, g_sbias, g_squery, g_sw2, g_sw3, g_sb3 = grad_params
    return (mixed_out, grad_in.astype(jnp.bfloat16), g_wqkv, g_bqv, g_wout, g_bout, g_lngain, g_lnbias, g_wup, g_bup, g_wdown, g_bdown, g_sw1, g_sbias, g_squery, g_sw2, g_sw3, g_sb3)
```

```python
import functools

import jax
import jax.numpy as jnp
from jax import lax
from jax.experimental import pallas as pl
from jax.experimental.pallas import tpu as pltpu
from jax.sharding import PartitionSpec as P

HEAD_DIM = 64
EPS = 1e-12
NEG = -1000000000.0
PRECISE = lax.Precision.HIGHEST
F32 = jnp.float32
BF16 = jnp.bfloat16
BLOCK = 512
VMEM_MOST = 62 * 1024 * 1024
NN = (((1,), (0,)), ((), ()))
NT = (((1,), (1,)), ((), ()))
TN = (((0,), (0,)), ((), ()))


def mm(left, right, dims=NN):
    return lax.dot_general(left, right, dims, preferred_element_type=F32)


def mm_exact(left, right, dims=NN):
    return lax.dot_general(left, right, dims, precision=PRECISE, preferred_element_type=F32)


def norm_parts(resid):
    center = resid - jnp.mean(resid, axis=-1, keepdims=True)
    spread = jnp.mean(center * center, axis=-1, keepdims=True)
    rstd = lax.rsqrt(spread + EPS)
    return center * rstd, rstd


def norm_back(upstream, xhat, rstd, gain):
    scaled = upstream * gain
    mean_u = jnp.mean(scaled, axis=-1, keepdims=True)
    mean_ux = jnp.mean(scaled * xhat, axis=-1, keepdims=True)
    return (scaled - mean_u - xhat * mean_ux) * rstd


def column_sum(value):
    return jnp.sum(value, axis=0, keepdims=True)


def mesh_place():
    g, b, z = lax.axis_index("grp"), lax.axis_index("batch"), lax.axis_index("mp")
    hi, lo, bit = g // 2, g % 2, b % 2
    return dict(
        g=g, b=b, z=z, hi=hi, lo=lo, bit=bit,
        far={"grp": (1 - hi) * 2 + lo}, twin={"grp": hi * 2 + 1 - lo}, side={"batch": b + 1 - 2 * bit},
        far_twin={"grp": (1 - hi) * 2 + 1 - lo},
    )


def remote(src, dst, send_sem, recv_sem, device):
    return pltpu.make_async_remote_copy(
        src_ref=src, dst_ref=dst, send_sem=send_sem, recv_sem=recv_sem,
        device_id=device, device_id_type=pl.DeviceIdType.MESH,
    )


def greet(at, batch_size, model_size):
    barrier = pltpu.get_barrier_semaphore()
    peers = [at["far"], at["twin"]]
    if batch_size > 1:
        peers += [{"batch": (at["b"] + j) % batch_size} for j in range(1, batch_size)]
    else:
        peers += [at["side"]]
    peers += [{"mp": (at["z"] + i) % model_size} for i in range(1, model_size)]
    for peer in peers:
        pl.semaphore_signal(barrier, inc=1, device_id=peer, device_id_type=pl.DeviceIdType.MESH)
    pl.semaphore_wait(barrier, len(peers))


def begin(copies):
    for copy in copies:
        copy.start()


def arrive(copies):
    for copy in copies:
        copy.wait_recv()


def sent(copies):
    for copy in copies:
        copy.wait_send()


SPLIT = 4


class Gather:
    def __init__(self, at, model_size, home, spot, send_sem, recv_sem, early=None):
        self.at, self.home, self.spot, self.early = at, home, spot, early
        self.send_sem, self.recv_sem = send_sem, recv_sem
        z, lo, hi, bit = at["z"], at["lo"], at["hi"], at["bit"]
        self.near = z + 1 - 2 * (z % 2)
        self.cross = (z + 2) % model_size
        self.chunks = (self.near, self.cross, (self.near + 2) % model_size)
        piece = home.shape[0] // 16
        half = pl.multiple_of(lo * (8 * piece), 16)
        self.one_a = pl.ds(pl.multiple_of(half + bit * (2 * piece) + hi * piece, 16), piece)
        self.one_b = pl.ds(pl.multiple_of(half + 4 * piece + hi * (2 * piece) + bit * piece, 16), piece)
        self.two_a = pl.ds(pl.multiple_of(half + bit * (2 * piece), 16), 2 * piece)
        self.two_b = pl.ds(pl.multiple_of(half + 4 * piece + hi * (2 * piece), 16), 2 * piece)
        self.half, self.step = half, 8 * piece // SPLIT

    def copies(self, stage, i):
        at, home, spot = self.at, self.home, self.spot

        def one(slot, src, dst, device):
            return remote(src, dst, self.send_sem.at[slot], self.recv_sem.at[slot], device)

        def same(slot, m, rows, device):
            return one(slot, spot.at[m, rows], spot.at[m, rows], device)

        m = self.chunks[i]
        if stage == 0 and i < 2:
            return [
                one(2 * i, home.at[self.one_a], spot.at[at["z"], self.one_a], {"mp": m}),
                one(2 * i + 1, home.at[self.one_b], spot.at[at["z"], self.one_b], {"mp": m}),
            ]
        if stage == 0:
            return [
                same(4, self.cross, self.one_a, {"mp": self.near}),
                same(5, self.cross, self.one_b, {"mp": self.near}),
            ]
        if stage == 1 and self.early is not None:
            return [
                one(6 + 2 * i, self.early.at[i, 0], spot.at[m, self.one_a], at["far"]),
                one(7 + 2 * i, self.early.at[i, 1], spot.at[m, self.one_b], at["side"]),
            ]
        if stage == 1:
            return [same(6 + 2 * i, m, self.one_a, at["far"]), same(7 + 2 * i, m, self.one_b, at["side"])]
        if stage == 2:
            return [same(12 + 2 * i, m, self.two_a, at["side"]), same(13 + 2 * i, m, self.two_b, at["far"])]
        return [
            same(18 + SPLIT * i + n, m, pl.ds(pl.multiple_of(self.half + n * self.step, 16), self.step), at["twin"])
            for n in range(SPLIT)
        ]

    def start(self):
        begin(self.copies(0, 1) + self.copies(0, 0))

    def early_copies(self, stage):
        def one(slot, src, dst, device):
            return remote(src, dst, self.send_sem.at[slot], self.recv_sem.at[slot], device)

        if stage == 0:
            return [
                one(2 * i + p, self.home.at[rows], self.early.at[i, p], {"mp": self.chunks[i]})
                for i in (1, 0)
                for p, rows in enumerate((self.one_a, self.one_b))
            ]
        return [one(4 + p, self.early.at[1, p], self.early.at[2, p], {"mp": self.near}) for p in range(2)]

    def own_pieces(self, sem):
        return [
            pltpu.make_async_copy(self.early.at[i, p], self.spot.at[self.chunks[i], rows], sem.at[2 * i + p])
            for i in range(3)
            for p, rows in enumerate((self.one_a, self.one_b))
        ]

    def advance(self, stage, *parts):
        for i in parts:
            arrive(self.copies(stage - 1, i))
            if stage == 1 and i == 1:
                begin(self.copies(0, 2))
            begin(self.copies(stage, i))

    def done(self, *parts):
        for i in parts:
            arrive(self.copies(3, i))

    def sent(self):
        for stage in range(0 if self.early is None else 1, 4):
            for i in range(3):
                sent(self.copies(stage, i))


GATHER_SEMS = 18 + 3 * SPLIT
PARTS = 2


class Reduce:
    def __init__(self, at, model_size, full, base, got_half, got_a, got_b, got_a2, got_b2, last, got_z, out,
                 send_sem, recv_sem, far_first=0, direct=False):
        self.far_first, self.direct = far_first, direct
        self.at, self.full, self.base, self.got_half = at, full, base, got_half
        self.got_a, self.got_b, self.got_a2, self.got_b2 = got_a, got_b, got_a2, got_b2
        self.last, self.got_z, self.out = last, got_z, out
        self.send_sem, self.recv_sem = send_sem, recv_sem
        z = at["z"]
        self.near, self.cross = z + 1 - 2 * (z % 2), (z + 2) % model_size

    def copies(self, stage, i=0):
        at, base = self.at, self.base
        b, lo, hi = at["b"], at["lo"], at["hi"]

        def one(slot, src, dst, device):
            return remote(src, dst, self.send_sem.at[slot], self.recv_sem.at[slot], device)

        m = chunk_of(at, i)
        if stage == 0:
            return [
                one(25 + 4 * i + 2 * y + p, self.full.at[m, y, 1 - lo, p], self.got_half.at[m, y, p], at["twin"])
                for y in range(2)
                for p in range(PARTS)
            ]
        if stage == 1 and i < self.far_first:
            return [
                one(4 + 2 * i, base.at[m, :, 0, 1 - hi], self.got_a.at[m], at["far"]),
                one(5 + 2 * i, base.at[m, :, 1, 1 - hi], self.got_b.at[m], at["far"]),
            ]
        if stage == 2 and i < self.far_first:
            return [
                one(12 + 2 * i, base.at[m, 1 - b, 0, hi], self.got_a2.at[m], at["side"]),
                one(13 + 2 * i, base.at[m, 1 - b, 1, hi], self.got_b2.at[m], at["side"]),
            ]
        if stage == 1:
            return [
                one(4 + 2 * i, base.at[m, :, 0, 1 - hi], self.got_a.at[m], at["far"]),
                one(5 + 2 * i, base.at[m, 1 - b, 1], self.got_b.at[m], at["side"]),
            ]
        if stage == 2:
            return [
                one(12 + 2 * i, base.at[m, 1 - b, 0, hi], self.got_a2.at[m], at["side"]),
                one(13 + 2 * i, base.at[m, b, 1, 1 - hi], self.got_b2.at[m], at["far"]),
            ]
        if stage == 3:
            device = {"mp": self.cross if i == 2 else self.near}
            return [one(20 + i, self.last.at[m], self.got_z.at[i], device)] if i < 3 else []
        mine = self.out.at[lo, :, hi]
        if stage == 4 and self.direct:
            return [one(23 + 18 * n, mine, mine, at[peer]) for n, peer in enumerate(("far", "twin", "far_twin"))]
        if stage == 4:
            return [one(23, mine, mine, at["far"])]
        if self.direct:
            return []
        return [one(24, self.out.at[lo], self.out.at[lo], at["twin"])]

    def start(self, i):
        begin(self.copies(0, i))

    def after_core(self, i, go_on=True):
        arrive(self.copies(0, i))
        m = chunk_of(self.at, i)

        def one(n, _):
            y, p, h = n // 4, n // 2 % 2, n % 2
            self.base[m, y, p, h] = self.base[m, y, p, h] + self.got_half[m, y, p, h]
            return 0

        lax.fori_loop(0, 8, one, 0)
        if go_on:
            begin(self.copies(1, i))

    def after_one(self, i):
        arrive(self.copies(1, i))
        m, b, hi, base = chunk_of(self.at, i), self.at["b"], self.at["hi"], self.base
        for h in range(2):
            base[m, h, 0, hi] = base[m, h, 0, hi] + self.got_a[m, h]
            if i < self.far_first:
                base[m, h, 1, hi] = base[m, h, 1, hi] + self.got_b[m, h]
            else:
                base[m, b, 1, h] = base[m, b, 1, h] + self.got_b[m, h]
        begin(self.copies(2, i))

    def after_two(self, i, go_on=True):
        arrive(self.copies(2, i))
        m, b, hi, base = chunk_of(self.at, i), self.at["b"], self.at["hi"], self.base
        found = [base[m, b, 0, hi] + self.got_a2[m], base[m, b, 1, hi] + self.got_b2[m]]
        if i == 2:
            arrive(self.copies(3, 0))
        for p in range(PARTS):
            self.last[m, p] = found[p] + self.got_z[0, p] if i == 2 else found[p]
        if go_on:
            begin(self.copies(3, i))

    def total(self, p):
        z = self.at["z"]
        found = self.last[z, p].astype(F32) + self.got_z[1, p].astype(F32) + self.got_z[2, p].astype(F32)
        return found.astype(BF16)

    def after_three(self):
        arrive(self.copies(3, 1) + self.copies(3, 2))
        for p in range(PARTS):
            self.out[self.at["lo"], p, self.at["hi"]] = self.total(p)
        begin(self.copies(4))

    def hand_over(self, own_ref, hand_ref):
        arrive(self.copies(3, 1))
        own_ref[...] = self.base[self.at["z"]]
        hand_ref[0] = self.last[self.cross]
        hand_ref[1] = self.got_z[1]

    def after_four(self):
        arrive(self.copies(4))
        begin(self.copies(5))

    def done(self):
        arrive(self.copies(4) if self.direct else self.copies(5))

    def sent(self):
        for stage in range(6):
            for i in range(4 if stage < 4 else 1):
                sent(self.copies(stage, i))

    def sent_early(self):
        for stage, count in enumerate((4, 3, 3, 2)):
            for i in range(count):
                sent(self.copies(stage, i))


class Finish:
    def __init__(self, at, model_size, own, hand, got_a, got_b, got_a2, got_b2, got_z, out, send_sem, recv_sem):
        self.at, self.own, self.hand, self.out = at, own, hand, out
        self.got_a, self.got_b, self.got_a2, self.got_b2, self.got_z = got_a, got_b, got_a2, got_b2, got_z
        self.send_sem, self.recv_sem = send_sem, recv_sem
        self.cross = (at["z"] + 2) % model_size

    def copies(self, stage):
        at, own = self.at, self.own
        b, lo, hi = at["b"], at["lo"], at["hi"]

        def one(slot, src, dst, device):
            return remote(src, dst, self.send_sem.at[slot], self.recv_sem.at[slot], device)

        if stage == 0:
            return [one(0, self.hand.at[0], self.got_z, {"mp": self.cross})]
        if stage == 1:
            return [
                one(1, own.at[:, 0, 1 - hi], self.got_a, at["far"]),
                one(2, own.at[1 - b, 1], self.got_b, at["side"]),
            ]
        if stage == 2:
            return [
                one(3, self.got_a.at[1 - b], self.got_a2, at["side"]),
                one(4, self.got_b.at[1 - hi], self.got_b2, at["far"]),
            ]
        if stage == 3:
            return [one(5, self.out.at[lo, :, hi], self.out.at[lo, :, hi], at["far"])]
        return [one(6, self.out.at[lo], self.out.at[lo], at["twin"])]

    def start(self):
        begin(self.copies(1) + self.copies(0))

    def after_one(self):
        arrive(self.copies(1))
        b, hi = self.at["b"], self.at["hi"]
        for h in range(2):
            self.got_a[h] = self.got_a[h] + self.own[h, 0, hi]
            self.got_b[h] = self.got_b[h] + self.own[b, 1, h]
        begin(self.copies(2))

    def after_two(self):
        arrive(self.copies(2) + self.copies(0))
        b, lo, hi = self.at["b"], self.at["lo"], self.at["hi"]
        halves = ((self.got_a[b], self.got_a2[...]), (self.got_b[hi], self.got_b2[...]))
        for p, (held, got) in enumerate(halves):
            total = held.astype(F32) + got.astype(F32) + self.hand[1, p].astype(F32) + self.got_z[p].astype(F32)
            self.out[lo, p, hi] = total.astype(BF16)
        begin(self.copies(3))

    def after_three(self):
        arrive(self.copies(3))
        begin(self.copies(4))

    def done(self):
        arrive(self.copies(4))

    def sent(self):
        for stage in range(5):
            sent(self.copies(stage))


REDUCE_SEMS = 60


def chunk_of(at, i):
    high, low = at["z"] // 2, at["z"] % 2
    flip_high, flip_low = 1 - i % 2, 1 - i // 2
    return 2 * (high + flip_high - 2 * high * flip_high) + low + flip_low - 2 * low * flip_low


def reduce_scratch(model_size, piece, dim):
    low = lambda *shape: pltpu.VMEM(shape, BF16)
    return [
        low(model_size, 2, PARTS, 2, piece, dim),
        low(model_size, 2, piece, dim),
        low(model_size, 2, piece, dim),
        low(model_size, piece, dim),
        low(model_size, piece, dim),
        low(model_size, PARTS, piece, dim),
        low(3, PARTS, piece, dim),
    ]


def pack_places(dim, width):
    ends = [dim]
    for size in (width, 16, 8, 8 * dim // width, 8 * dim // width):
        ends.append(ends[-1] + size)
    return [slice(first, last) for first, last in zip(ends[:-1], ends[1:])]


def pack_rows(dim, width):
    return -(-pack_places(dim, width)[-1].stop // 128) * 128


def student_step(
    stud_ref, own_ref, query_ref, w2_ref, bmid, w3_ref, b3_ref,
    dstud_ref, gw2_ref, gw3_ref, gsmall_ref, classes, pairs,
):
    row_count, seq, width = stud_ref.shape
    head = own_ref.shape[1] - seq
    tag_cells = [
        [own_ref[r : r + 1, p : p + 1] for p in range(2 * pairs)] for r in range(row_count)
    ]
    labels = jnp.concatenate([cells[p] for cells in tag_cells for p in range(pairs)], axis=0)
    weights = jnp.concatenate([cells[pairs + p] for cells in tag_cells for p in range(pairs)], axis=0)
    half = width // 2
    lane = lax.broadcasted_iota(jnp.int32, (2 * pairs, width), 1)
    row = lax.broadcasted_iota(jnp.int32, (2 * pairs, width), 0)
    mine = (lane >= half) == (row >= pairs)
    query_rows = jnp.where(mine, query_ref[...].reshape(1, width) * half ** (-0.5), 0.0)
    pair_of = lax.rem(lax.broadcasted_iota(jnp.int32, (2 * pairs, seq), 0), pairs).astype(F32)
    members, shares_all, pooled_all = [], [], []
    for r in range(row_count):
        scores = mm_exact(query_rows, stud_ref[r], NT)
        member = own_ref[r : r + 1, head:] == pair_of
        masked = jnp.where(member, scores, NEG)
        terms = jnp.exp(masked - jnp.max(masked, axis=1, keepdims=True))
        shares = terms / jnp.sum(terms, axis=1, keepdims=True)
        pooled = jnp.where(mine, mm_exact(shares, stud_ref[r]), 0.0)
        members.append(member)
        shares_all.append(shares)
        pooled_all.append(pooled[:pairs] + pooled[pairs:])
    pooled = jnp.concatenate(pooled_all, axis=0)
    middle = jnp.tanh(mm_exact(pooled, w2_ref[...]) + bmid)
    logits = mm_exact(middle, w3_ref[...], NT) + b3_ref[...]
    class_of = lax.broadcasted_iota(jnp.int32, logits.shape, 1)
    logits = jnp.where(class_of < classes, logits, NEG)
    terms = jnp.exp(logits - jnp.max(logits, axis=1, keepdims=True))
    chance = terms / jnp.sum(terms, axis=1, keepdims=True)
    grad_logits = weights * (chance - jnp.where(class_of.astype(F32) == labels, 1.0, 0.0))
    gw3_ref[...] = mm_exact(grad_logits, middle, TN)[: gw3_ref.shape[0]]
    grad_pre = mm_exact(grad_logits, w3_ref[...]) * (1.0 - middle * middle)
    gw2_ref[...] = mm_exact(pooled, grad_pre, TN)
    grad_pooled = mm_exact(grad_pre, w2_ref[...], NT)
    grad_query = jnp.zeros((1, width), F32)
    grad_bias = jnp.zeros((1, width), F32)
    for r in range(row_count):
        part = grad_pooled[r * pairs : (r + 1) * pairs]
        grad_parts = jnp.where(mine, jnp.concatenate([part, part], axis=0), 0.0)
        shares = shares_all[r]
        grad_shares = mm_exact(grad_parts, stud_ref[r], NT)
        inner = jnp.sum(shares * grad_shares, axis=1, keepdims=True)
        grad_scores = jnp.where(members[r], shares * (grad_shares - inner), 0.0)
        grad_hidden = mm_exact(
            jnp.concatenate([shares, grad_scores], axis=0),
            jnp.concatenate([grad_parts, query_rows], axis=0),
            TN,
        )
        low = grad_hidden.astype(BF16)
        dstud_ref[r] = low
        grad_bias += column_sum(low.astype(F32))
        found = mm_exact(grad_scores, stud_ref[r]) * half ** (-0.5)
        grad_query += column_sum(jnp.where(mine, found, 0.0))
    gsmall_ref[0:1] = grad_bias
    gsmall_ref[1:2] = column_sum(grad_pre)
    gsmall_ref[2:3] = grad_query
    gsmall_ref[3:4] = column_sum(grad_logits)
    gsmall_ref[4:8] = jnp.zeros((4, width), F32)


def gelu_parts(value):
    size = jnp.abs(value)
    bell = jnp.exp(value * value * -0.5)
    base = 1.0 + (0.3275911 * 0.5 ** 0.5) * size
    t = pl.reciprocal(base, approx=True)
    t = t * (2.0 - base * t)
    terms = ((((1.061405429 * t - 1.453152027) * t + 1.421413741) * t - 0.284496736) * t + 0.254829592) * t
    tail = 0.5 * terms * bell
    return jnp.where(value < 0.0, tail, 1.0 - tail), bell * 0.3989422804014327


COLUMNS = 256


def ffn_kernel(
    classes, pairs, scatter,
    xhat1_ref, rstd1_ref, gain_ref, shift_ref, wb_ref, wc_home, early_ref, vecs_ref, bdown_ref, cot_ref, own_ref,
    sw1_ref, sbias_ref, query_ref, w2_in, w3_in, b3_in,
    mixed_ref, gres_ref, dwb_ref, out_ref, hand_ref, pack_ref,
    w2_ref, w3_ref, b3_ref, gbup_ref, gvec_ref, gsw1_ref, act_ref, slope_ref, xhat2_ref, rstd2_ref,
    stud_ref, dstud_ref, low_ref, flip_ref, wc_ref, dwc_ref, wsend, wrecv, msend, mrecv, local_sem, piece_sem, *parts,
):
    row_count, seq, dim = xhat1_ref.shape
    model_size = wb_ref.shape[0]
    inner = wb_ref.shape[2]
    per_row = seq // BLOCK
    blocks = row_count * per_row
    width = sw1_ref.shape[1]
    at = mesh_place()
    gather = Gather(at, model_size, wc_home, wc_ref, wsend, wrecv, early_ref)
    own_pieces = gather.own_pieces(piece_sem)
    own_copy = pltpu.make_async_copy(wc_home, wc_ref.at[at["z"]], local_sem.at[0])
    own_copy.start()
    for copy in own_pieces:
        copy.start()
    greet(at, 2 if scatter else 1, model_size)
    for i in (1, 0, 2):
        begin(gather.copies(1, i))
    if scatter:
        reducer = Reduce(at, model_size, dwc_ref, dwc_ref.at[:, :, at["lo"]], *parts, None, msend, mrecv)

    w2_at, w3_at, small_at, vec_at, bup_at = pack_places(dim, width)
    sb1, bmid = sbias_ref[0:1], sbias_ref[1:2]
    w2_ref[...] = w2_in[...].astype(F32)
    w3_ref[...] = jnp.zeros_like(w3_ref)
    w3_ref[:classes] = w3_in[...].astype(F32)
    b3_ref[...] = jnp.zeros_like(b3_ref)
    b3_ref[:, :classes] = b3_in[...].reshape(1, classes)
    gain_one, gain_two = gain_ref[0:1], gain_ref[1:2]
    shift_one, shift_two = shift_ref[0:1], shift_ref[1:2]

    def live(r):
        cells = [own_ref[i : i + 1, 2 * pairs : 2 * pairs + 1] for i in range(row_count)]
        return sum(jnp.where(r == i, 1.0, 0.0) * cells[i] for i in range(row_count))

    def place(t):
        return t // per_row, pl.ds(pl.multiple_of(t % per_row * BLOCK, BLOCK), BLOCK)

    def prepare(t, _):
        r, part = place(t)
        hidden = xhat1_ref[r, part] * gain_one + shift_one
        low_ref[t] = hidden.astype(BF16)
        xhat2_ref[r, part] = hidden + bdown_ref[...].reshape(1, dim)
        return 0

    lax.fori_loop(0, blocks, prepare, 0)
    for copy in own_pieces:
        copy.wait()
    def during(m, table):
        for when, actions in table.items():
            @pl.when(m == when)
            def _():
                for action, *args in actions:
                    action(*args)

    def up(m, _):
        during(m, {
            1: [(gather.advance, 2, 1, 0)],
            2: [(gather.advance, 2, 2), (gather.advance, 3, 1)],
            3: [(gather.advance, 3, 0)],
        })

        def one(t, _):
            low = low_ref[t]
            for c in range(0, inner, COLUMNS):
                columns = slice(c, c + COLUMNS)
                pre = mm(low, wb_ref[m, :, columns]) + vecs_ref[m, 1:2, columns]
                cdf, pdf = gelu_parts(pre)
                act_ref[m, t, :, columns] = (pre * cdf).astype(BF16)
                slope_ref[m, t, :, columns] = (cdf + pre * pdf).astype(BF16)
            return 0

        lax.fori_loop(0, blocks, one, 0)
        return 0

    lax.fori_loop(0, model_size, up, 0)
    gather.advance(3, 2)
    own_copy.wait()

    def down(m):
        def one(t, _):
            r, part = place(t)
            xhat2_ref[r, part] = xhat2_ref[r, part] + mm(act_ref[m, t], wc_ref[m])
            return 0

        lax.fori_loop(0, blocks, one, 0)

    down(at["z"])
    for i in (1, 0, 2):
        gather.done(i)
        down(gather.chunks[i])

    def norm_two(t, _):
        r, part = place(t)
        xhat, rstd = norm_parts(xhat2_ref[r, part])
        xhat2_ref[r, part] = xhat
        rstd2_ref[r, part] = rstd
        hidden_two = xhat * gain_two + shift_two
        mixed_ref[r, part] = (hidden_two * live(r)).astype(BF16)
        stud_ref[r, part] = mm(hidden_two.astype(BF16), sw1_ref[...]) + sb1
        return 0

    lax.fori_loop(0, blocks, norm_two, 0)
    student_step(
        stud_ref, own_ref, query_ref, w2_ref, bmid, w3_ref, b3_ref,
        dstud_ref, pack_ref.at[w2_at], pack_ref.at[w3_at], pack_ref.at[small_at], classes, pairs,
    )
    gvec_ref[...] = jnp.zeros_like(gvec_ref)
    gsw1_ref[...] = jnp.zeros_like(gsw1_ref)
    gbup_ref[...] = jnp.zeros_like(gbup_ref)

    def norm_two_back(t, _):
        r, part = place(t)
        xhat = xhat2_ref[r, part]
        two_low = (xhat * gain_two + shift_two).astype(BF16)
        grad_low = dstud_ref[r, part]
        gsw1_ref[...] += mm(grad_low, two_low, TN)
        upstream = cot_ref[r, part].astype(F32) * live(r) + mm(grad_low, sw1_ref[...], NT)
        gvec_ref[1:2] += column_sum(upstream * xhat)
        gvec_ref[3:4] += column_sum(upstream)
        grad = norm_back(upstream, xhat, rstd2_ref[r, part], gain_two)
        low = grad.astype(BF16)
        gvec_ref[4:5] += column_sum(low.astype(F32))
        gres_ref[r, part] = grad
        low_ref[t] = low
        flip_ref[:, pl.ds(pl.multiple_of(t * BLOCK, BLOCK), BLOCK)] = low.T
        return 0

    lax.fori_loop(0, blocks, norm_two_back, 0)
    half = dim // 2

    def weight_grads(out, right_ref, m):
        def one(y, _):
            part = pl.ds(pl.multiple_of(y * half, 128), half)
            total = mm(flip_ref[part, :], right_ref[m].reshape(blocks * BLOCK, inner)).astype(BF16)
            out[m, y] = total.reshape(out.shape[2:])
            return 0

        lax.fori_loop(0, 2, one, 0)

    def first_grads(i, _):
        weight_grads(dwc_ref, act_ref, chunk_of(at, i))
        if scatter:
            during(i, {n: [(reducer.start, n)] for n in range(model_size)})
        return 0

    lax.fori_loop(0, model_size, first_grads, 0)
    def backward(m, _):
        if scatter:
            during(m, {
                1: [(reducer.after_core, 0)],
                2: [(reducer.after_core, 1), (reducer.after_one, 0)],
                3: [(reducer.after_two, 0), (reducer.after_one, 1), (reducer.after_core, 2)],
            })

        def one(t, _):
            r, part = place(t)
            grad_pre = (mm(low_ref[t], wc_ref[m], NT) * slope_ref[m, t].astype(F32)).astype(BF16)
            slope_ref[m, t] = grad_pre
            gbup_ref[m] += column_sum(grad_pre.astype(F32))
            gres_ref[r, part] = gres_ref[r, part] + mm(grad_pre, wb_ref[m], NT)
            return 0

        lax.fori_loop(0, blocks, one, 0)
        return 0

    lax.fori_loop(0, model_size, backward, 0)

    def norm_one_back(t, _):
        r, part = place(t)
        upstream = gres_ref[r, part]
        xhat = xhat1_ref[r, part]
        gvec_ref[0:1] += column_sum(upstream * xhat)
        gvec_ref[2:3] += column_sum(upstream)
        resid = norm_back(upstream, xhat, rstd1_ref[r, part], gain_one)
        gres_ref[r, part] = resid
        gvec_ref[5:6] += column_sum(resid.astype(BF16).astype(F32))
        flip_ref[:, pl.ds(pl.multiple_of(t * BLOCK, BLOCK), BLOCK)] = (xhat * gain_one + shift_one).astype(BF16).T
        return 0

    lax.fori_loop(0, blocks, norm_one_back, 0)
    def second_grads(m, _):
        if scatter:
            during(m, {
                1: [(reducer.after_two, 1), (reducer.after_one, 2)],
                3: [(reducer.after_core, 3, False), (reducer.after_two, 2, False)],
            })
        weight_grads(dwb_ref, slope_ref, m)
        return 0

    lax.fori_loop(0, model_size, second_grads, 0)
    for m in range(model_size):
        bup = gbup_ref[m]
        for j in range(dim // width):
            pack_ref[bup_at.start + j * 8 + m : bup_at.start + j * 8 + m + 1] = bup[:, j * width : (j + 1) * width]
    for j in range(dim // width):
        columns = slice(j * width, (j + 1) * width)
        pack_ref[columns] = gsw1_ref[:, columns]
        pack_ref[vec_at.start + j * 8 : vec_at.start + j * 8 + 8] = gvec_ref[:, columns]
        if model_size < 8:
            first = bup_at.start + j * 8
            pack_ref[first + model_size : first + 8] = jnp.zeros((8 - model_size, width), F32)
    pack_ref[bup_at.stop :] = jnp.zeros((pack_ref.shape[0] - bup_at.stop, width), F32)
    if scatter:
        reducer.hand_over(out_ref, hand_ref)
        reducer.sent_early()
    else:
        out_ref[...] = dwc_ref[...]
        hand_ref[...] = jnp.zeros_like(hand_ref)
    gather.sent()


def ffn_both(xhat1, rstd1, gain, shift, w_b, w_c, early, vecs, b_down, cot, own, pairs, scatter,
             s_w1, s_bias, s_query, s_w2, s_w3, s_b3):
    rows, seq, dim = xhat1.shape
    model_size = w_b.shape[0]
    inner = w_b.shape[2]
    width = s_w1.shape[1]
    classes = s_w3.shape[1]
    blocks = rows * seq // BLOCK
    piece = dim // 16
    grid_shape = (model_size, 2, 2, PARTS, 2, piece, inner)
    low = lambda *shape: pltpu.VMEM(shape, BF16)
    f32 = lambda *shape: pltpu.VMEM(shape, F32)
    dma = pltpu.SemaphoreType.DMA
    vmem = pl.BlockSpec(memory_space=pltpu.VMEM)
    hbm = pl.BlockSpec(memory_space=pl.ANY)
    return pl.pallas_call(
        functools.partial(ffn_kernel, classes, pairs, scatter),
        in_specs=[vmem] * 5 + [hbm, hbm] + [vmem] * 10,
        out_specs=[vmem] * 6,
        out_shape=(
            jax.ShapeDtypeStruct((rows, seq, dim), BF16),
            jax.ShapeDtypeStruct((rows, seq, dim), F32),
            jax.ShapeDtypeStruct(grid_shape, BF16),
            jax.ShapeDtypeStruct(grid_shape[1:2] + grid_shape[3:] if scatter else grid_shape, BF16),
            jax.ShapeDtypeStruct((2, PARTS, piece, inner), BF16),
            jax.ShapeDtypeStruct((pack_rows(dim, width), width), F32),
        ),
        scratch_shapes=[
            f32(width, width),
            f32(width, width),
            f32(1, width),
            f32(model_size, 1, inner),
            f32(8, dim),
            f32(width, dim),
            low(model_size, blocks, BLOCK, inner),
            low(model_size, blocks, BLOCK, inner),
            f32(rows, seq, dim),
            f32(rows, seq, 1),
            f32(rows, seq, width),
            low(rows, seq, width),
            low(blocks, BLOCK, dim),
            low(dim, rows * seq),
            low(model_size, inner, dim),
            low(*grid_shape),
            dma((GATHER_SEMS,)),
            dma((GATHER_SEMS,)),
            dma((REDUCE_SEMS,)),
            dma((REDUCE_SEMS,)),
            dma((1,)),
            dma((6,)),
            *(reduce_scratch(model_size, piece, inner) if scatter else ()),
        ],
        compiler_params=pltpu.CompilerParams(
            vmem_limit_bytes=VMEM_MOST, collective_id=1, has_side_effects=True
        ),
        name="ffn_both",
    )(
        xhat1, rstd1, gain, shift, w_b, w_c, early, vecs, b_down, cot, own,
        s_w1, s_bias, s_query, s_w2, s_w3.T, s_b3,
    )


TILE_Q = 256
TILE_BACK = 64


def backward_group(grad_ctx, ctx_of, load, store, mask, lse_of, group_dim, p_ref, s_ref):
    scale = HEAD_DIM ** (-0.5)
    for j in range(group_dim // HEAD_DIM):
        rows = slice(j * HEAD_DIM, (j + 1) * HEAD_DIM)
        k_rows = slice(group_dim + rows.start, group_dim + rows.stop)
        v_rows = slice(2 * group_dim + rows.start, 2 * group_dim + rows.stop)
        q_t = load(rows) * scale
        k_t = load(k_rows)
        v_t = load(v_rows)
        d_t = grad_ctx[rows]
        seq = q_t.shape[1]
        inner = column_sum(d_t.astype(F32) * ctx_of(rows).astype(F32))
        lse = lse_of(j)
        k_n, v_n = k_t.T, v_t.T
        probs_ref, grads_ref = p_ref.at[j % 2], s_ref.at[j % 2]
        for q0 in range(0, seq, TILE_Q):
            columns = slice(q0, q0 + TILE_Q)
            q, d = q_t[:, columns], d_t[:, columns]
            for k0 in range(0, seq, TILE_BACK):
                part = slice(k0, k0 + TILE_BACK)
                probs = jnp.exp(mm(k_n[part], q) + mask[part, columns] - lse[:, columns])
                grad_probs = mm(v_n[part], d)
                probs_ref[part, columns] = probs.astype(BF16)
                grads_ref[part, columns] = (probs * (grad_probs - inner[:, columns])).astype(BF16)
        store(rows, mm(k_t * scale, grads_ref[...]).astype(BF16))
        store(k_rows, mm(q_t, grads_ref[...], NT).astype(BF16))
        store(v_rows, mm(d_t, probs_ref[...], NT).astype(BF16))


def attn_backward_kernel(
    x_ref, gres_ref, wa_ref, qkv_ref, ctx_ref, lse_ref, own_ref, dx_ref, dwa_ref, bias_ref,
    mask_ref, acc_ref, work_ref, xflip_ref, gflip_ref, p_ref, s_ref,
):
    row_count, seq, dim = x_ref.shape
    model_size = wa_ref.shape[0]
    group_dim = ctx_ref.shape[2]
    bias_ref[...] = jnp.zeros_like(bias_ref)
    seg_rows = own_ref[:, own_ref.shape[1] - seq :]
    seg_cols = seg_rows.T
    for r in range(row_count):
        mask_ref[...] = jnp.where(seg_cols[:, r : r + 1] == seg_rows[r : r + 1], 0.0, NEG)
        acc_ref[...] = gres_ref[r]
        grad_low = gres_ref[r].astype(BF16)
        columns = slice(r * seq, (r + 1) * seq)
        gflip_ref[:, columns] = grad_low.T
        xflip_ref[:, columns] = x_ref[r].T

        def one_group(m, _):
            grad_ctx = mm(wa_ref[m, 3 * group_dim :, :], grad_low, NT).astype(BF16)

            def store(rows, value):
                work_ref[r, m, rows, :] = value

            backward_group(
                grad_ctx, lambda rows: ctx_ref[r, m, rows, :], lambda rows: qkv_ref[r, m, rows, :], store,
                mask_ref, lambda j: lse_ref[r, m, j : j + 1, :], group_dim, p_ref, s_ref,
            )
            grads = work_ref[r, m]
            bias_ref[m] += mm(jnp.ones((8, seq), BF16), grads, NT)
            acc_ref[...] += mm(grads, wa_ref[m, : 3 * group_dim, :], TN)
            return 0

        lax.fori_loop(0, model_size, one_group, 0)
        dx_ref[r] = acc_ref[...].astype(BF16)

    def weight_grads(i, _):
        m, part = i // 2, pl.ds(pl.multiple_of(i % 2 * (dim // 2), 128), dim // 2)
        left, right = 0.0, 0.0
        for r in range(row_count):
            columns = slice(r * seq, (r + 1) * seq)
            left += mm(xflip_ref[part, columns], work_ref[r, m], NT)
            right += mm(gflip_ref[part, columns], ctx_ref[r, m], NT)
        dwa_ref[m, part, : 3 * group_dim] = left.astype(BF16)
        dwa_ref[m, part, 3 * group_dim :] = right.astype(BF16)
        return 0

    lax.fori_loop(0, 2 * model_size, weight_grads, 0)


def attn_backward(x, gres, w_a, qkv, ctx, lse, own):
    rows, seq, dim = x.shape
    model_size = w_a.shape[0]
    group_dim = dim // model_size
    return pl.pallas_call(
        attn_backward_kernel,
        out_shape=(
            jax.ShapeDtypeStruct((rows, seq, dim), BF16),
            jax.ShapeDtypeStruct((model_size, dim, 4 * group_dim), BF16),
            jax.ShapeDtypeStruct((model_size, 8, 3 * group_dim), F32),
        ),
        scratch_shapes=[
            pltpu.VMEM((seq, seq), F32),
            pltpu.VMEM((seq, dim), F32),
            pltpu.VMEM((rows, model_size, 3 * group_dim, seq), BF16),
            pltpu.VMEM((dim, rows * seq), BF16),
            pltpu.VMEM((dim, rows * seq), BF16),
            pltpu.VMEM((2, seq, seq), BF16),
            pltpu.VMEM((2, seq, seq), BF16),
        ],
        compiler_params=pltpu.CompilerParams(vmem_limit_bytes=VMEM_MOST),
        name="attn_backward",
    )(x, gres, w_a, qkv, ctx, lse, own)
def slot_of_rows(exit_ref, target_ref, depth):
    count = exit_ref.shape[0]
    flat = []
    for i in range(count):
        rank = 0
        for h in range(i):
            rank = rank + jnp.where(target_ref[h] == target_ref[i], 1 - exit_ref[h], 0)
        flat.append(jnp.where(exit_ref[i] == 0, target_ref[i] * depth + rank, -1))
    return flat


def pick_of_slots(tag_ref, depth, flag_at, capacity):
    seen = jnp.zeros((1, 1), F32)
    picks = []
    for k in range(tag_ref.shape[0] * depth):
        live = tag_ref[k // depth, k % depth : k % depth + 1, flag_at : flag_at + 1]
        picks.append([jnp.where(seen == float(c), live, 0.0) for c in range(min(capacity, k + 1))])
        seen = seen + live
    return picks


def slots_of_tags(tag_ref, depth, flag_at, capacity):
    seen, slots = 0, []
    for k in range(tag_ref.shape[0] * depth):
        cell = tag_ref[k // depth, k % depth : k % depth + 1, flag_at : flag_at + 1]
        live = jnp.where(jnp.sum(cell) > 0.5, 1, 0)
        slots.append((jnp.minimum(seen, capacity - 1), live))
        seen = seen + live
    return slots


TOKENS = 32
CUTS = 3


def enter_kernel(
    depth, pairs,
    exit_ref, target_ref, rows_ref, seg_ref, lab_ref, wt_ref, wqkv_ref, wout_ref, bqv_ref, bup_ref, bout_ref,
    wb_loc, wc_loc,
    own_ref, got_tags_ref, vecs_ref, x_out, wa_out, wb_ref, early_ref,
    qkv_ref, ctx_ref, lse_ref, xhat_ref, rstd_ref,
    tags_ref, vec_ref, wa_loc, slot_ref, part_ref, x_ref, wa_ref, tag_ref, taggot_ref, taglocal_ref, vecgot_ref,
    mask_ref, acc_ref, wsend, wrecv, rsend, rrecv, local_sem, *got_refs,
):
    row_count, token_part, dim = rows_ref.shape
    own_rows, seq = x_ref.shape[:2]
    model_size = wa_ref.shape[0]
    batch_size = taggot_ref.shape[0]
    capacity = own_rows * model_size
    group_dim = wout_ref.shape[0]
    flag_at = 2 * pairs
    head = tag_ref.shape[2] - seq
    at = mesh_place()
    b, z = at["b"], at["z"]
    gathers = [
        Gather(at, model_size, home, spot, wsend.at[k], wrecv.at[k])
        for k, (home, spot) in enumerate(((wa_loc, wa_ref), (wb_loc, wb_ref)))
    ]
    first_gather, second_gather = gathers
    third_gather = Gather(at, model_size, wc_loc, None, wsend.at[2], wrecv.at[2], early_ref)
    vec_first = (CUTS + 1) * batch_size + CUTS * model_size

    def vec_copies():
        return [
            remote(vec_ref, vecgot_ref.at[z], rsend.at[vec_first + i], rrecv.at[vec_first + i],
                   {"mp": (z + i) % model_size})
            for i in range(1, model_size)
        ]

    wide = dim // CUTS

    def batch_copies(cut):
        columns = pl.ds(cut * wide, wide)
        copies = []
        for j in range(1, batch_size):
            t = (b + j) % batch_size
            n = cut * batch_size + j
            copies.append(remote(slot_ref.at[pl.ds(t * depth, depth), :, columns],
                                 got_refs[cut].at[pl.ds(b * depth, depth)],
                                 rsend.at[n], rrecv.at[n], {"batch": t}))
            if cut == 0:
                n = CUTS * batch_size + j
                copies.append(remote(tag_ref.at[t], taggot_ref.at[b], rsend.at[n], rrecv.at[n], {"batch": t}))
        return copies

    mine = pl.ds(pl.multiple_of(z * token_part, 128), token_part)

    def row_copies(cut, r):
        columns = pl.ds(cut * wide, wide)
        first = (CUTS + 1) * (batch_size + model_size) + (cut * own_rows + r) * model_size
        return [
            remote(part_ref.at[(z + i) % model_size * own_rows + r, :, columns], x_ref.at[r, mine, columns],
                   rsend.at[first + i], rrecv.at[first + i], {"mp": (z + i) % model_size})
            for i in range(1, model_size)
        ]

    def local_copies():
        return [
            pltpu.make_async_copy(gather.home, gather.spot.at[z], local_sem.at[k])
            for k, gather in enumerate(gathers)
        ]

    for j in range(3):
        wa_loc[j * group_dim : (j + 1) * group_dim, :] = wqkv_ref[j]
    wa_loc[3 * group_dim :, :] = wout_ref[...]
    vec_ref[...] = jnp.zeros_like(vec_ref)
    vec_ref[0:1, :group_dim] = bqv_ref[0:1]
    vec_ref[0:1, 2 * group_dim : 3 * group_dim] = bqv_ref[1:2]
    vec_ref[1:2] = bup_ref[...].reshape(1, dim)
    greet(at, batch_size, model_size)
    first_gather.start()
    begin(vec_copies())
    begin(local_copies())

    flat = slot_of_rows(exit_ref, target_ref, depth)
    tags_ref[...] = jnp.zeros_like(tags_ref)
    taglocal_ref[0] = jnp.zeros_like(taglocal_ref[0])
    taglocal_ref[0, :pairs, :row_count] = lab_ref[...].astype(F32)
    taglocal_ref[0, pairs : 2 * pairs, :row_count] = wt_ref[...].astype(F32)
    tags_ref[:, : 2 * pairs] = taglocal_ref[0, : 2 * pairs, :128].T[: tags_ref.shape[0]]
    tags_ref[:row_count, flag_at : flag_at + 1] = jnp.ones((row_count, 1), F32)
    tags_ref[:row_count, head:] = seg_ref[...].astype(F32)
    tag_ref[...] = jnp.zeros_like(tag_ref)

    def taken(k):
        hits = [jnp.where(flat[r] == k, 1, 0) for r in range(row_count)]
        return sum(r * hits[r] for r in range(row_count)), sum(hits).astype(F32)

    def fill(t, dst_ref, cut):
        columns = pl.ds(cut * wide, wide)
        for s in range(depth):
            row, there = taken(t * depth + s)
            found = (rows_ref[row, :, columns].astype(F32) * there).astype(BF16)
            if dst_ref is None:
                got_refs[cut][t * depth + s] = found
            else:
                dst_ref[t * depth + s, :, columns] = found

    def fill_tags(t):
        for s in range(depth):
            total = jnp.zeros((1, tags_ref.shape[1]), F32)
            for r in range(row_count):
                total += jnp.where(flat[r] == t * depth + s, 1.0, 0.0) * tags_ref[r : r + 1]
            tag_ref[t, s : s + 1] = total

    for j in range(1, batch_size):
        fill_tags((b + j) % batch_size)
    for cut in range(CUTS):
        for j in range(1, batch_size):
            fill((b + j) % batch_size, slot_ref, cut)
        if cut == 0:
            begin(batch_copies(0))
            fill_tags(b)
            taggot_ref[b] = tag_ref[b]
            fill(b, None, 0)
    for cut in range(1, CUTS):
        fill(b, None, cut)
    arrive(batch_copies(0))
    begin(batch_copies(1))

    picks = pick_of_slots(taggot_ref, depth, flag_at, capacity)

    slots = slots_of_tags(taggot_ref, depth, flag_at, capacity)

    def compact(cut):
        columns = pl.ds(cut * wide, wide)
        for c in range(capacity):
            hits = [jnp.where(place == c, live, 0) for place, live in slots]
            k = sum(n * hits[n] for n in range(c, len(slots)))
            there = sum(hits[c:]).astype(F32)
            part_ref[c, :, columns] = (got_refs[cut][k].astype(F32) * there).astype(BF16)
        begin(row_copies(cut, 0))

    compact(0)
    first_gather.advance(1, 1, 0)
    arrive(batch_copies(1))
    for cut in range(2, CUTS):
        begin(batch_copies(cut))
        compact(cut - 1)
        if cut == 2:
            first_gather.advance(1, 2)
        arrive(batch_copies(cut))
    compact(CUTS - 1)
    first_gather.advance(2, 1, 0, 2)
    second_gather.start()
    for r in range(1, own_rows):
        for cut in range(CUTS):
            begin(row_copies(cut, r))
    for c in range(capacity):
        total = jnp.zeros((1, tags_ref.shape[1]), F32)
        for k in range(c, len(picks)):
            total += picks[k][c] * taggot_ref[k // depth, k % depth : k % depth + 1]
        taglocal_ref[c, 0:1] = total
    for i in range(own_rows):
        x_ref[i, mine] = part_ref[z * own_rows + i]
    own_ref[...] = jnp.zeros_like(own_ref)
    for i in range(own_rows):
        own_ref[i : i + 1] = taglocal_ref[z * own_rows + i, 0:1]
    got_tags_ref[...] = taggot_ref[...]

    first_gather.advance(3, 1, 0, 2)
    arrive(vec_copies())
    vecgot_ref[z] = vec_ref[...]
    vecs_ref[...] = vecgot_ref[...]
    for copy in local_copies():
        copy.wait()
    keep = [
        pltpu.make_async_copy(x_ref, x_out, local_sem.at[3]),
        pltpu.make_async_copy(wa_ref, wa_out, local_sem.at[4]),
    ]

    def rows_here(r):
        for cut in range(CUTS):
            arrive(row_copies(cut, r))

    rows_here(0)
    seg_rows = own_ref[:, head:]
    seg_cols = seg_rows.T
    def forward_early():
        arrive(third_gather.early_copies(0))
        begin(third_gather.early_copies(1))

    late = {
        (0, 1): ((first_gather.done, 1),),
        (0, 2): ((first_gather.done, 0), (second_gather.advance, 1, 1, 0)),
        (0, 3): ((first_gather.done, 2), (second_gather.advance, 1, 2)),
        (1, 0): ((second_gather.advance, 2, 2),),
        (1, 1): ((second_gather.advance, 3, 1, 0),),
        (1, 2): ((second_gather.advance, 3, 2), (forward_early,)),
    }

    for r in range(own_rows):
        if r == 1:
            second_gather.advance(2, 1, 0)
            begin(third_gather.early_copies(0))
            for n in range(1, own_rows):
                rows_here(n)
            begin(keep)
        mask_ref[...] = jnp.where(seg_cols[:, r : r + 1] == seg_rows[r : r + 1], 0.0, NEG)
        acc_ref[...] = jnp.zeros_like(acc_ref)

        def one_group(i, _):
            m = chunk_of(at, model_size - 1 - i)
            for step in range(model_size):
                if (r, step) in late:
                    @pl.when(i == step)
                    def _():
                        for action, *args in late[r, step]:
                            action(*args)

            bias = vecgot_ref[m].T[: 3 * group_dim, 0:1]
            low = (mm(wa_ref[m, : 3 * group_dim, :], x_ref[r], NT) + bias).astype(BF16)
            qkv_ref[r, m] = low
            for j in range(group_dim // HEAD_DIM):
                rows = slice(j * HEAD_DIM, (j + 1) * HEAD_DIM)
                q_t = low[rows] * HEAD_DIM ** (-0.5)
                k_t = low[group_dim + rows.start : group_dim + rows.stop]
                v_t = low[2 * group_dim + rows.start : 2 * group_dim + rows.stop]
                scores = mm(k_t, q_t, TN) + mask_ref[...]
                top = jnp.max(scores, axis=0, keepdims=True)
                terms = jnp.exp(scores - top)
                total = jnp.sum(terms, axis=0, keepdims=True)
                ctx_t = mm(v_t, terms.astype(BF16)) / total
                ctx_ref[r, m, rows, :] = ctx_t.astype(BF16)
                lse_ref[r, m, j : j + 1, :] = top + jnp.log(total)
            acc_ref[...] += mm(ctx_ref[r, m], wa_ref[m, 3 * group_dim :, :], TN)
            return 0

        lax.fori_loop(0, model_size, one_group, 0)
        xhat, rstd = norm_parts(x_ref[r].astype(F32) + (acc_ref[...] + bout_ref[...].reshape(1, dim)))
        xhat_ref[r] = xhat
        rstd_ref[r] = rstd

    second_gather.done(0, 1, 2)
    arrive(third_gather.early_copies(1))
    for copy in keep:
        copy.wait()
    for gather in gathers:
        gather.sent()
    sent(third_gather.early_copies(0) + third_gather.early_copies(1))
    sent(vec_copies())
    for cut in range(CUTS):
        sent(batch_copies(cut))
        for r in range(own_rows):
            sent(row_copies(cut, r))


def enter(exit_flag, target, rows_in, seg, labels, weights, w_qkv, w_out, b_qv, b_up, b_out, w_b, w_c,
          own_rows, batch_size, model_size):
    row_count, token_part, dim = rows_in.shape
    seq = token_part * model_size
    capacity = own_rows * model_size
    depth = (capacity + batch_size - 1) // batch_size
    group_dim = dim // model_size
    pairs = labels.shape[1]
    tag_wide = 128 + seq
    smem = pl.BlockSpec(memory_space=pltpu.SMEM)
    vmem = pl.BlockSpec(memory_space=pltpu.VMEM)
    hbm = pl.BlockSpec(memory_space=pl.ANY)
    full = jax.ShapeDtypeStruct((model_size, dim, dim), BF16)
    f32 = lambda *shape: jax.ShapeDtypeStruct(shape, F32)
    low = lambda *shape: jax.ShapeDtypeStruct(shape, BF16)
    moves = (CUTS + 1) * (batch_size + model_size) + CUTS * own_rows * model_size
    return pl.pallas_call(
        functools.partial(enter_kernel, depth, pairs),
        in_specs=[smem, smem] + [vmem] * 9 + [hbm, hbm],
        out_specs=[vmem, vmem, vmem, hbm, hbm, hbm, hbm] + [vmem] * 5,
        out_shape=(
            f32(8, tag_wide),
            f32(batch_size, 8, tag_wide),
            f32(model_size, 8, dim),
            low(own_rows, seq, dim),
            full,
            full,
            low(3, 2, dim // 16, dim),
            low(own_rows, model_size, 3 * group_dim, seq),
            low(own_rows, model_size, group_dim, seq),
            f32(own_rows, model_size, group_dim // HEAD_DIM, seq),
            f32(own_rows, seq, dim),
            f32(own_rows, seq, 1),
        ),
        scratch_shapes=[
            pltpu.VMEM((-(-row_count // 8) * 8, tag_wide), F32),
            pltpu.VMEM((8, dim), F32),
            pltpu.VMEM((dim, dim), BF16),
            pltpu.VMEM((batch_size * depth, token_part, dim), BF16),
            pltpu.VMEM((capacity, token_part, dim), BF16),
            pltpu.VMEM((own_rows, seq, dim), BF16),
            pltpu.VMEM((model_size, dim, dim), BF16),
            pltpu.VMEM((batch_size, 8, tag_wide), F32),
            pltpu.VMEM((batch_size, 8, tag_wide), F32),
            pltpu.VMEM((capacity, 8, tag_wide), F32),
            pltpu.VMEM((model_size, 8, dim), F32),
            pltpu.VMEM((seq, seq), F32),
            pltpu.VMEM((seq, dim), F32),
            pltpu.SemaphoreType.DMA((3, GATHER_SEMS)),
            pltpu.SemaphoreType.DMA((3, GATHER_SEMS)),
            pltpu.SemaphoreType.DMA((moves,)),
            pltpu.SemaphoreType.DMA((moves,)),
            pltpu.SemaphoreType.DMA((5,)),
            *[pltpu.VMEM((batch_size * depth, token_part, dim // CUTS), BF16) for _ in range(CUTS)],
        ],
        compiler_params=pltpu.CompilerParams(
            vmem_limit_bytes=VMEM_MOST, collective_id=0, has_side_effects=True
        ),
        name="enter",
    )(
        exit_flag, target, rows_in, seg, labels.T, weights.T, jnp.transpose(w_qkv, (0, 2, 1)), w_out, b_qv, b_up, b_out,
        w_b, w_c,
    )


def leave_kernel(
    depth, pairs,
    exit_ref, target_ref, tags_ref, own_ref, x_ref, gres_hbm, wa_ref, qkv_hbm, ctx_ref, lse_ref,
    dwb_hbm, ownc_ref, hand_ref, pack_ref,
    rows_ref, mats_ref, sums_ref, bias_ref,
    work_ref, acc_ref, mask_ref, p_ref, s_ref, xflip_ref, gflip_ref, dx_ref, dwa_ref,
    own_half, *rest,
):
    parts_a, parts_b, parts_c, rest = rest[:7], rest[7:14], rest[14:19], rest[19:]
    (
        small_acc, small_got, small_z, bias_acc, bias_got, bias_z, back_ref, back_got,
        msend, mrecv, ssend, srecv, bsend, brecv, rsend, rrecv, local_sem, *mine_refs,
    ) = rest
    row_count, seq, dim = x_ref.shape
    model_size = wa_ref.shape[0]
    batch_size = tags_ref.shape[0]
    group_dim = ctx_ref.shape[2]
    token_part = seq // model_size
    capacity = row_count * model_size
    others = model_size - 1
    at = mesh_place()
    b, z, lo, hi = at["b"], at["z"], at["lo"], at["hi"]
    far, twin, side = at["far"], at["twin"], at["side"]

    def shard(i):
        return {"mp": (z + i) % model_size}

    first = Reduce(at, model_size, dwb_hbm, own_half, *parts_b, mats_ref.at[1], msend.at[1], mrecv.at[1])
    second = Reduce(at, model_size, dwa_ref, dwa_ref.at[:, :, lo], *parts_a, mats_ref.at[0], msend.at[0], mrecv.at[0], 2, True)
    third = Finish(at, model_size, ownc_ref, hand_ref, *parts_c, mats_ref.at[2], msend.at[2], mrecv.at[2])

    def small_copies(stage):
        def one(slot, src, dst, device):
            return remote(src, dst, ssend.at[slot], srecv.at[slot], device)

        if stage == 0:
            return [one(0, pack_ref.at[1 - lo], small_got.at[0], twin)]
        if stage < 3:
            return [one(stage, small_acc.at[stage - 1], small_got.at[stage], (far, side)[stage - 1])]
        if stage == 3:
            return [
                one(2 + i, small_acc.at[2, (z + i) % model_size], small_z.at[i - 1], shard(i))
                for i in range(1, model_size)
            ]
        if stage == 4:
            return [
                one(2 + others + i, sums_ref.at[lo, z], sums_ref.at[lo, z], shard(i))
                for i in range(1, model_size)
            ]
        return [one(3 + 2 * others, sums_ref.at[lo], sums_ref.at[lo], twin)]

    def bias_copies(stage):
        def one(slot, src, dst, device):
            return remote(src, dst, bsend.at[slot], brecv.at[slot], device)

        if stage < 3:
            return [one(stage, bias_acc.at[stage], bias_got.at[stage], (twin, far, side)[stage])]
        return [
            one(2 + i, bias_acc.at[3, (z + i) % model_size], bias_z.at[i - 1], shard(i))
            for i in range(1, model_size)
        ]

    wide = dim // CUTS

    def row_copies(r, cut):
        columns = pl.ds(cut * wide, wide)
        first = (r * CUTS + cut) * others - 1
        return [
            remote(
                dx_ref.at[r, pl.ds(pl.multiple_of((z + i) % model_size * token_part, 128), token_part), columns],
                mine_refs[cut].at[z * row_count + r],
                rsend.at[first + i], rrecv.at[first + i], shard(i),
            )
            for i in range(1, model_size)
        ]

    def batch_copies(cut):
        columns = pl.ds(cut * wide, wide)
        first = row_count * CUTS * others + cut * (batch_size - 1) - 1
        copies = []
        for j in range(1, batch_size):
            t = (b + j) % batch_size
            copies.append(remote(
                back_ref.at[pl.ds(t * depth, depth), :, columns],
                back_got.at[pl.ds(b * depth, depth), :, columns],
                rsend.at[first + j], rrecv.at[first + j], {"batch": t},
            ))
        return copies

    def local_copies():
        return [
            pltpu.make_async_copy(dwb_hbm.at[:, :, lo], own_half, local_sem.at[0]),
        ]

    def inputs():
        return [
            pltpu.make_async_copy(qkv_hbm, work_ref, local_sem.at[2]),
            pltpu.make_async_copy(gres_hbm, acc_ref, local_sem.at[3]),
        ]

    def small_step(stage):
        arrive(small_copies(stage))
        if stage == 0:
            small_acc[0] = pack_ref[lo] + small_got[0]
        if stage in (1, 2):
            small_acc[stage] = small_acc[stage - 1] + small_got[stage]
        if stage == 3:
            total = small_acc[2, z]
            for i in range(others):
                total += small_z[i]
            sums_ref[lo, z] = total
        if stage < 5:
            begin(small_copies(stage + 1))

    def bias_step(stage):
        arrive(bias_copies(stage))
        if stage < 3:
            bias_acc[stage + 1] = bias_acc[stage] + bias_got[stage]
            begin(bias_copies(stage + 1))
        else:
            total = bias_acc[3, z]
            for i in range(others):
                total += bias_z[i]
            bias_ref[...] = total

    begin(inputs())
    begin(local_copies())
    greet(at, batch_size, model_size)
    begin(small_copies(0))
    third.start()
    for i in range(model_size):
        first.start(i)
    seg_rows = own_ref[:, own_ref.shape[1] - seq :]
    seg_cols = seg_rows.T
    for copy in inputs() + local_copies():
        copy.wait()

    steps = {
        0: [],
        1: [(small_step, 0), (third.after_one,), (first.after_core, 0)],
        2: [(first.after_core, 1), (first.after_one, 0)],
        3: [(first.after_core, 2), (first.after_one, 1), (first.after_two, 0), (small_step, 1), (third.after_two,)],
        4: [(first.after_core, 3), (first.after_one, 2), (first.after_two, 1), (small_step, 2)],
        5: [(first.after_one, 3), (first.after_two, 2), (small_step, 3), (third.after_three,)],
        6: [(second.after_core, 0), (first.after_two, 3), (small_step, 4)],
        7: [(second.after_core, 1), (second.after_one, 0), (first.after_three,)],
    }

    def weight_grads(i):
        m, rows_y = chunk_of(at, i), dim // 2

        def one(y, _):
            part = pl.ds(pl.multiple_of(y * rows_y, 128), rows_y)
            left, right = 0.0, 0.0
            for q in range(row_count):
                cols = slice(q * seq, (q + 1) * seq)
                left += mm(xflip_ref[part, cols], work_ref[q, m], NT)
                right += mm(gflip_ref[part, cols], ctx_ref[q, m], NT)
            shape = dwa_ref.shape[2:-1]
            dwa_ref[m, y, :, :, :, :, : 3 * group_dim] = left.astype(BF16).reshape(*shape, 3 * group_dim)
            dwa_ref[m, y, :, :, :, :, 3 * group_dim :] = right.astype(BF16).reshape(*shape, group_dim)
            return 0

        lax.fori_loop(0, 2, one, 0)

    for r in range(row_count):
        mask_ref[...] = jnp.where(seg_cols[:, r : r + 1] == seg_rows[r : r + 1], 0.0, NEG)
        grad_low = acc_ref[r].astype(BF16)
        columns = slice(r * seq, (r + 1) * seq)
        gflip_ref[:, columns] = grad_low.T
        xflip_ref[:, columns] = x_ref[r].T

        def one_group(i, _):
            if r == row_count - 1:
                @pl.when(i > 0)
                def _():
                    weight_grads(i - 1)

            for step in range(model_size):
                @pl.when(i == step)
                def _():
                    if r == row_count - 1 and step > 0:
                        second.start(step - 1)
                    for action, *args in steps[r * model_size + step]:
                        action(*args)

            m = chunk_of(at, i)
            grad_ctx = mm(wa_ref[m, 3 * group_dim :, :], grad_low, NT).astype(BF16)

            def store(rows, value):
                work_ref[r, m, rows, :] = value

            backward_group(
                grad_ctx, lambda rows: ctx_ref[r, m, rows, :], lambda rows: work_ref[r, m, rows, :], store,
                mask_ref, lambda j: lse_ref[r, m, j : j + 1, :], group_dim, p_ref, s_ref,
            )
            grads = work_ref[r, m]
            found = mm(jnp.ones((8, seq), BF16), grads, NT)
            if r == 0:
                bias_acc[0, m] = found
            else:
                bias_acc[0, m] = bias_acc[0, m] + found
            acc_ref[r] = acc_ref[r] + mm(grads, wa_ref[m, : 3 * group_dim, :], TN)
            return 0

        lax.fori_loop(0, model_size, one_group, 0)
        dx_ref[r] = acc_ref[r].astype(BF16)
        for cut in range(CUTS if r < row_count - 1 else 2):
            begin(row_copies(r, cut))

    weight_grads(model_size - 1)
    second.start(model_size - 1)
    for r in range(row_count):
        for cut in range(CUTS):
            part = pl.ds(pl.multiple_of(z * token_part, 128), token_part)
            mine_refs[cut][z * row_count + r] = dx_ref[r, part, cut * wide : (cut + 1) * wide]
    second.after_core(2)
    slots = slots_of_tags(tags_ref, depth, 2 * pairs, capacity)

    def give(cut):
        columns = pl.ds(cut * wide, wide)
        for k, (place, live) in enumerate(slots):
            found = mine_refs[cut][place].astype(F32) * live.astype(F32)
            back_ref[k, :, columns] = found.astype(BF16)
        begin(batch_copies(cut))

    def returned(cut):
        for r in range(row_count):
            arrive(row_copies(r, cut))
        if cut + 2 < CUTS:
            begin(row_copies(row_count - 1, cut + 2))
        give(cut)

    returned(0)
    second.after_core(3)
    second.after_one(1)
    second.after_two(0)
    begin(bias_copies(0))
    returned(1)
    second.after_one(2)
    second.after_two(1)
    first.after_four()
    returned(2)
    second.after_one(3)
    second.after_two(2)
    bias_step(0)
    small_step(5)
    own_slots = pl.ds(b * depth, depth)
    back_got[own_slots] = back_ref[own_slots]
    bias_step(1)
    second.after_two(3)
    second.after_three()
    bias_step(2)
    third.done()
    bias_step(3)
    flat = slot_of_rows(exit_ref, target_ref, depth)
    for cut in range(CUTS):
        arrive(batch_copies(cut))

    for r in range(rows_ref.shape[0]):
        k = jnp.minimum(jnp.maximum(flat[r], 0), batch_size * depth - 1)
        alive = jnp.where(flat[r] >= 0, 1.0, 0.0)
        rows_ref[r] = (back_got[k].astype(F32) * alive).astype(BF16)
    for reducer in (first, second):
        reducer.done()
        reducer.sent()
    third.sent()
    for stage in range(6):
        sent(small_copies(stage))
    for stage in range(4):
        sent(bias_copies(stage))
    for cut in range(CUTS):
        for r in range(row_count):
            sent(row_copies(r, cut))
        sent(batch_copies(cut))


def leave(exit_flag, target, tags, own, x, gres, w_a, qkv, ctx, lse, d_wb, mat_c, hand, pack, row_total, batch_size, pairs):
    rows, seq, dim = x.shape
    model_size = w_a.shape[0]
    group_dim = dim // model_size
    token_part = seq // model_size
    capacity = rows * model_size
    depth = (capacity + batch_size - 1) // batch_size
    slots = batch_size * depth
    piece = dim // 16
    others = model_size - 1
    grid_shape = (model_size, 2, 2, PARTS, 2, piece, dim)
    pack_shape = (2, model_size, pack.shape[0] // (2 * model_size), pack.shape[1])
    smem = pl.BlockSpec(memory_space=pltpu.SMEM)
    vmem = pl.BlockSpec(memory_space=pltpu.VMEM)
    hbm = pl.BlockSpec(memory_space=pl.ANY)
    dma = pltpu.SemaphoreType.DMA
    low = lambda *shape: pltpu.VMEM(shape, BF16)
    f32 = lambda *shape: pltpu.VMEM(shape, F32)
    row_moves = CUTS * (rows * others + batch_size - 1)
    return pl.pallas_call(
        functools.partial(leave_kernel, depth, pairs),
        in_specs=[smem, smem, vmem, vmem, vmem, hbm, vmem, hbm, vmem, vmem, hbm, vmem, vmem, vmem],
        out_specs=[vmem, vmem, vmem, vmem],
        out_shape=(
            jax.ShapeDtypeStruct((row_total, token_part, dim), BF16),
            jax.ShapeDtypeStruct((3,) + grid_shape[2:], BF16),
            jax.ShapeDtypeStruct(pack_shape, F32),
            jax.ShapeDtypeStruct((8, 3 * group_dim), F32),
        ),
        scratch_shapes=[
            low(rows, model_size, 3 * group_dim, seq),
            f32(rows, seq, dim),
            f32(seq, seq),
            low(2, seq, seq),
            low(2, seq, seq),
            low(dim, rows * seq),
            low(dim, rows * seq),
            low(rows, seq, dim),
            low(*grid_shape),
            low(model_size, 2, PARTS, 2, piece, dim),
            *reduce_scratch(model_size, piece, dim),
            *reduce_scratch(model_size, piece, dim),
            low(2, piece, dim),
            low(2, piece, dim),
            low(piece, dim),
            low(piece, dim),
            low(PARTS, piece, dim),
            f32(3, *pack_shape[1:]),
            f32(3, *pack_shape[1:]),
            f32(others, *pack_shape[2:]),
            f32(4, model_size, 8, 3 * group_dim),
            f32(3, model_size, 8, 3 * group_dim),
            f32(others, 8, 3 * group_dim),
            low(slots, token_part, dim),
            low(slots, token_part, dim),
            dma((3, REDUCE_SEMS)),
            dma((3, REDUCE_SEMS)),
            dma((4 + 2 * others,)),
            dma((4 + 2 * others,)),
            dma((3 + others,)),
            dma((3 + others,)),
            dma((row_moves,)),
            dma((row_moves,)),
            dma((4,)),
            *[low(capacity, token_part, dim // CUTS) for _ in range(CUTS)],
        ],
        compiler_params=pltpu.CompilerParams(
            vmem_limit_bytes=VMEM_MOST, collective_id=2, has_side_effects=True
        ),
        name="leave",
    )(
        exit_flag, target, tags, own, x, gres, w_a, qkv, ctx, lse,
        d_wb.reshape(grid_shape), mat_c, hand, pack.reshape(pack_shape),
    )


def finish_kernel(
    classes, mats_ref, sums_ref, bias_ref,
    gqkv_ref, gbqv_ref, gout_ref, gbout_ref, ggain_ref, gshift_ref, gup_ref, gbup_ref, gdown_ref, gbdown_ref,
    gsw1_ref, gsbias_ref, gquery_ref, gsw2_ref, gsw3_ref, gsb3_ref,
):
    dim, width = gsw1_ref.shape
    group_dim = gout_ref.shape[0]
    b, z = lax.axis_index("batch"), lax.axis_index("mp")
    w2_at, w3_at, small_at, vec_at, bup_at = pack_places(dim, width)
    blocks = dim // width

    def vector(first, row):
        return jnp.concatenate([sums_ref[first + j * 8 + row : first + j * 8 + row + 1] for j in range(blocks)], axis=1)

    def share(value, parts):
        size = value.shape[1] // parts
        return sum(jnp.where(b == i, 1.0, 0.0) * value[:, i * size : (i + 1) * size] for i in range(parts))

    parts = dim // gbup_ref.shape[-1]
    flipped = mats_ref[0].astype(F32).T
    for j in range(3):
        gqkv_ref[j] = flipped[j * group_dim : (j + 1) * group_dim]
    gout_ref[...] = flipped[3 * group_dim :]
    gup_ref[...] = mats_ref[1].astype(F32)
    gdown_ref[...] = mats_ref[2].astype(F32).T
    for n in range(2):
        gbqv_ref[n : n + 1] = share(bias_ref[0:1, 2 * n * group_dim : (2 * n + 1) * group_dim], parts)
    gbout_ref[...] = (vector(vec_at.start, 5)).reshape(dim)
    for n in range(2):
        ggain_ref[n : n + 1] = vector(vec_at.start, n)
        gshift_ref[n : n + 1] = vector(vec_at.start, 2 + n)
    gbdown_ref[...] = (vector(vec_at.start, 4)).reshape(dim)
    ups = [vector(bup_at.start, m) for m in range(dim // group_dim)]
    gbup_ref[...] = (share(sum(jnp.where(z == m, 1.0, 0.0) * ups[m] for m in range(len(ups))), parts)).reshape(gbup_ref.shape[0])
    for j in range(blocks):
        gsw1_ref[j * width : (j + 1) * width] = sums_ref[j * width : (j + 1) * width].T
    gsbias_ref[...] = sums_ref[small_at.start : small_at.start + 2]
    gquery_ref[...] = (sums_ref[small_at.start + 2 : small_at.start + 3]).reshape(width)
    gsb3_ref[...] = (sums_ref[small_at.start + 3 : small_at.start + 4][:, :classes]).reshape(classes)
    gsw2_ref[...] = sums_ref[w2_at]
    gsw3_ref[...] = sums_ref[w3_at][:classes]


def finish(mats, sums, bias, model_size, classes):
    depth, dim = mats.shape[1:]
    width = sums.shape[1]
    group_dim = dim // model_size
    batch_size = dim // depth
    f32 = lambda *shape: jax.ShapeDtypeStruct(shape, F32)
    return pl.pallas_call(
        functools.partial(finish_kernel, classes),
        out_shape=(
            f32(3, group_dim, depth),
            f32(2, group_dim // batch_size),
            f32(group_dim, depth),
            f32(dim),
            f32(2, dim),
            f32(2, dim),
            f32(depth, dim),
            f32(depth),
            f32(dim, depth),
            f32(dim),
            f32(dim, width),
            f32(2, width),
            f32(width),
            f32(width, width),
            f32(classes, width),
            f32(classes),
        ),
        compiler_params=pltpu.CompilerParams(vmem_limit_bytes=VMEM_MOST),
        name="finish",
    )(mats, sums, bias)


def rows_back(grad_x, exit_flag, target, live, slot_depth):
    batch_size, model_size = lax.axis_size("batch"), lax.axis_size("mp")
    own_rows, seq, dim = grad_x.shape
    row_count = exit_flag.shape[0]
    capacity, slot_count = own_rows * model_size, batch_size * slot_depth
    alive_rows = 1 - exit_flag > 0
    same_goal = (target[:, None] == target[None, :]) & alive_rows[:, None] & alive_rows[None, :]
    row_order = jnp.arange(row_count, dtype=jnp.int32)
    slot_in = jnp.sum(
        (same_goal & (row_order[None, :] < row_order[:, None])).astype(jnp.int32), axis=1
    )
    flat_slot = target * slot_depth + slot_in
    send_low = (
        (jnp.arange(slot_count, dtype=jnp.int32)[:, None] == flat_slot[None, :]) & alive_rows[None, :]
    ).astype(BF16)
    live_flat = live.reshape(-1)
    position = jnp.cumsum(live_flat.astype(jnp.int32)) - 1
    pick_low = (
        (jnp.arange(capacity, dtype=jnp.int32)[:, None] == position[None, :]) & (live_flat[None, :] > 0)
    ).astype(BF16)
    mine = lax.all_to_all(grad_x, "mp", split_axis=1, concat_axis=0, tiled=True)
    back = jnp.einsum("ck,csd->ksd", pick_low, mine, preferred_element_type=F32).astype(BF16)
    back = back.reshape((batch_size, slot_depth) + back.shape[1:])
    got = lax.all_to_all(back, "batch", split_axis=0, concat_axis=0, tiled=True)
    got = got.reshape((slot_count,) + got.shape[2:])
    return jnp.einsum("kr,ksd->rsd", send_low, got, preferred_element_type=F32).astype(BF16)


def matrix_sums(grads):
    sums = []
    for grad in grads:
        part = lax.psum_scatter(grad, "mp", scatter_dimension=0, tiled=True)[0]
        part = lax.psum_scatter(part, "batch", scatter_dimension=0, tiled=True)
        sums.append(lax.psum(part, "grp"))
    return sums


def on_device(
    rows_in, segment_ids, pair_labels, pair_mask, exit_flag, target, cot_out,
    w_qkv, b_qv, w_out, b_out, ln_gain, ln_bias, w_up, b_up, w_down, b_down,
    s_w1, s_bias, s_query, s_w2, s_w3, s_b3,
):
    batch_size = lax.axis_size("batch")
    model_size = lax.axis_size("mp")
    row_count, _, model_dim = rows_in.shape
    own_rows = cot_out.shape[0]
    capacity = own_rows * model_size
    slot_depth = (capacity + batch_size - 1) // batch_size
    pair_count = pair_labels.shape[1]
    my_mp = lax.axis_index("mp")
    own, got_tags, vecs, rows_own, w_a, w_b, early, qkv, ctx, lse, xhat_one, rstd_one = enter(
        exit_flag, target, rows_in, segment_ids, pair_labels, pair_mask, w_qkv, w_out, b_qv, b_up, b_out,
        w_up, w_down, own_rows, batch_size, model_size,
    )
    scatter = batch_size == 2
    mixed_out, grad_resid, d_wb, mat_c, hand, pack = ffn_both(
        xhat_one, rstd_one, ln_gain, ln_bias, w_b, w_down, early, vecs, b_down, cot_out, own, pair_count, scatter,
        s_w1, s_bias, s_query, s_w2, s_w3, s_b3,
    )
    if scatter:
        grad_rows, mats, sums, bias_sum = leave(
            exit_flag, target, got_tags, own, rows_own, grad_resid, w_a, qkv, ctx, lse, d_wb, mat_c, hand, pack,
            row_count, batch_size, pair_count,
        )
        mats = mats.reshape(3, model_dim // batch_size, model_dim)
        sums = sums.reshape(pack.shape)
    else:
        grad_x, d_wa, bias_part = attn_backward(rows_own, grad_resid, w_a, qkv, ctx, lse, own)
        grad_rows = rows_back(grad_x, exit_flag, target, got_tags[:, :slot_depth, 2 * pair_count], slot_depth)
        whole = (model_size, model_dim, model_dim)
        mats = matrix_sums((d_wa, d_wb.reshape(whole), mat_c.reshape(whole)))
        sums, bias_sum = lax.psum((pack, bias_part[:, 0]), ("grp", "batch", "mp"))
        bias_sum = lax.dynamic_index_in_dim(bias_sum, my_mp, 0)
        mats = jnp.stack(mats)

    (
        g_wqkv, g_bqv, g_wout, g_bout, g_gain, g_shift, g_wup, g_bup, g_wdown, g_bdown,
        g_sw1, g_sbias, g_query, g_sw2, g_sw3, g_sb3,
    ) = finish(mats, sums, bias_sum, model_size, s_w3.shape[1])
    return (
        mixed_out, grad_rows, jnp.transpose(g_wqkv, (0, 2, 1)), g_bqv, g_wout, g_bout, g_gain, g_shift, g_wup,
        g_bup, g_wdown, g_bdown, g_sw1, g_sbias, g_query, g_sw2, g_sw3.T, g_sb3,
    )


def solution(mesh):
    return jax.shard_map(
        on_device,
        mesh=mesh,
        in_specs=(
            P(("grp", "batch"), "mp", None),
            P(("grp", "batch"), None),
            P(("grp", "batch"), None),
            P(("grp", "batch"), None),
            P(("grp", "batch")),
            P(("grp", "batch")),
            P(("grp", "batch", "mp"), None, None),
            P(None, None, "mp"),
            P(None, "mp"),
            P("mp", None),
            P(),
            P(),
            P(),
            P(None, "mp"),
            P("mp"),
            P("mp", None),
            P(),
            P(),
            P(),
            P(),
            P(),
            P(),
            P(),
        ),
        out_specs=(
            P(("grp", "batch", "mp"), None, None),
            P(("grp", "batch"), "mp", None),
            P(None, "batch", "mp"),
            P(None, ("mp", "batch")),
            P("mp", "batch"),
            P(),
            P(),
            P(),
            P("batch", "mp"),
            P(("mp", "batch")),
            P("mp", "batch"),
            P(),
            P(),
            P(),
            P(),
            P(),
            P(),
            P(),
        ),
        check_vma=False,
    )
```

```python
import functools

import jax
import jax.numpy as jnp
from jax import lax
from jax.experimental import pallas as pl
from jax.experimental.pallas import tpu as pltpu
from jax.sharding import PartitionSpec as P

HEAD_DIM = 64
EPS = 1e-12
NEG = -1000000000.0
PRECISE = lax.Precision.HIGHEST
F32 = jnp.float32
BF16 = jnp.bfloat16
BLOCK = 512
VMEM_MOST = 62 * 1024 * 1024
NN = (((1,), (0,)), ((), ()))
NT = (((1,), (1,)), ((), ()))
TN = (((0,), (0,)), ((), ()))


def mm(left, right, dims=NN):
    return lax.dot_general(left, right, dims, preferred_element_type=F32)


def mm_exact(left, right, dims=NN):
    return lax.dot_general(left, right, dims, precision=PRECISE, preferred_element_type=F32)


def norm_parts(resid):
    center = resid - jnp.mean(resid, axis=-1, keepdims=True)
    spread = jnp.mean(center * center, axis=-1, keepdims=True)
    rstd = lax.rsqrt(spread + EPS)
    return center * rstd, rstd


def norm_back(upstream, xhat, rstd, gain):
    scaled = upstream * gain
    mean_u = jnp.mean(scaled, axis=-1, keepdims=True)
    mean_ux = jnp.mean(scaled * xhat, axis=-1, keepdims=True)
    return (scaled - mean_u - xhat * mean_ux) * rstd


def column_sum(value):
    return jnp.sum(value, axis=0, keepdims=True)


def mesh_place():
    g, b, z = lax.axis_index("grp"), lax.axis_index("batch"), lax.axis_index("mp")
    hi, lo, bit = g // 2, g % 2, b % 2
    return dict(
        g=g, b=b, z=z, hi=hi, lo=lo, bit=bit,
        far={"grp": (1 - hi) * 2 + lo}, twin={"grp": hi * 2 + 1 - lo}, side={"batch": b + 1 - 2 * bit},
        far_twin={"grp": (1 - hi) * 2 + 1 - lo},
    )


def remote(src, dst, send_sem, recv_sem, device):
    return pltpu.make_async_remote_copy(
        src_ref=src, dst_ref=dst, send_sem=send_sem, recv_sem=recv_sem,
        device_id=device, device_id_type=pl.DeviceIdType.MESH,
    )


def greet(at, batch_size, model_size):
    barrier = pltpu.get_barrier_semaphore()
    peers = [at["far"], at["twin"]]
    if batch_size > 1:
        peers += [{"batch": (at["b"] + j) % batch_size} for j in range(1, batch_size)]
    else:
        peers += [at["side"]]
    peers += [{"mp": (at["z"] + i) % model_size} for i in range(1, model_size)]
    for peer in peers:
        pl.semaphore_signal(barrier, inc=1, device_id=peer, device_id_type=pl.DeviceIdType.MESH)
    pl.semaphore_wait(barrier, len(peers))


def begin(copies):
    for copy in copies:
        copy.start()


def arrive(copies):
    for copy in copies:
        copy.wait_recv()


def sent(copies):
    for copy in copies:
        copy.wait_send()


class Gather:
    def __init__(self, at, model_size, home, spot, send_sem, recv_sem, early=None):
        self.at, self.home, self.spot, self.early = at, home, spot, early
        self.send_sem, self.recv_sem = send_sem, recv_sem
        z, lo, hi, bit = at["z"], at["lo"], at["hi"], at["bit"]
        self.near = z + 1 - 2 * (z % 2)
        self.cross = (z + 2) % model_size
        self.chunks = (self.near, self.cross, (self.near + 2) % model_size)
        piece = home.shape[0] // 16
        half = pl.multiple_of(lo * (8 * piece), 16)
        self.one_a = pl.ds(pl.multiple_of(half + bit * (2 * piece) + hi * piece, 16), piece)
        self.one_b = pl.ds(pl.multiple_of(half + 4 * piece + hi * (2 * piece) + bit * piece, 16), piece)
        self.two_a = pl.ds(pl.multiple_of(half + bit * (2 * piece), 16), 2 * piece)
        self.two_b = pl.ds(pl.multiple_of(half + 4 * piece + hi * (2 * piece), 16), 2 * piece)
        rows = lambda first, count: pl.ds(pl.multiple_of(half + first * piece, 16), count * piece)
        self.pieces = (
            (self.one_a, self.one_b),
            (rows(bit * 2 + 1 - hi, 1), rows(4 + hi * 2 + 1 - bit, 1)),
            (rows(2 - 2 * bit, 2), rows(6 - 2 * hi, 2)),
        )

    def copies(self, stage, i):
        at, home, spot = self.at, self.home, self.spot

        def one(slot, src, dst, device):
            return remote(src, dst, self.send_sem.at[slot], self.recv_sem.at[slot], device)

        def same(slot, m, rows, device):
            return one(slot, spot.at[m, rows], spot.at[m, rows], device)

        m = self.chunks[i]
        if stage == 0 and i < 2:
            return [
                one(2 * i, home.at[self.one_a], spot.at[at["z"], self.one_a], {"mp": m}),
                one(2 * i + 1, home.at[self.one_b], spot.at[at["z"], self.one_b], {"mp": m}),
            ]
        if stage == 0:
            return [
                same(4, self.cross, self.one_a, {"mp": self.near}),
                same(5, self.cross, self.one_b, {"mp": self.near}),
            ]
        if stage == 1 and self.early is not None:
            return [
                one(6 + 2 * i, self.early.at[i, 0], spot.at[m, self.one_a], at["far"]),
                one(7 + 2 * i, self.early.at[i, 1], spot.at[m, self.one_b], at["side"]),
            ]
        if stage == 1:
            return [same(6 + 2 * i, m, self.one_a, at["far"]), same(7 + 2 * i, m, self.one_b, at["side"])]
        if stage == 2:
            return [same(12 + 2 * i, m, self.two_a, at["side"]), same(13 + 2 * i, m, self.two_b, at["far"])]
        raise ValueError(stage)

    def to_twin(self, stage, i):
        m, twin = self.chunks[i], self.at["twin"]
        source = [self.spot.at[m, rows] for rows in self.pieces[stage]]
        if stage == 0 and self.early is not None:
            source = [self.early.at[i, p] for p in range(2)]
        slot = 18 + 6 * i + 2 * stage
        return [
            remote(src, self.spot.at[m, rows], self.send_sem.at[slot + n], self.recv_sem.at[slot + n], twin)
            for n, (src, rows) in enumerate(zip(source, self.pieces[stage]))
        ]

    def start(self):
        begin(self.copies(0, 1) + self.copies(0, 0))

    def early_copies(self, stage):
        def one(slot, src, dst, device):
            return remote(src, dst, self.send_sem.at[slot], self.recv_sem.at[slot], device)

        if stage == 0:
            return [
                one(2 * i + p, self.home.at[rows], self.early.at[i, p], {"mp": self.chunks[i]})
                for i in (1, 0)
                for p, rows in enumerate((self.one_a, self.one_b))
            ]
        return [one(4 + p, self.early.at[1, p], self.early.at[2, p], {"mp": self.near}) for p in range(2)]

    def own_pieces(self, sem):
        return [
            pltpu.make_async_copy(self.early.at[i, p], self.spot.at[self.chunks[i], rows], sem.at[2 * i + p])
            for i in range(3)
            for p, rows in enumerate((self.one_a, self.one_b))
        ]

    def advance(self, stage, *parts):
        for i in parts:
            arrive(self.copies(stage - 1, i))
            if stage == 1 and i == 1:
                begin(self.copies(0, 2))
            begin((self.copies(stage, i) if stage < 3 else []) + self.to_twin(stage - 1, i))

    def done(self, *parts):
        for i in parts:
            for stage in range(3):
                arrive(self.to_twin(stage, i))

    def sent(self):
        for stage in range(3):
            for i in range(3):
                if stage > 0 or self.early is None:
                    sent(self.copies(stage, i))
                sent(self.to_twin(stage, i))


GATHER_SEMS = 36
PARTS = 2


class Reduce:
    def __init__(self, at, model_size, full, base, got_half, got_a, got_b, got_a2, got_b2, last, got_z, out,
                 send_sem, recv_sem, far_first=0, direct=False):
        self.far_first, self.direct = far_first, direct
        self.at, self.full, self.base, self.got_half = at, full, base, got_half
        self.got_a, self.got_b, self.got_a2, self.got_b2 = got_a, got_b, got_a2, got_b2
        self.last, self.got_z, self.out = last, got_z, out
        self.send_sem, self.recv_sem = send_sem, recv_sem
        z = at["z"]
        self.near, self.cross = z + 1 - 2 * (z % 2), (z + 2) % model_size

    def copies(self, stage, i=0):
        at, base = self.at, self.base
        b, lo, hi = at["b"], at["lo"], at["hi"]

        def one(slot, src, dst, device):
            return remote(src, dst, self.send_sem.at[slot], self.recv_sem.at[slot], device)

        m = chunk_of(at, i)
        if stage == 0:
            return [
                one(25 + 4 * i + 2 * y + p, self.full.at[m, y, 1 - lo, p], self.got_half.at[m, y, p], at["twin"])
                for y in range(2)
                for p in range(PARTS)
            ]
        if stage == 1 and i < self.far_first:
            return [
                one(4 + 2 * i, base.at[m, :, 0, 1 - hi], self.got_a.at[m], at["far"]),
                one(5 + 2 * i, base.at[m, :, 1, 1 - hi], self.got_b.at[m], at["far"]),
            ]
        if stage == 2 and i < self.far_first:
            return [
                one(12 + 2 * i, base.at[m, 1 - b, 0, hi], self.got_a2.at[m], at["side"]),
                one(13 + 2 * i, base.at[m, 1 - b, 1, hi], self.got_b2.at[m], at["side"]),
            ]
        if stage == 1:
            return [
                one(4 + 2 * i, base.at[m, :, 0, 1 - hi], self.got_a.at[m], at["far"]),
                one(5 + 2 * i, base.at[m, 1 - b, 1], self.got_b.at[m], at["side"]),
            ]
        if stage == 2:
            return [
                one(12 + 2 * i, base.at[m, 1 - b, 0, hi], self.got_a2.at[m], at["side"]),
                one(13 + 2 * i, base.at[m, b, 1, 1 - hi], self.got_b2.at[m], at["far"]),
            ]
        if stage == 3:
            device = {"mp": self.cross if i == 2 else self.near}
            return [one(20 + i, self.last.at[m], self.got_z.at[i], device)] if i < 3 else []
        mine = self.out.at[lo, :, hi]
        if stage == 4 and self.direct:
            return [one(23 + 18 * n, mine, mine, at[peer]) for n, peer in enumerate(("far", "twin", "far_twin"))]
        if stage == 4:
            return [one(23, mine, mine, at["far"])]
        if self.direct:
            return []
        return [one(24, self.out.at[lo], self.out.at[lo], at["twin"])]

    def start(self, i):
        begin(self.copies(0, i))

    def after_core(self, i, go_on=True):
        arrive(self.copies(0, i))
        m = chunk_of(self.at, i)

        def one(n, _):
            y, p, h = n // 4, n // 2 % 2, n % 2
            self.base[m, y, p, h] = self.base[m, y, p, h] + self.got_half[m, y, p, h]
            return 0

        lax.fori_loop(0, 8, one, 0)
        if go_on:
            begin(self.copies(1, i))

    def after_one(self, i):
        arrive(self.copies(1, i))
        m, b, hi, base = chunk_of(self.at, i), self.at["b"], self.at["hi"], self.base
        for h in range(2):
            base[m, h, 0, hi] = base[m, h, 0, hi] + self.got_a[m, h]
            if i < self.far_first:
                base[m, h, 1, hi] = base[m, h, 1, hi] + self.got_b[m, h]
            else:
                base[m, b, 1, h] = base[m, b, 1, h] + self.got_b[m, h]
        begin(self.copies(2, i))

    def after_two(self, i, go_on=True):
        arrive(self.copies(2, i))
        m, b, hi, base = chunk_of(self.at, i), self.at["b"], self.at["hi"], self.base
        found = [base[m, b, 0, hi] + self.got_a2[m], base[m, b, 1, hi] + self.got_b2[m]]
        if i == 2:
            arrive(self.copies(3, 0))
        for p in range(PARTS):
            self.last[m, p] = found[p] + self.got_z[0, p] if i == 2 else found[p]
        if go_on:
            begin(self.copies(3, i))

    def total(self, p):
        z = self.at["z"]
        found = self.last[z, p].astype(F32) + self.got_z[1, p].astype(F32) + self.got_z[2, p].astype(F32)
        return found.astype(BF16)

    def after_three(self):
        arrive(self.copies(3, 1) + self.copies(3, 2))
        for p in range(PARTS):
            self.out[self.at["lo"], p, self.at["hi"]] = self.total(p)
        begin(self.copies(4))

    def hand_over(self, own_ref, hand_ref):
        arrive(self.copies(3, 1))
        own_ref[...] = self.base[self.at["z"]]
        hand_ref[0] = self.last[self.cross]
        hand_ref[1] = self.got_z[1]

    def after_four(self):
        arrive(self.copies(4))
        begin(self.copies(5))

    def done(self):
        arrive(self.copies(4) if self.direct else self.copies(5))

    def sent(self):
        for stage in range(6):
            for i in range(4 if stage < 4 else 1):
                sent(self.copies(stage, i))

    def sent_early(self):
        for stage, count in enumerate((4, 3, 3, 2)):
            for i in range(count):
                sent(self.copies(stage, i))


class Finish:
    def __init__(self, at, model_size, own, hand, got_a, got_b, got_a2, got_b2, got_z, out, send_sem, recv_sem):
        self.at, self.own, self.hand, self.out = at, own, hand, out
        self.got_a, self.got_b, self.got_a2, self.got_b2, self.got_z = got_a, got_b, got_a2, got_b2, got_z
        self.send_sem, self.recv_sem = send_sem, recv_sem
        self.cross = (at["z"] + 2) % model_size

    def copies(self, stage):
        at, own = self.at, self.own
        b, lo, hi = at["b"], at["lo"], at["hi"]

        def one(slot, src, dst, device):
            return remote(src, dst, self.send_sem.at[slot], self.recv_sem.at[slot], device)

        if stage == 0:
            return [one(0, self.hand.at[0], self.got_z, {"mp": self.cross})]
        if stage == 1:
            return [
                one(1, own.at[:, 0, 1 - hi], self.got_a, at["far"]),
                one(2, own.at[1 - b, 1], self.got_b, at["side"]),
            ]
        if stage == 2:
            return [
                one(3, self.got_a.at[1 - b], self.got_a2, at["side"]),
                one(4, self.got_b.at[1 - hi], self.got_b2, at["far"]),
            ]
        if stage == 3:
            return [one(5, self.out.at[lo, :, hi], self.out.at[lo, :, hi], at["far"])]
        return [one(6, self.out.at[lo], self.out.at[lo], at["twin"])]

    def start(self):
        begin(self.copies(1) + self.copies(0))

    def after_one(self):
        arrive(self.copies(1))
        b, hi = self.at["b"], self.at["hi"]
        for h in range(2):
            self.got_a[h] = self.got_a[h] + self.own[h, 0, hi]
            self.got_b[h] = self.got_b[h] + self.own[b, 1, h]
        begin(self.copies(2))

    def after_two(self):
        arrive(self.copies(2) + self.copies(0))
        b, lo, hi = self.at["b"], self.at["lo"], self.at["hi"]
        halves = ((self.got_a[b], self.got_a2[...]), (self.got_b[hi], self.got_b2[...]))
        for p, (held, got) in enumerate(halves):
            total = held.astype(F32) + got.astype(F32) + self.hand[1, p].astype(F32) + self.got_z[p].astype(F32)
            self.out[lo, p, hi] = total.astype(BF16)
        begin(self.copies(3))

    def after_three(self):
        arrive(self.copies(3))
        begin(self.copies(4))

    def done(self):
        arrive(self.copies(4))

    def sent(self):
        for stage in range(5):
            sent(self.copies(stage))


REDUCE_SEMS = 60


def chunk_of(at, i):
    high, low = at["z"] // 2, at["z"] % 2
    flip_high, flip_low = 1 - i % 2, 1 - i // 2
    return 2 * (high + flip_high - 2 * high * flip_high) + low + flip_low - 2 * low * flip_low


def reduce_scratch(model_size, piece, dim):
    low = lambda *shape: pltpu.VMEM(shape, BF16)
    return [
        low(model_size, 2, PARTS, 2, piece, dim),
        low(model_size, 2, piece, dim),
        low(model_size, 2, piece, dim),
        low(model_size, piece, dim),
        low(model_size, piece, dim),
        low(model_size, PARTS, piece, dim),
        low(3, PARTS, piece, dim),
    ]


def pack_places(dim, width):
    ends = [dim]
    for size in (width, 16, 8, 8 * dim // width, 8 * dim // width):
        ends.append(ends[-1] + size)
    return [slice(first, last) for first, last in zip(ends[:-1], ends[1:])]


def pack_rows(dim, width):
    return -(-pack_places(dim, width)[-1].stop // 128) * 128


def student_step(
    stud_ref, own_ref, query_ref, w2_ref, bmid, w3_ref, b3_ref,
    dstud_ref, gw2_ref, gw3_ref, gsmall_ref, classes, pairs,
):
    row_count, seq, width = stud_ref.shape
    head = own_ref.shape[1] - seq
    tag_cells = [
        [own_ref[r : r + 1, p : p + 1] for p in range(2 * pairs)] for r in range(row_count)
    ]
    labels = jnp.concatenate([cells[p] for cells in tag_cells for p in range(pairs)], axis=0)
    weights = jnp.concatenate([cells[pairs + p] for cells in tag_cells for p in range(pairs)], axis=0)
    half = width // 2
    lane = lax.broadcasted_iota(jnp.int32, (2 * pairs, width), 1)
    row = lax.broadcasted_iota(jnp.int32, (2 * pairs, width), 0)
    mine = (lane >= half) == (row >= pairs)
    query_rows = jnp.where(mine, query_ref[...].reshape(1, width) * half ** (-0.5), 0.0)
    pair_of = lax.rem(lax.broadcasted_iota(jnp.int32, (2 * pairs, seq), 0), pairs).astype(F32)
    members, shares_all, pooled_all = [], [], []
    for r in range(row_count):
        scores = mm_exact(query_rows, stud_ref[r], NT)
        member = own_ref[r : r + 1, head:] == pair_of
        masked = jnp.where(member, scores, NEG)
        terms = jnp.exp(masked - jnp.max(masked, axis=1, keepdims=True))
        shares = terms / jnp.sum(terms, axis=1, keepdims=True)
        pooled = jnp.where(mine, mm_exact(shares, stud_ref[r]), 0.0)
        members.append(member)
        shares_all.append(shares)
        pooled_all.append(pooled[:pairs] + pooled[pairs:])
    pooled = jnp.concatenate(pooled_all, axis=0)
    middle = jnp.tanh(mm_exact(pooled, w2_ref[...]) + bmid)
    logits = mm_exact(middle, w3_ref[...], NT) + b3_ref[...]
    class_of = lax.broadcasted_iota(jnp.int32, logits.shape, 1)
    logits = jnp.where(class_of < classes, logits, NEG)
    terms = jnp.exp(logits - jnp.max(logits, axis=1, keepdims=True))
    chance = terms / jnp.sum(terms, axis=1, keepdims=True)
    grad_logits = weights * (chance - jnp.where(class_of.astype(F32) == labels, 1.0, 0.0))
    gw3_ref[...] = mm_exact(grad_logits, middle, TN)[: gw3_ref.shape[0]]
    grad_pre = mm_exact(grad_logits, w3_ref[...]) * (1.0 - middle * middle)
    gw2_ref[...] = mm_exact(pooled, grad_pre, TN)
    grad_pooled = mm_exact(grad_pre, w2_ref[...], NT)
    grad_query = jnp.zeros((1, width), F32)
    grad_bias = jnp.zeros((1, width), F32)
    for r in range(row_count):
        part = grad_pooled[r * pairs : (r + 1) * pairs]
        grad_parts = jnp.where(mine, jnp.concatenate([part, part], axis=0), 0.0)
        shares = shares_all[r]
        grad_shares = mm_exact(grad_parts, stud_ref[r], NT)
        inner = jnp.sum(shares * grad_shares, axis=1, keepdims=True)
        grad_scores = jnp.where(members[r], shares * (grad_shares - inner), 0.0)
        grad_hidden = mm_exact(
            jnp.concatenate([shares, grad_scores], axis=0),
            jnp.concatenate([grad_parts, query_rows], axis=0),
            TN,
        )
        low = grad_hidden.astype(BF16)
        dstud_ref[r] = low
        grad_bias += column_sum(low.astype(F32))
        found = mm_exact(grad_scores, stud_ref[r]) * half ** (-0.5)
        grad_query += column_sum(jnp.where(mine, found, 0.0))
    gsmall_ref[0:1] = grad_bias
    gsmall_ref[1:2] = column_sum(grad_pre)
    gsmall_ref[2:3] = grad_query
    gsmall_ref[3:4] = column_sum(grad_logits)
    gsmall_ref[4:8] = jnp.zeros((4, width), F32)


def gelu_parts(value):
    size = jnp.abs(value)
    bell = jnp.exp(value * value * -0.5)
    base = 1.0 + (0.3275911 * 0.5 ** 0.5) * size
    t = pl.reciprocal(base, approx=True)
    t = t * (2.0 - base * t)
    terms = ((((1.061405429 * t - 1.453152027) * t + 1.421413741) * t - 0.284496736) * t + 0.254829592) * t
    tail = 0.5 * terms * bell
    return jnp.where(value < 0.0, tail, 1.0 - tail), bell * 0.3989422804014327


COLUMNS = 256


def ffn_kernel(
    classes, pairs, scatter,
    xhat1_ref, rstd1_ref, gain_ref, shift_ref, wb_hbm, wc_home, early_ref, vecs_ref, bdown_ref, cot_hbm, own_ref,
    sw1_ref, sbias_ref, query_ref, w2_in, w3_in, b3_in,
    mixed_ref, gres_ref, dwb_ref, out_ref, hand_ref, pack_ref,
    w2_ref, w3_ref, b3_ref, gbup_ref, gvec_ref, gsw1_ref, act_ref, slope_ref, xhat2_ref, rstd2_ref,
    stud_ref, dstud_ref, low_ref, flip_ref, wc_ref, dwc_ref, wsend, wrecv, msend, mrecv, local_sem, piece_sem, wb_ref, cot_ref, *parts,
):
    row_count, seq, dim = xhat1_ref.shape
    model_size = wb_ref.shape[0]
    inner = wb_ref.shape[2]
    per_row = seq // BLOCK
    blocks = row_count * per_row
    width = sw1_ref.shape[1]
    at = mesh_place()
    gather = Gather(at, model_size, wc_home, wc_ref, wsend, wrecv, early_ref)
    own_pieces = gather.own_pieces(piece_sem)
    own_copy = pltpu.make_async_copy(wc_home, wc_ref.at[at["z"]], local_sem.at[0])
    own_copy.start()
    loads = [
        pltpu.make_async_copy(wb_hbm, wb_ref, local_sem.at[1]),
        pltpu.make_async_copy(cot_hbm, cot_ref, local_sem.at[2]),
    ]
    begin(loads)
    for copy in own_pieces:
        copy.start()
    greet(at, 2 if scatter else 1, model_size)
    for i in (1, 0, 2):
        begin(gather.copies(1, i) + gather.to_twin(0, i))
    if scatter:
        reducer = Reduce(at, model_size, dwc_ref, dwc_ref.at[:, :, at["lo"]], *parts, None, msend, mrecv)

    w2_at, w3_at, small_at, vec_at, bup_at = pack_places(dim, width)
    sb1, bmid = sbias_ref[0:1], sbias_ref[1:2]
    w2_ref[...] = w2_in[...].astype(F32)
    w3_ref[...] = jnp.zeros_like(w3_ref)
    w3_ref[:classes] = w3_in[...].astype(F32)
    b3_ref[...] = jnp.zeros_like(b3_ref)
    b3_ref[:, :classes] = b3_in[...].reshape(1, classes)
    gain_one, gain_two = gain_ref[0:1], gain_ref[1:2]
    shift_one, shift_two = shift_ref[0:1], shift_ref[1:2]

    def live(r):
        cells = [own_ref[i : i + 1, 2 * pairs : 2 * pairs + 1] for i in range(row_count)]
        return sum(jnp.where(r == i, 1.0, 0.0) * cells[i] for i in range(row_count))

    def place(t):
        return t // per_row, pl.ds(pl.multiple_of(t % per_row * BLOCK, BLOCK), BLOCK)

    def prepare(t, _):
        r, part = place(t)
        hidden = xhat1_ref[r, part] * gain_one + shift_one
        low_ref[t] = hidden.astype(BF16)
        xhat2_ref[r, part] = hidden + bdown_ref[...].reshape(1, dim)
        return 0

    lax.fori_loop(0, blocks, prepare, 0)
    for copy in own_pieces:
        copy.wait()
    loads[0].wait()

    def during(m, table):
        for when, actions in table.items():
            @pl.when(m == when)
            def _():
                for action, *args in actions:
                    action(*args)

    def up(m, _):
        during(m, {
            1: [(gather.advance, 2, 1, 0)],
            2: [(gather.advance, 2, 2), (gather.advance, 3, 1)],
            3: [(gather.advance, 3, 0)],
        })

        def one(t, _):
            low = low_ref[t]
            for c in range(0, inner, COLUMNS):
                columns = slice(c, c + COLUMNS)
                pre = mm(low, wb_ref[m, :, columns]) + vecs_ref[m, 1:2, columns]
                cdf, pdf = gelu_parts(pre)
                act_ref[m, t, :, columns] = (pre * cdf).astype(BF16)
                slope_ref[m, t, :, columns] = (cdf + pre * pdf).astype(BF16)
            return 0

        lax.fori_loop(0, blocks, one, 0)
        return 0

    lax.fori_loop(0, model_size, up, 0)
    gather.advance(3, 2)
    own_copy.wait()

    def down(m):
        def one(t, _):
            r, part = place(t)
            xhat2_ref[r, part] = xhat2_ref[r, part] + mm(act_ref[m, t], wc_ref[m])
            return 0

        lax.fori_loop(0, blocks, one, 0)

    down(at["z"])
    for i in (1, 0, 2):
        gather.done(i)
        down(gather.chunks[i])

    def norm_two(t, _):
        r, part = place(t)
        xhat, rstd = norm_parts(xhat2_ref[r, part])
        xhat2_ref[r, part] = xhat
        rstd2_ref[r, part] = rstd
        hidden_two = xhat * gain_two + shift_two
        mixed_ref[r, part] = (hidden_two * live(r)).astype(BF16)
        stud_ref[r, part] = mm(hidden_two.astype(BF16), sw1_ref[...]) + sb1
        return 0

    lax.fori_loop(0, blocks, norm_two, 0)
    student_step(
        stud_ref, own_ref, query_ref, w2_ref, bmid, w3_ref, b3_ref,
        dstud_ref, pack_ref.at[w2_at], pack_ref.at[w3_at], pack_ref.at[small_at], classes, pairs,
    )
    gvec_ref[...] = jnp.zeros_like(gvec_ref)
    gsw1_ref[...] = jnp.zeros_like(gsw1_ref)
    gbup_ref[...] = jnp.zeros_like(gbup_ref)

    loads[1].wait()

    def norm_two_back(t, _):
        r, part = place(t)
        xhat = xhat2_ref[r, part]
        two_low = (xhat * gain_two + shift_two).astype(BF16)
        grad_low = dstud_ref[r, part]
        gsw1_ref[...] += mm(grad_low, two_low, TN)
        upstream = cot_ref[r, part].astype(F32) * live(r) + mm(grad_low, sw1_ref[...], NT)
        gvec_ref[1:2] += column_sum(upstream * xhat)
        gvec_ref[3:4] += column_sum(upstream)
        grad = norm_back(upstream, xhat, rstd2_ref[r, part], gain_two)
        low = grad.astype(BF16)
        gvec_ref[4:5] += column_sum(low.astype(F32))
        gres_ref[r, part] = grad
        low_ref[t] = low
        flip_ref[:, pl.ds(pl.multiple_of(t * BLOCK, BLOCK), BLOCK)] = low.T
        return 0

    lax.fori_loop(0, blocks, norm_two_back, 0)
    half = dim // 2

    def weight_grads(out, right_ref, m):
        def one(y, _):
            part = pl.ds(pl.multiple_of(y * half, 128), half)
            total = mm(flip_ref[part, :], right_ref[m].reshape(blocks * BLOCK, inner)).astype(BF16)
            out[m, y] = total.reshape(out.shape[2:])
            return 0

        lax.fori_loop(0, 2, one, 0)

    def first_grads(i, _):
        weight_grads(dwc_ref, act_ref, chunk_of(at, i))
        if scatter:
            during(i, {n: [(reducer.start, n)] for n in range(model_size)})
        return 0

    lax.fori_loop(0, model_size, first_grads, 0)
    def backward(m, _):
        if scatter:
            during(m, {
                1: [(reducer.after_core, 0)],
                2: [(reducer.after_core, 1), (reducer.after_one, 0)],
                3: [(reducer.after_two, 0), (reducer.after_one, 1), (reducer.after_core, 2)],
            })

        def one(t, _):
            r, part = place(t)
            grad_pre = (mm(low_ref[t], wc_ref[m], NT) * slope_ref[m, t].astype(F32)).astype(BF16)
            slope_ref[m, t] = grad_pre
            gbup_ref[m] += column_sum(grad_pre.astype(F32))
            gres_ref[r, part] = gres_ref[r, part] + mm(grad_pre, wb_ref[m], NT)
            return 0

        lax.fori_loop(0, blocks, one, 0)
        return 0

    lax.fori_loop(0, model_size, backward, 0)

    def norm_one_back(t, _):
        r, part = place(t)
        upstream = gres_ref[r, part]
        xhat = xhat1_ref[r, part]
        gvec_ref[0:1] += column_sum(upstream * xhat)
        gvec_ref[2:3] += column_sum(upstream)
        resid = norm_back(upstream, xhat, rstd1_ref[r, part], gain_one)
        gres_ref[r, part] = resid
        gvec_ref[5:6] += column_sum(resid.astype(BF16).astype(F32))
        flip_ref[:, pl.ds(pl.multiple_of(t * BLOCK, BLOCK), BLOCK)] = (xhat * gain_one + shift_one).astype(BF16).T
        return 0

    lax.fori_loop(0, blocks, norm_one_back, 0)
    def second_grads(m, _):
        if scatter:
            during(m, {
                1: [(reducer.after_two, 1), (reducer.after_one, 2)],
                3: [(reducer.after_core, 3, False), (reducer.after_two, 2, False)],
            })
        weight_grads(dwb_ref, slope_ref, m)
        return 0

    lax.fori_loop(0, model_size, second_grads, 0)
    for m in range(model_size):
        bup = gbup_ref[m]
        for j in range(dim // width):
            pack_ref[bup_at.start + j * 8 + m : bup_at.start + j * 8 + m + 1] = bup[:, j * width : (j + 1) * width]
    for j in range(dim // width):
        columns = slice(j * width, (j + 1) * width)
        pack_ref[columns] = gsw1_ref[:, columns]
        pack_ref[vec_at.start + j * 8 : vec_at.start + j * 8 + 8] = gvec_ref[:, columns]
        if model_size < 8:
            first = bup_at.start + j * 8
            pack_ref[first + model_size : first + 8] = jnp.zeros((8 - model_size, width), F32)
    pack_ref[bup_at.stop :] = jnp.zeros((pack_ref.shape[0] - bup_at.stop, width), F32)
    if scatter:
        reducer.hand_over(out_ref, hand_ref)
        reducer.sent_early()
    else:
        out_ref[...] = dwc_ref[...]
        hand_ref[...] = jnp.zeros_like(hand_ref)
    gather.sent()


def ffn_both(xhat1, rstd1, gain, shift, w_b, w_c, early, vecs, b_down, cot, own, pairs, scatter,
             s_w1, s_bias, s_query, s_w2, s_w3, s_b3):
    rows, seq, dim = xhat1.shape
    model_size = w_b.shape[0]
    inner = w_b.shape[2]
    width = s_w1.shape[1]
    classes = s_w3.shape[1]
    blocks = rows * seq // BLOCK
    piece = dim // 16
    grid_shape = (model_size, 2, 2, PARTS, 2, piece, inner)
    low = lambda *shape: pltpu.VMEM(shape, BF16)
    f32 = lambda *shape: pltpu.VMEM(shape, F32)
    dma = pltpu.SemaphoreType.DMA
    vmem = pl.BlockSpec(memory_space=pltpu.VMEM)
    hbm = pl.BlockSpec(memory_space=pl.ANY)
    return pl.pallas_call(
        functools.partial(ffn_kernel, classes, pairs, scatter),
        in_specs=[vmem] * 4 + [hbm] * 3 + [vmem, vmem, hbm] + [vmem] * 7,
        out_specs=[vmem] * 6,
        out_shape=(
            jax.ShapeDtypeStruct((rows, seq, dim), BF16),
            jax.ShapeDtypeStruct((rows, seq, dim), F32),
            jax.ShapeDtypeStruct(grid_shape, BF16),
            jax.ShapeDtypeStruct(grid_shape[1:2] + grid_shape[3:] if scatter else grid_shape, BF16),
            jax.ShapeDtypeStruct((2, PARTS, piece, inner), BF16),
            jax.ShapeDtypeStruct((pack_rows(dim, width), width), F32),
        ),
        scratch_shapes=[
            f32(width, width),
            f32(width, width),
            f32(1, width),
            f32(model_size, 1, inner),
            f32(8, dim),
            f32(width, dim),
            low(model_size, blocks, BLOCK, inner),
            low(model_size, blocks, BLOCK, inner),
            f32(rows, seq, dim),
            f32(rows, seq, 1),
            f32(rows, seq, width),
            low(rows, seq, width),
            low(blocks, BLOCK, dim),
            low(dim, rows * seq),
            low(model_size, inner, dim),
            low(*grid_shape),
            dma((GATHER_SEMS,)),
            dma((GATHER_SEMS,)),
            dma((REDUCE_SEMS,)),
            dma((REDUCE_SEMS,)),
            dma((3,)),
            dma((6,)),
            low(model_size, dim, inner),
            low(rows, seq, dim),
            *(reduce_scratch(model_size, piece, inner) if scatter else ()),
        ],
        compiler_params=pltpu.CompilerParams(
            vmem_limit_bytes=VMEM_MOST, collective_id=1, has_side_effects=True
        ),
        name="ffn_both",
    )(
        xhat1, rstd1, gain, shift, w_b, w_c, early, vecs, b_down, cot, own,
        s_w1, s_bias, s_query, s_w2, s_w3.T, s_b3,
    )


TILE_Q = 256
TILE_BACK = 64


def backward_group(grad_ctx, ctx_of, load, store, mask, lse_of, group_dim, p_ref, s_ref):
    scale = HEAD_DIM ** (-0.5)
    for j in range(group_dim // HEAD_DIM):
        rows = slice(j * HEAD_DIM, (j + 1) * HEAD_DIM)
        k_rows = slice(group_dim + rows.start, group_dim + rows.stop)
        v_rows = slice(2 * group_dim + rows.start, 2 * group_dim + rows.stop)
        q_t = load(rows) * scale
        k_t = load(k_rows)
        v_t = load(v_rows)
        d_t = grad_ctx[rows]
        seq = q_t.shape[1]
        inner = column_sum(d_t.astype(F32) * ctx_of(rows).astype(F32))
        lse = lse_of(j)
        k_n, v_n = k_t.T, v_t.T
        probs_ref, grads_ref = p_ref.at[j % 2], s_ref.at[j % 2]
        for q0 in range(0, seq, TILE_Q):
            columns = slice(q0, q0 + TILE_Q)
            q, d = q_t[:, columns], d_t[:, columns]
            for k0 in range(0, seq, TILE_BACK):
                part = slice(k0, k0 + TILE_BACK)
                probs = jnp.exp(mm(k_n[part], q) + mask[part, columns] - lse[:, columns])
                grad_probs = mm(v_n[part], d)
                probs_ref[part, columns] = probs.astype(BF16)
                grads_ref[part, columns] = (probs * (grad_probs - inner[:, columns])).astype(BF16)
        store(rows, mm(k_t * scale, grads_ref[...]).astype(BF16))
        store(k_rows, mm(q_t, grads_ref[...], NT).astype(BF16))
        store(v_rows, mm(d_t, probs_ref[...], NT).astype(BF16))


def attn_backward_kernel(
    x_ref, gres_ref, wa_ref, qkv_ref, ctx_ref, lse_ref, own_ref, dx_ref, dwa_ref, bias_ref,
    mask_ref, acc_ref, work_ref, xflip_ref, gflip_ref, p_ref, s_ref,
):
    row_count, seq, dim = x_ref.shape
    model_size = wa_ref.shape[0]
    group_dim = ctx_ref.shape[2]
    bias_ref[...] = jnp.zeros_like(bias_ref)
    seg_rows = own_ref[:, own_ref.shape[1] - seq :]
    seg_cols = seg_rows.T
    for r in range(row_count):
        mask_ref[...] = jnp.where(seg_cols[:, r : r + 1] == seg_rows[r : r + 1], 0.0, NEG)
        acc_ref[...] = gres_ref[r]
        grad_low = gres_ref[r].astype(BF16)
        columns = slice(r * seq, (r + 1) * seq)
        gflip_ref[:, columns] = grad_low.T
        xflip_ref[:, columns] = x_ref[r].T

        def one_group(m, _):
            grad_ctx = mm(wa_ref[m, 3 * group_dim :, :], grad_low, NT).astype(BF16)

            def store(rows, value):
                work_ref[r, m, rows, :] = value

            backward_group(
                grad_ctx, lambda rows: ctx_ref[r, m, rows, :], lambda rows: qkv_ref[r, m, rows, :], store,
                mask_ref, lambda j: lse_ref[r, m, j : j + 1, :], group_dim, p_ref, s_ref,
            )
            grads = work_ref[r, m]
            bias_ref[m] += mm(jnp.ones((8, seq), BF16), grads, NT)
            acc_ref[...] += mm(grads, wa_ref[m, : 3 * group_dim, :], TN)
            return 0

        lax.fori_loop(0, model_size, one_group, 0)
        dx_ref[r] = acc_ref[...].astype(BF16)

    def weight_grads(i, _):
        m, part = i // 2, pl.ds(pl.multiple_of(i % 2 * (dim // 2), 128), dim // 2)
        left, right = 0.0, 0.0
        for r in range(row_count):
            columns = slice(r * seq, (r + 1) * seq)
            left += mm(xflip_ref[part, columns], work_ref[r, m], NT)
            right += mm(gflip_ref[part, columns], ctx_ref[r, m], NT)
        dwa_ref[m, part, : 3 * group_dim] = left.astype(BF16)
        dwa_ref[m, part, 3 * group_dim :] = right.astype(BF16)
        return 0

    lax.fori_loop(0, 2 * model_size, weight_grads, 0)


def attn_backward(x, gres, w_a, qkv, ctx, lse, own):
    rows, seq, dim = x.shape
    model_size = w_a.shape[0]
    group_dim = dim // model_size
    return pl.pallas_call(
        attn_backward_kernel,
        out_shape=(
            jax.ShapeDtypeStruct((rows, seq, dim), BF16),
            jax.ShapeDtypeStruct((model_size, dim, 4 * group_dim), BF16),
            jax.ShapeDtypeStruct((model_size, 8, 3 * group_dim), F32),
        ),
        scratch_shapes=[
            pltpu.VMEM((seq, seq), F32),
            pltpu.VMEM((seq, dim), F32),
            pltpu.VMEM((rows, model_size, 3 * group_dim, seq), BF16),
            pltpu.VMEM((dim, rows * seq), BF16),
            pltpu.VMEM((dim, rows * seq), BF16),
            pltpu.VMEM((2, seq, seq), BF16),
            pltpu.VMEM((2, seq, seq), BF16),
        ],
        compiler_params=pltpu.CompilerParams(vmem_limit_bytes=VMEM_MOST),
        name="attn_backward",
    )(x, gres, w_a, qkv, ctx, lse, own)
def slot_of_rows(exit_ref, target_ref, depth):
    count = exit_ref.shape[0]
    flat = []
    for i in range(count):
        rank = 0
        for h in range(i):
            rank = rank + jnp.where(target_ref[h] == target_ref[i], 1 - exit_ref[h], 0)
        flat.append(jnp.where(exit_ref[i] == 0, target_ref[i] * depth + rank, -1))
    return flat


def pick_of_slots(tag_ref, depth, flag_at, capacity):
    seen = jnp.zeros((1, 1), F32)
    picks = []
    for k in range(tag_ref.shape[0] * depth):
        live = tag_ref[k // depth, k % depth : k % depth + 1, flag_at : flag_at + 1]
        picks.append([jnp.where(seen == float(c), live, 0.0) for c in range(min(capacity, k + 1))])
        seen = seen + live
    return picks


def slots_of_tags(tag_ref, depth, flag_at, capacity):
    seen, slots = 0, []
    for k in range(tag_ref.shape[0] * depth):
        cell = tag_ref[k // depth, k % depth : k % depth + 1, flag_at : flag_at + 1]
        live = jnp.where(jnp.sum(cell) > 0.5, 1, 0)
        slots.append((jnp.minimum(seen, capacity - 1), live))
        seen = seen + live
    return slots


TOKENS = 32
CUTS = 3


def enter_kernel(
    depth, pairs,
    exit_ref, target_ref, rows_ref, seg_ref, lab_ref, wt_ref, wqkv_ref, wout_ref, bqv_ref, bup_ref, bout_ref,
    wb_loc, wc_loc,
    own_ref, got_tags_ref, vecs_ref, x_out, wa_out, wb_ref, early_ref,
    qkv_ref, ctx_ref, lse_ref, xhat_ref, rstd_ref,
    tags_ref, vec_ref, wa_loc, slot_ref, part_ref, x_ref, wa_ref, tag_ref, taggot_ref, taglocal_ref, vecgot_ref,
    mask_ref, acc_ref, wsend, wrecv, rsend, rrecv, local_sem, *got_refs,
):
    row_count, token_part, dim = rows_ref.shape
    own_rows, seq = x_ref.shape[:2]
    model_size = wa_ref.shape[0]
    batch_size = taggot_ref.shape[0]
    capacity = own_rows * model_size
    group_dim = wout_ref.shape[0]
    flag_at = 2 * pairs
    head = tag_ref.shape[2] - seq
    at = mesh_place()
    b, z = at["b"], at["z"]
    gathers = [
        Gather(at, model_size, home, spot, wsend.at[k], wrecv.at[k])
        for k, (home, spot) in enumerate(((wa_loc, wa_ref), (wb_loc, wb_ref)))
    ]
    first_gather, second_gather = gathers
    third_gather = Gather(at, model_size, wc_loc, None, wsend.at[2], wrecv.at[2], early_ref)
    vec_first = (CUTS + 1) * batch_size + CUTS * model_size

    def vec_copies():
        return [
            remote(vec_ref, vecgot_ref.at[z], rsend.at[vec_first + i], rrecv.at[vec_first + i],
                   {"mp": (z + i) % model_size})
            for i in range(1, model_size)
        ]

    wide = dim // CUTS

    def batch_copies(cut):
        columns = pl.ds(cut * wide, wide)
        copies = []
        for j in range(1, batch_size):
            t = (b + j) % batch_size
            n = cut * batch_size + j
            copies.append(remote(slot_ref.at[pl.ds(t * depth, depth), :, columns],
                                 got_refs[cut].at[pl.ds(b * depth, depth)],
                                 rsend.at[n], rrecv.at[n], {"batch": t}))
            if cut == 0:
                n = CUTS * batch_size + j
                copies.append(remote(tag_ref.at[t], taggot_ref.at[b], rsend.at[n], rrecv.at[n], {"batch": t}))
        return copies

    mine = pl.ds(pl.multiple_of(z * token_part, 128), token_part)

    def row_copies(cut, r):
        columns = pl.ds(cut * wide, wide)
        first = (CUTS + 1) * (batch_size + model_size) + (cut * own_rows + r) * model_size
        return [
            remote(part_ref.at[(z + i) % model_size * own_rows + r, :, columns], x_ref.at[r, mine, columns],
                   rsend.at[first + i], rrecv.at[first + i], {"mp": (z + i) % model_size})
            for i in range(1, model_size)
        ]

    def local_copies():
        return [
            pltpu.make_async_copy(gather.home, gather.spot.at[z], local_sem.at[k])
            for k, gather in enumerate(gathers)
        ]

    for j in range(3):
        wa_loc[j * group_dim : (j + 1) * group_dim, :] = wqkv_ref[j]
    wa_loc[3 * group_dim :, :] = wout_ref[...]
    vec_ref[...] = jnp.zeros_like(vec_ref)
    vec_ref[0:1, :group_dim] = bqv_ref[0:1]
    vec_ref[0:1, 2 * group_dim : 3 * group_dim] = bqv_ref[1:2]
    vec_ref[1:2] = bup_ref[...].reshape(1, dim)
    greet(at, batch_size, model_size)
    first_gather.start()
    begin(vec_copies())
    begin(local_copies())

    flat = slot_of_rows(exit_ref, target_ref, depth)
    tags_ref[...] = jnp.zeros_like(tags_ref)
    taglocal_ref[0] = jnp.zeros_like(taglocal_ref[0])
    taglocal_ref[0, :pairs, :row_count] = lab_ref[...].astype(F32)
    taglocal_ref[0, pairs : 2 * pairs, :row_count] = wt_ref[...].astype(F32)
    tags_ref[:, : 2 * pairs] = taglocal_ref[0, : 2 * pairs, :128].T[: tags_ref.shape[0]]
    tags_ref[:row_count, flag_at : flag_at + 1] = jnp.ones((row_count, 1), F32)
    tags_ref[:row_count, head:] = seg_ref[...].astype(F32)
    tag_ref[...] = jnp.zeros_like(tag_ref)

    def taken(k):
        hits = [jnp.where(flat[r] == k, 1, 0) for r in range(row_count)]
        return sum(r * hits[r] for r in range(row_count)), sum(hits).astype(F32)

    def fill(t, dst_ref, cut):
        columns = pl.ds(cut * wide, wide)
        for s in range(depth):
            row, there = taken(t * depth + s)
            found = (rows_ref[row, :, columns].astype(F32) * there).astype(BF16)
            if dst_ref is None:
                got_refs[cut][t * depth + s] = found
            else:
                dst_ref[t * depth + s, :, columns] = found

    def fill_tags(t):
        for s in range(depth):
            total = jnp.zeros((1, tags_ref.shape[1]), F32)
            for r in range(row_count):
                total += jnp.where(flat[r] == t * depth + s, 1.0, 0.0) * tags_ref[r : r + 1]
            tag_ref[t, s : s + 1] = total

    for j in range(1, batch_size):
        fill_tags((b + j) % batch_size)
    for cut in range(CUTS):
        for j in range(1, batch_size):
            fill((b + j) % batch_size, slot_ref, cut)
        if cut == 0:
            begin(batch_copies(0))
            fill_tags(b)
            taggot_ref[b] = tag_ref[b]
            fill(b, None, 0)
    for cut in range(1, CUTS):
        fill(b, None, cut)
    arrive(batch_copies(0))
    begin(batch_copies(1))

    picks = pick_of_slots(taggot_ref, depth, flag_at, capacity)

    slots = slots_of_tags(taggot_ref, depth, flag_at, capacity)

    def compact(cut):
        columns = pl.ds(cut * wide, wide)
        for c in range(capacity):
            hits = [jnp.where(place == c, live, 0) for place, live in slots]
            k = sum(n * hits[n] for n in range(c, len(slots)))
            there = sum(hits[c:]).astype(F32)
            part_ref[c, :, columns] = (got_refs[cut][k].astype(F32) * there).astype(BF16)
        begin(row_copies(cut, 0))

    compact(0)
    first_gather.advance(1, 1, 0)
    arrive(batch_copies(1))
    for cut in range(2, CUTS):
        begin(batch_copies(cut))
        compact(cut - 1)
        if cut == 2:
            first_gather.advance(1, 2)
        arrive(batch_copies(cut))
    compact(CUTS - 1)
    first_gather.advance(2, 1, 0, 2)
    second_gather.start()
    for r in range(1, own_rows):
        for cut in range(CUTS):
            begin(row_copies(cut, r))
    for c in range(capacity):
        total = jnp.zeros((1, tags_ref.shape[1]), F32)
        for k in range(c, len(picks)):
            total += picks[k][c] * taggot_ref[k // depth, k % depth : k % depth + 1]
        taglocal_ref[c, 0:1] = total
    for i in range(own_rows):
        x_ref[i, mine] = part_ref[z * own_rows + i]
    own_ref[...] = jnp.zeros_like(own_ref)
    for i in range(own_rows):
        own_ref[i : i + 1] = taglocal_ref[z * own_rows + i, 0:1]
    got_tags_ref[...] = taggot_ref[...]

    first_gather.advance(3, 1, 0, 2)
    arrive(vec_copies())
    vecgot_ref[z] = vec_ref[...]
    vecs_ref[...] = vecgot_ref[...]
    for copy in local_copies():
        copy.wait()
    keep = [
        pltpu.make_async_copy(x_ref, x_out, local_sem.at[3]),
        pltpu.make_async_copy(wa_ref, wa_out, local_sem.at[4]),
    ]

    def rows_here(r):
        for cut in range(CUTS):
            arrive(row_copies(cut, r))

    rows_here(0)
    seg_rows = own_ref[:, head:]
    seg_cols = seg_rows.T
    def forward_early():
        arrive(third_gather.early_copies(0))
        begin(third_gather.early_copies(1))

    late = {
        (0, 1): ((first_gather.done, 1),),
        (0, 2): ((first_gather.done, 0), (second_gather.advance, 1, 1, 0)),
        (0, 3): ((first_gather.done, 2), (second_gather.advance, 1, 2)),
        (1, 0): ((second_gather.advance, 2, 2),),
        (1, 1): ((second_gather.advance, 3, 1, 0),),
        (1, 2): ((second_gather.advance, 3, 2), (forward_early,)),
    }

    for r in range(own_rows):
        if r == 1:
            second_gather.advance(2, 1, 0)
            begin(third_gather.early_copies(0))
            for n in range(1, own_rows):
                rows_here(n)
            begin(keep)
        mask_ref[...] = jnp.where(seg_cols[:, r : r + 1] == seg_rows[r : r + 1], 0.0, NEG)
        acc_ref[...] = jnp.zeros_like(acc_ref)

        def one_group(i, _):
            m = chunk_of(at, model_size - 1 - i)
            for step in range(model_size):
                if (r, step) in late:
                    @pl.when(i == step)
                    def _():
                        for action, *args in late[r, step]:
                            action(*args)

            bias = vecgot_ref[m].T[: 3 * group_dim, 0:1]
            low = (mm(wa_ref[m, : 3 * group_dim, :], x_ref[r], NT) + bias).astype(BF16)
            qkv_ref[r, m] = low
            for j in range(group_dim // HEAD_DIM):
                rows = slice(j * HEAD_DIM, (j + 1) * HEAD_DIM)
                q_t = low[rows] * HEAD_DIM ** (-0.5)
                k_t = low[group_dim + rows.start : group_dim + rows.stop]
                v_t = low[2 * group_dim + rows.start : 2 * group_dim + rows.stop]
                scores = mm(k_t, q_t, TN) + mask_ref[...]
                top = jnp.max(scores, axis=0, keepdims=True)
                terms = jnp.exp(scores - top)
                total = jnp.sum(terms, axis=0, keepdims=True)
                ctx_t = mm(v_t, terms.astype(BF16)) / total
                ctx_ref[r, m, rows, :] = ctx_t.astype(BF16)
                lse_ref[r, m, j : j + 1, :] = top + jnp.log(total)
            acc_ref[...] += mm(ctx_ref[r, m], wa_ref[m, 3 * group_dim :, :], TN)
            return 0

        lax.fori_loop(0, model_size, one_group, 0)
        xhat, rstd = norm_parts(x_ref[r].astype(F32) + (acc_ref[...] + bout_ref[...].reshape(1, dim)))
        xhat_ref[r] = xhat
        rstd_ref[r] = rstd

    second_gather.done(0, 1, 2)
    arrive(third_gather.early_copies(1))
    for copy in keep:
        copy.wait()
    for gather in gathers:
        gather.sent()
    sent(third_gather.early_copies(0) + third_gather.early_copies(1))
    sent(vec_copies())
    for cut in range(CUTS):
        sent(batch_copies(cut))
        for r in range(own_rows):
            sent(row_copies(cut, r))


def enter(exit_flag, target, rows_in, seg, labels, weights, w_qkv, w_out, b_qv, b_up, b_out, w_b, w_c,
          own_rows, batch_size, model_size):
    row_count, token_part, dim = rows_in.shape
    seq = token_part * model_size
    capacity = own_rows * model_size
    depth = (capacity + batch_size - 1) // batch_size
    group_dim = dim // model_size
    pairs = labels.shape[1]
    tag_wide = 128 + seq
    smem = pl.BlockSpec(memory_space=pltpu.SMEM)
    vmem = pl.BlockSpec(memory_space=pltpu.VMEM)
    hbm = pl.BlockSpec(memory_space=pl.ANY)
    full = jax.ShapeDtypeStruct((model_size, dim, dim), BF16)
    f32 = lambda *shape: jax.ShapeDtypeStruct(shape, F32)
    low = lambda *shape: jax.ShapeDtypeStruct(shape, BF16)
    moves = (CUTS + 1) * (batch_size + model_size) + CUTS * own_rows * model_size
    return pl.pallas_call(
        functools.partial(enter_kernel, depth, pairs),
        in_specs=[smem, smem] + [vmem] * 9 + [hbm, hbm],
        out_specs=[vmem, vmem, vmem, hbm, hbm, hbm, hbm] + [vmem] * 5,
        out_shape=(
            f32(8, tag_wide),
            f32(batch_size, 8, tag_wide),
            f32(model_size, 8, dim),
            low(own_rows, seq, dim),
            full,
            full,
            low(3, 2, dim // 16, dim),
            low(own_rows, model_size, 3 * group_dim, seq),
            low(own_rows, model_size, group_dim, seq),
            f32(own_rows, model_size, group_dim // HEAD_DIM, seq),
            f32(own_rows, seq, dim),
            f32(own_rows, seq, 1),
        ),
        scratch_shapes=[
            pltpu.VMEM((-(-row_count // 8) * 8, tag_wide), F32),
            pltpu.VMEM((8, dim), F32),
            pltpu.VMEM((dim, dim), BF16),
            pltpu.VMEM((batch_size * depth, token_part, dim), BF16),
            pltpu.VMEM((capacity, token_part, dim), BF16),
            pltpu.VMEM((own_rows, seq, dim), BF16),
            pltpu.VMEM((model_size, dim, dim), BF16),
            pltpu.VMEM((batch_size, 8, tag_wide), F32),
            pltpu.VMEM((batch_size, 8, tag_wide), F32),
            pltpu.VMEM((capacity, 8, tag_wide), F32),
            pltpu.VMEM((model_size, 8, dim), F32),
            pltpu.VMEM((seq, seq), F32),
            pltpu.VMEM((seq, dim), F32),
            pltpu.SemaphoreType.DMA((3, GATHER_SEMS)),
            pltpu.SemaphoreType.DMA((3, GATHER_SEMS)),
            pltpu.SemaphoreType.DMA((moves,)),
            pltpu.SemaphoreType.DMA((moves,)),
            pltpu.SemaphoreType.DMA((5,)),
            *[pltpu.VMEM((batch_size * depth, token_part, dim // CUTS), BF16) for _ in range(CUTS)],
        ],
        compiler_params=pltpu.CompilerParams(
            vmem_limit_bytes=VMEM_MOST, collective_id=0, has_side_effects=True
        ),
        name="enter",
    )(
        exit_flag, target, rows_in, seg, labels.T, weights.T, jnp.transpose(w_qkv, (0, 2, 1)), w_out, b_qv, b_up, b_out,
        w_b, w_c,
    )


def leave_kernel(
    depth, pairs,
    exit_ref, target_ref, tags_ref, own_ref, x_hbm, gres_hbm, wa_hbm, qkv_hbm, ctx_hbm, lse_ref,
    dwb_hbm, ownc_ref, hand_ref, pack_ref,
    rows_ref, mats_ref, sums_ref, bias_ref,
    x_ref, wa_ref, ctx_ref, work_ref, acc_ref, mask_ref, p_ref, s_ref, xflip_ref, gflip_ref, dx_ref, dwa_ref,
    own_half, *rest,
):
    parts_a, parts_b, parts_c, rest = rest[:7], rest[7:14], rest[14:19], rest[19:]
    (
        small_acc, small_got, small_z, bias_acc, bias_got, bias_z, back_ref, back_got,
        msend, mrecv, ssend, srecv, bsend, brecv, rsend, rrecv, local_sem, *mine_refs,
    ) = rest
    row_count, seq, dim = x_ref.shape
    model_size = wa_ref.shape[0]
    batch_size = tags_ref.shape[0]
    group_dim = ctx_ref.shape[2]
    token_part = seq // model_size
    capacity = row_count * model_size
    others = model_size - 1
    at = mesh_place()
    b, z, lo, hi = at["b"], at["z"], at["lo"], at["hi"]
    far, twin, side = at["far"], at["twin"], at["side"]

    def shard(i):
        return {"mp": (z + i) % model_size}

    first = Reduce(at, model_size, dwb_hbm, own_half, *parts_b, mats_ref.at[1], msend.at[1], mrecv.at[1])
    second = Reduce(at, model_size, dwa_ref, dwa_ref.at[:, :, lo], *parts_a, mats_ref.at[0], msend.at[0], mrecv.at[0], 2, True)
    third = Finish(at, model_size, ownc_ref, hand_ref, *parts_c, mats_ref.at[2], msend.at[2], mrecv.at[2])

    def small_copies(stage):
        def one(slot, src, dst, device):
            return remote(src, dst, ssend.at[slot], srecv.at[slot], device)

        if stage == 0:
            return [one(0, pack_ref.at[1 - lo], small_got.at[0], twin)]
        if stage < 3:
            return [one(stage, small_acc.at[stage - 1], small_got.at[stage], (far, side)[stage - 1])]
        if stage == 3:
            return [
                one(2 + i, small_acc.at[2, (z + i) % model_size], small_z.at[i - 1], shard(i))
                for i in range(1, model_size)
            ]
        if stage == 4:
            return [
                one(2 + others + i, sums_ref.at[lo, z], sums_ref.at[lo, z], shard(i))
                for i in range(1, model_size)
            ]
        return [one(3 + 2 * others, sums_ref.at[lo], sums_ref.at[lo], twin)]

    def bias_copies(stage):
        def one(slot, src, dst, device):
            return remote(src, dst, bsend.at[slot], brecv.at[slot], device)

        if stage < 3:
            return [one(stage, bias_acc.at[stage], bias_got.at[stage], (twin, far, side)[stage])]
        return [
            one(2 + i, bias_acc.at[3, (z + i) % model_size], bias_z.at[i - 1], shard(i))
            for i in range(1, model_size)
        ]

    wide = dim // CUTS

    def row_copies(r, cut):
        columns = pl.ds(cut * wide, wide)
        first = (r * CUTS + cut) * others - 1
        return [
            remote(
                dx_ref.at[r, pl.ds(pl.multiple_of((z + i) % model_size * token_part, 128), token_part), columns],
                mine_refs[cut].at[z * row_count + r],
                rsend.at[first + i], rrecv.at[first + i], shard(i),
            )
            for i in range(1, model_size)
        ]

    def batch_copies(cut):
        columns = pl.ds(cut * wide, wide)
        first = row_count * CUTS * others + cut * (batch_size - 1) - 1
        copies = []
        for j in range(1, batch_size):
            t = (b + j) % batch_size
            copies.append(remote(
                back_ref.at[pl.ds(t * depth, depth), :, columns],
                back_got.at[pl.ds(b * depth, depth), :, columns],
                rsend.at[first + j], rrecv.at[first + j], {"batch": t},
            ))
        return copies

    def local_copies():
        return [
            pltpu.make_async_copy(dwb_hbm.at[:, :, lo], own_half, local_sem.at[0]),
        ]

    def inputs():
        return [
            pltpu.make_async_copy(qkv_hbm, work_ref, local_sem.at[2]),
            pltpu.make_async_copy(gres_hbm, acc_ref, local_sem.at[3]),
            pltpu.make_async_copy(x_hbm, x_ref, local_sem.at[4]),
            pltpu.make_async_copy(wa_hbm, wa_ref, local_sem.at[5]),
            pltpu.make_async_copy(ctx_hbm, ctx_ref, local_sem.at[6]),
        ]

    def small_step(stage):
        arrive(small_copies(stage))
        if stage == 0:
            small_acc[0] = pack_ref[lo] + small_got[0]
        if stage in (1, 2):
            small_acc[stage] = small_acc[stage - 1] + small_got[stage]
        if stage == 3:
            total = small_acc[2, z]
            for i in range(others):
                total += small_z[i]
            sums_ref[lo, z] = total
        if stage < 5:
            begin(small_copies(stage + 1))

    def bias_step(stage):
        arrive(bias_copies(stage))
        if stage < 3:
            bias_acc[stage + 1] = bias_acc[stage] + bias_got[stage]
            begin(bias_copies(stage + 1))
        else:
            total = bias_acc[3, z]
            for i in range(others):
                total += bias_z[i]
            bias_ref[...] = total

    begin(inputs())
    begin(local_copies())
    greet(at, batch_size, model_size)
    begin(small_copies(0))
    third.start()
    for i in range(model_size):
        first.start(i)
    seg_rows = own_ref[:, own_ref.shape[1] - seq :]
    seg_cols = seg_rows.T
    for copy in inputs() + local_copies():
        copy.wait()

    steps = {
        0: [],
        1: [(small_step, 0), (third.after_one,)],
        2: [],
        3: [(first.after_core, 0), (small_step, 1), (third.after_two,)],
        4: [(first.after_core, 1), (small_step, 2)],
        5: [(first.after_one, 0), (small_step, 3), (third.after_three,)],
        6: [(first.after_core, 2), (first.after_one, 1), (first.after_two, 0), (small_step, 4)],
        7: [(first.after_core, 3), (first.after_one, 2), (first.after_two, 1), (second.after_core, 0)],
    }

    def weight_grads(i):
        m, rows_y = chunk_of(at, i), dim // 2

        def one(y, _):
            part = pl.ds(pl.multiple_of(y * rows_y, 128), rows_y)
            left, right = 0.0, 0.0
            for q in range(row_count):
                cols = slice(q * seq, (q + 1) * seq)
                left += mm(xflip_ref[part, cols], work_ref[q, m], NT)
                right += mm(gflip_ref[part, cols], ctx_ref[q, m], NT)
            shape = dwa_ref.shape[2:-1]
            dwa_ref[m, y, :, :, :, :, : 3 * group_dim] = left.astype(BF16).reshape(*shape, 3 * group_dim)
            dwa_ref[m, y, :, :, :, :, 3 * group_dim :] = right.astype(BF16).reshape(*shape, group_dim)
            return 0

        lax.fori_loop(0, 2, one, 0)

    for r in range(row_count):
        mask_ref[...] = jnp.where(seg_cols[:, r : r + 1] == seg_rows[r : r + 1], 0.0, NEG)
        grad_low = acc_ref[r].astype(BF16)
        columns = slice(r * seq, (r + 1) * seq)
        gflip_ref[:, columns] = grad_low.T
        xflip_ref[:, columns] = x_ref[r].T

        def one_group(i, _):
            if r == row_count - 1:
                @pl.when(i > 0)
                def _():
                    weight_grads(i - 1)

            for step in range(model_size):
                @pl.when(i == step)
                def _():
                    if r == row_count - 1 and step > 0:
                        second.start(step - 1)
                    for action, *args in steps[r * model_size + step]:
                        action(*args)

            m = chunk_of(at, i)
            grad_ctx = mm(wa_ref[m, 3 * group_dim :, :], grad_low, NT).astype(BF16)

            def store(rows, value):
                work_ref[r, m, rows, :] = value

            backward_group(
                grad_ctx, lambda rows: ctx_ref[r, m, rows, :], lambda rows: work_ref[r, m, rows, :], store,
                mask_ref, lambda j: lse_ref[r, m, j : j + 1, :], group_dim, p_ref, s_ref,
            )
            grads = work_ref[r, m]
            found = mm(jnp.ones((8, seq), BF16), grads, NT)
            if r == 0:
                bias_acc[0, m] = found
            else:
                bias_acc[0, m] = bias_acc[0, m] + found
            acc_ref[r] = acc_ref[r] + mm(grads, wa_ref[m, : 3 * group_dim, :], TN)
            return 0

        lax.fori_loop(0, model_size, one_group, 0)
        dx_ref[r] = acc_ref[r].astype(BF16)
        for cut in range(CUTS if r < row_count - 1 else 2):
            begin(row_copies(r, cut))

    weight_grads(model_size - 1)
    second.start(model_size - 1)
    for r in range(row_count):
        for cut in range(CUTS):
            part = pl.ds(pl.multiple_of(z * token_part, 128), token_part)
            mine_refs[cut][z * row_count + r] = dx_ref[r, part, cut * wide : (cut + 1) * wide]
    first.after_one(3)
    second.after_core(1)
    slots = slots_of_tags(tags_ref, depth, 2 * pairs, capacity)

    def give(cut):
        columns = pl.ds(cut * wide, wide)
        for k, (place, live) in enumerate(slots):
            found = mine_refs[cut][place].astype(F32) * live.astype(F32)
            back_ref[k, :, columns] = found.astype(BF16)
        begin(batch_copies(cut))

    def returned(cut):
        for r in range(row_count):
            arrive(row_copies(r, cut))
        if cut + 2 < CUTS:
            begin(row_copies(row_count - 1, cut + 2))
        give(cut)

    returned(0)
    first.after_two(2)
    second.after_one(0)
    second.after_core(2)
    returned(1)
    begin(bias_copies(0))
    first.after_two(3)
    second.after_core(3)
    second.after_one(1)
    returned(2)
    second.after_two(0)
    own_slots = pl.ds(b * depth, depth)
    back_got[own_slots] = back_ref[own_slots]
    second.after_two(1)
    second.after_one(2)
    bias_step(0)
    first.after_three()
    second.after_two(2)
    second.after_one(3)
    bias_step(1)
    small_step(5)
    first.after_four()
    third.done()
    second.after_two(3)
    bias_step(2)
    second.after_three()
    bias_step(3)
    flat = slot_of_rows(exit_ref, target_ref, depth)
    for cut in range(CUTS):
        arrive(batch_copies(cut))

    for r in range(rows_ref.shape[0]):
        k = jnp.minimum(jnp.maximum(flat[r], 0), batch_size * depth - 1)
        alive = jnp.where(flat[r] >= 0, 1.0, 0.0)
        rows_ref[r] = (back_got[k].astype(F32) * alive).astype(BF16)
    for reducer in (first, second):
        reducer.done()
        reducer.sent()
    third.sent()
    for stage in range(6):
        sent(small_copies(stage))
    for stage in range(4):
        sent(bias_copies(stage))
    for cut in range(CUTS):
        for r in range(row_count):
            sent(row_copies(r, cut))
        sent(batch_copies(cut))


def leave(exit_flag, target, tags, own, x, gres, w_a, qkv, ctx, lse, d_wb, mat_c, hand, pack, row_total, batch_size, pairs):
    rows, seq, dim = x.shape
    model_size = w_a.shape[0]
    group_dim = dim // model_size
    token_part = seq // model_size
    capacity = rows * model_size
    depth = (capacity + batch_size - 1) // batch_size
    slots = batch_size * depth
    piece = dim // 16
    others = model_size - 1
    grid_shape = (model_size, 2, 2, PARTS, 2, piece, dim)
    pack_shape = (2, model_size, pack.shape[0] // (2 * model_size), pack.shape[1])
    smem = pl.BlockSpec(memory_space=pltpu.SMEM)
    vmem = pl.BlockSpec(memory_space=pltpu.VMEM)
    hbm = pl.BlockSpec(memory_space=pl.ANY)
    dma = pltpu.SemaphoreType.DMA
    low = lambda *shape: pltpu.VMEM(shape, BF16)
    f32 = lambda *shape: pltpu.VMEM(shape, F32)
    row_moves = CUTS * (rows * others + batch_size - 1)
    return pl.pallas_call(
        functools.partial(leave_kernel, depth, pairs),
        in_specs=[smem, smem, vmem, vmem, hbm, hbm, hbm, hbm, hbm, vmem, hbm, vmem, vmem, vmem],
        out_specs=[vmem, vmem, vmem, vmem],
        out_shape=(
            jax.ShapeDtypeStruct((row_total, token_part, dim), BF16),
            jax.ShapeDtypeStruct((3,) + grid_shape[2:], BF16),
            jax.ShapeDtypeStruct(pack_shape, F32),
            jax.ShapeDtypeStruct((8, 3 * group_dim), F32),
        ),
        scratch_shapes=[
            low(rows, seq, dim),
            low(model_size, dim, dim),
            low(rows, model_size, group_dim, seq),
            low(rows, model_size, 3 * group_dim, seq),
            f32(rows, seq, dim),
            f32(seq, seq),
            low(2, seq, seq),
            low(2, seq, seq),
            low(dim, rows * seq),
            low(dim, rows * seq),
            low(rows, seq, dim),
            low(*grid_shape),
            low(model_size, 2, PARTS, 2, piece, dim),
            *reduce_scratch(model_size, piece, dim),
            *reduce_scratch(model_size, piece, dim),
            low(2, piece, dim),
            low(2, piece, dim),
            low(piece, dim),
            low(piece, dim),
            low(PARTS, piece, dim),
            f32(3, *pack_shape[1:]),
            f32(3, *pack_shape[1:]),
            f32(others, *pack_shape[2:]),
            f32(4, model_size, 8, 3 * group_dim),
            f32(3, model_size, 8, 3 * group_dim),
            f32(others, 8, 3 * group_dim),
            low(slots, token_part, dim),
            low(slots, token_part, dim),
            dma((3, REDUCE_SEMS)),
            dma((3, REDUCE_SEMS)),
            dma((4 + 2 * others,)),
            dma((4 + 2 * others,)),
            dma((3 + others,)),
            dma((3 + others,)),
            dma((row_moves,)),
            dma((row_moves,)),
            dma((7,)),
            *[low(capacity, token_part, dim // CUTS) for _ in range(CUTS)],
        ],
        compiler_params=pltpu.CompilerParams(
            vmem_limit_bytes=VMEM_MOST, collective_id=2, has_side_effects=True
        ),
        name="leave",
    )(
        exit_flag, target, tags, own, x, gres, w_a, qkv, ctx, lse,
        d_wb.reshape(grid_shape), mat_c, hand, pack.reshape(pack_shape),
    )


def finish_kernel(
    classes, mats_ref, sums_ref, bias_ref,
    gqkv_ref, gbqv_ref, gout_ref, gbout_ref, ggain_ref, gshift_ref, gup_ref, gbup_ref, gdown_ref, gbdown_ref,
    gsw1_ref, gsbias_ref, gquery_ref, gsw2_ref, gsw3_ref, gsb3_ref,
):
    dim, width = gsw1_ref.shape
    group_dim = gout_ref.shape[0]
    b, z = lax.axis_index("batch"), lax.axis_index("mp")
    w2_at, w3_at, small_at, vec_at, bup_at = pack_places(dim, width)
    blocks = dim // width

    def vector(first, row):
        return jnp.concatenate([sums_ref[first + j * 8 + row : first + j * 8 + row + 1] for j in range(blocks)], axis=1)

    def share(value, parts):
        size = value.shape[1] // parts
        return sum(jnp.where(b == i, 1.0, 0.0) * value[:, i * size : (i + 1) * size] for i in range(parts))

    parts = dim // gbup_ref.shape[-1]
    flipped = mats_ref[0].astype(F32).T
    for j in range(3):
        gqkv_ref[j] = flipped[j * group_dim : (j + 1) * group_dim]
    gout_ref[...] = flipped[3 * group_dim :]
    gup_ref[...] = mats_ref[1].astype(F32)
    gdown_ref[...] = mats_ref[2].astype(F32).T
    for n in range(2):
        gbqv_ref[n : n + 1] = share(bias_ref[0:1, 2 * n * group_dim : (2 * n + 1) * group_dim], parts)
    gbout_ref[...] = (vector(vec_at.start, 5)).reshape(dim)
    for n in range(2):
        ggain_ref[n : n + 1] = vector(vec_at.start, n)
        gshift_ref[n : n + 1] = vector(vec_at.start, 2 + n)
    gbdown_ref[...] = (vector(vec_at.start, 4)).reshape(dim)
    ups = [vector(bup_at.start, m) for m in range(dim // group_dim)]
    gbup_ref[...] = (share(sum(jnp.where(z == m, 1.0, 0.0) * ups[m] for m in range(len(ups))), parts)).reshape(gbup_ref.shape[0])
    for j in range(blocks):
        gsw1_ref[j * width : (j + 1) * width] = sums_ref[j * width : (j + 1) * width].T
    gsbias_ref[...] = sums_ref[small_at.start : small_at.start + 2]
    gquery_ref[...] = (sums_ref[small_at.start + 2 : small_at.start + 3]).reshape(width)
    gsb3_ref[...] = (sums_ref[small_at.start + 3 : small_at.start + 4][:, :classes]).reshape(classes)
    gsw2_ref[...] = sums_ref[w2_at]
    gsw3_ref[...] = sums_ref[w3_at][:classes]


def finish(mats, sums, bias, model_size, classes):
    depth, dim = mats.shape[1:]
    width = sums.shape[1]
    group_dim = dim // model_size
    batch_size = dim // depth
    f32 = lambda *shape: jax.ShapeDtypeStruct(shape, F32)
    return pl.pallas_call(
        functools.partial(finish_kernel, classes),
        out_shape=(
            f32(3, group_dim, depth),
            f32(2, group_dim // batch_size),
            f32(group_dim, depth),
            f32(dim),
            f32(2, dim),
            f32(2, dim),
            f32(depth, dim),
            f32(depth),
            f32(dim, depth),
            f32(dim),
            f32(dim, width),
            f32(2, width),
            f32(width),
            f32(width, width),
            f32(classes, width),
            f32(classes),
        ),
        compiler_params=pltpu.CompilerParams(vmem_limit_bytes=VMEM_MOST),
        name="finish",
    )(mats, sums, bias)


def rows_back(grad_x, exit_flag, target, live, slot_depth):
    batch_size, model_size = lax.axis_size("batch"), lax.axis_size("mp")
    own_rows, seq, dim = grad_x.shape
    row_count = exit_flag.shape[0]
    capacity, slot_count = own_rows * model_size, batch_size * slot_depth
    alive_rows = 1 - exit_flag > 0
    same_goal = (target[:, None] == target[None, :]) & alive_rows[:, None] & alive_rows[None, :]
    row_order = jnp.arange(row_count, dtype=jnp.int32)
    slot_in = jnp.sum(
        (same_goal & (row_order[None, :] < row_order[:, None])).astype(jnp.int32), axis=1
    )
    flat_slot = target * slot_depth + slot_in
    send_low = (
        (jnp.arange(slot_count, dtype=jnp.int32)[:, None] == flat_slot[None, :]) & alive_rows[None, :]
    ).astype(BF16)
    live_flat = live.reshape(-1)
    position = jnp.cumsum(live_flat.astype(jnp.int32)) - 1
    pick_low = (
        (jnp.arange(capacity, dtype=jnp.int32)[:, None] == position[None, :]) & (live_flat[None, :] > 0)
    ).astype(BF16)
    mine = lax.all_to_all(grad_x, "mp", split_axis=1, concat_axis=0, tiled=True)
    back = jnp.einsum("ck,csd->ksd", pick_low, mine, preferred_element_type=F32).astype(BF16)
    back = back.reshape((batch_size, slot_depth) + back.shape[1:])
    got = lax.all_to_all(back, "batch", split_axis=0, concat_axis=0, tiled=True)
    got = got.reshape((slot_count,) + got.shape[2:])
    return jnp.einsum("kr,ksd->rsd", send_low, got, preferred_element_type=F32).astype(BF16)


def matrix_sums(grads):
    sums = []
    for grad in grads:
        part = lax.psum_scatter(grad, "mp", scatter_dimension=0, tiled=True)[0]
        part = lax.psum_scatter(part, "batch", scatter_dimension=0, tiled=True)
        sums.append(lax.psum(part, "grp"))
    return sums


def on_device(
    rows_in, segment_ids, pair_labels, pair_mask, exit_flag, target, cot_out,
    w_qkv, b_qv, w_out, b_out, ln_gain, ln_bias, w_up, b_up, w_down, b_down,
    s_w1, s_bias, s_query, s_w2, s_w3, s_b3,
):
    batch_size = lax.axis_size("batch")
    model_size = lax.axis_size("mp")
    row_count, _, model_dim = rows_in.shape
    own_rows = cot_out.shape[0]
    capacity = own_rows * model_size
    slot_depth = (capacity + batch_size - 1) // batch_size
    pair_count = pair_labels.shape[1]
    my_mp = lax.axis_index("mp")
    own, got_tags, vecs, rows_own, w_a, w_b, early, qkv, ctx, lse, xhat_one, rstd_one = enter(
        exit_flag, target, rows_in, segment_ids, pair_labels, pair_mask, w_qkv, w_out, b_qv, b_up, b_out,
        w_up, w_down, own_rows, batch_size, model_size,
    )
    scatter = batch_size == 2
    mixed_out, grad_resid, d_wb, mat_c, hand, pack = ffn_both(
        xhat_one, rstd_one, ln_gain, ln_bias, w_b, w_down, early, vecs, b_down, cot_out, own, pair_count, scatter,
        s_w1, s_bias, s_query, s_w2, s_w3, s_b3,
    )
    if scatter:
        grad_rows, mats, sums, bias_sum = leave(
            exit_flag, target, got_tags, own, rows_own, grad_resid, w_a, qkv, ctx, lse, d_wb, mat_c, hand, pack,
            row_count, batch_size, pair_count,
        )
        mats = mats.reshape(3, model_dim // batch_size, model_dim)
        sums = sums.reshape(pack.shape)
    else:
        grad_x, d_wa, bias_part = attn_backward(rows_own, grad_resid, w_a, qkv, ctx, lse, own)
        grad_rows = rows_back(grad_x, exit_flag, target, got_tags[:, :slot_depth, 2 * pair_count], slot_depth)
        whole = (model_size, model_dim, model_dim)
        mats = matrix_sums((d_wa, d_wb.reshape(whole), mat_c.reshape(whole)))
        sums, bias_sum = lax.psum((pack, bias_part[:, 0]), ("grp", "batch", "mp"))
        bias_sum = lax.dynamic_index_in_dim(bias_sum, my_mp, 0)
        mats = jnp.stack(mats)

    (
        g_wqkv, g_bqv, g_wout, g_bout, g_gain, g_shift, g_wup, g_bup, g_wdown, g_bdown,
        g_sw1, g_sbias, g_query, g_sw2, g_sw3, g_sb3,
    ) = finish(mats, sums, bias_sum, model_size, s_w3.shape[1])
    return (
        mixed_out, grad_rows, jnp.transpose(g_wqkv, (0, 2, 1)), g_bqv, g_wout, g_bout, g_gain, g_shift, g_wup,
        g_bup, g_wdown, g_bdown, g_sw1, g_sbias, g_query, g_sw2, g_sw3.T, g_sb3,
    )


def solution(mesh):
    return jax.shard_map(
        on_device,
        mesh=mesh,
        in_specs=(
            P(("grp", "batch"), "mp", None),
            P(("grp", "batch"), None),
            P(("grp", "batch"), None),
            P(("grp", "batch"), None),
            P(("grp", "batch")),
            P(("grp", "batch")),
            P(("grp", "batch", "mp"), None, None),
            P(None, None, "mp"),
            P(None, "mp"),
            P("mp", None),
            P(),
            P(),
            P(),
            P(None, "mp"),
            P("mp"),
            P("mp", None),
            P(),
            P(),
            P(),
            P(),
            P(),
            P(),
            P(),
        ),
        out_specs=(
            P(("grp", "batch", "mp"), None, None),
            P(("grp", "batch"), "mp", None),
            P(None, "batch", "mp"),
            P(None, ("mp", "batch")),
            P("mp", "batch"),
            P(),
            P(),
            P(),
            P("batch", "mp"),
            P(("mp", "batch")),
            P("mp", "batch"),
            P(),
            P(),
            P(),
            P(),
            P(),
            P(),
            P(),
        ),
        check_vma=False,
    )
```

```python
import functools

import jax
import jax.numpy as jnp
from jax import lax
from jax.experimental import pallas as pl
from jax.experimental.pallas import tpu as pltpu
from jax.sharding import PartitionSpec as P

HEAD_DIM = 64
EPS = 1e-12
NEG = -1000000000.0
PRECISE = lax.Precision.HIGHEST
F32 = jnp.float32
BF16 = jnp.bfloat16
BLOCK = 512
VMEM_MOST = 62 * 1024 * 1024
NN = (((1,), (0,)), ((), ()))
NT = (((1,), (1,)), ((), ()))
TN = (((0,), (0,)), ((), ()))


def mm(left, right, dims=NN):
    return lax.dot_general(left, right, dims, preferred_element_type=F32)


def mm_exact(left, right, dims=NN):
    return lax.dot_general(left, right, dims, precision=PRECISE, preferred_element_type=F32)


def norm_parts(resid):
    center = resid - jnp.mean(resid, axis=-1, keepdims=True)
    spread = jnp.mean(center * center, axis=-1, keepdims=True)
    rstd = lax.rsqrt(spread + EPS)
    return center * rstd, rstd


def norm_back(upstream, xhat, rstd, gain):
    scaled = upstream * gain
    mean_u = jnp.mean(scaled, axis=-1, keepdims=True)
    mean_ux = jnp.mean(scaled * xhat, axis=-1, keepdims=True)
    return (scaled - mean_u - xhat * mean_ux) * rstd


def column_sum(value):
    return jnp.sum(value, axis=0, keepdims=True)


def mesh_place():
    g, b, z = lax.axis_index("grp"), lax.axis_index("batch"), lax.axis_index("mp")
    hi, lo, bit = g // 2, g % 2, b % 2
    return dict(
        g=g, b=b, z=z, hi=hi, lo=lo, bit=bit,
        far={"grp": (1 - hi) * 2 + lo}, twin={"grp": hi * 2 + 1 - lo}, side={"batch": b + 1 - 2 * bit},
        far_twin={"grp": (1 - hi) * 2 + 1 - lo},
    )


def remote(src, dst, send_sem, recv_sem, device):
    return pltpu.make_async_remote_copy(
        src_ref=src, dst_ref=dst, send_sem=send_sem, recv_sem=recv_sem,
        device_id=device, device_id_type=pl.DeviceIdType.MESH,
    )


def greet(at, batch_size, model_size):
    barrier = pltpu.get_barrier_semaphore()
    peers = [at["far"], at["twin"]]
    if batch_size > 1:
        peers += [{"batch": (at["b"] + j) % batch_size} for j in range(1, batch_size)]
    else:
        peers += [at["side"]]
    peers += [{"mp": (at["z"] + i) % model_size} for i in range(1, model_size)]
    for peer in peers:
        pl.semaphore_signal(barrier, inc=1, device_id=peer, device_id_type=pl.DeviceIdType.MESH)
    pl.semaphore_wait(barrier, len(peers))


def begin(copies):
    for copy in copies:
        copy.start()


def arrive(copies):
    for copy in copies:
        copy.wait_recv()


def sent(copies):
    for copy in copies:
        copy.wait_send()


class Gather:
    def __init__(self, at, model_size, home, spot, send_sem, recv_sem, early=None):
        self.at, self.home, self.spot, self.early = at, home, spot, early
        self.send_sem, self.recv_sem = send_sem, recv_sem
        z, lo, hi, bit = at["z"], at["lo"], at["hi"], at["bit"]
        self.near = z + 1 - 2 * (z % 2)
        self.cross = (z + 2) % model_size
        self.chunks = (self.near, self.cross, (self.near + 2) % model_size)
        piece = home.shape[0] // 16
        half = pl.multiple_of(lo * (8 * piece), 16)
        self.one_a = pl.ds(pl.multiple_of(half + bit * (2 * piece) + hi * piece, 16), piece)
        self.one_b = pl.ds(pl.multiple_of(half + 4 * piece + hi * (2 * piece) + bit * piece, 16), piece)
        self.two_a = pl.ds(pl.multiple_of(half + bit * (2 * piece), 16), 2 * piece)
        self.two_b = pl.ds(pl.multiple_of(half + 4 * piece + hi * (2 * piece), 16), 2 * piece)
        rows = lambda first, count: pl.ds(pl.multiple_of(half + first * piece, 16), count * piece)
        self.pieces = (
            (self.one_a, self.one_b),
            (rows(bit * 2 + 1 - hi, 1), rows(4 + hi * 2 + 1 - bit, 1)),
            (rows(2 - 2 * bit, 2), rows(6 - 2 * hi, 2)),
        )

    def copies(self, stage, i):
        at, home, spot = self.at, self.home, self.spot

        def one(slot, src, dst, device):
            return remote(src, dst, self.send_sem.at[slot], self.recv_sem.at[slot], device)

        def same(slot, m, rows, device):
            return one(slot, spot.at[m, rows], spot.at[m, rows], device)

        m = self.chunks[i]
        if stage == 0 and i < 2:
            return [
                one(2 * i, home.at[self.one_a], spot.at[at["z"], self.one_a], {"mp": m}),
                one(2 * i + 1, home.at[self.one_b], spot.at[at["z"], self.one_b], {"mp": m}),
            ]
        if stage == 0:
            return [
                same(4, self.cross, self.one_a, {"mp": self.near}),
                same(5, self.cross, self.one_b, {"mp": self.near}),
            ]
        if stage == 1 and self.early is not None:
            return [
                one(6 + 2 * i, self.early.at[i, 0], spot.at[m, self.one_a], at["far"]),
                one(7 + 2 * i, self.early.at[i, 1], spot.at[m, self.one_b], at["side"]),
            ]
        if stage == 1:
            return [same(6 + 2 * i, m, self.one_a, at["far"]), same(7 + 2 * i, m, self.one_b, at["side"])]
        if stage == 2:
            return [same(12 + 2 * i, m, self.two_a, at["side"]), same(13 + 2 * i, m, self.two_b, at["far"])]
        raise ValueError(stage)

    def to_twin(self, stage, i):
        m, twin = self.chunks[i], self.at["twin"]
        source = [self.spot.at[m, rows] for rows in self.pieces[stage]]
        if stage == 0 and self.early is not None:
            source = [self.early.at[i, p] for p in range(2)]
        slot = 18 + 6 * i + 2 * stage
        return [
            remote(src, self.spot.at[m, rows], self.send_sem.at[slot + n], self.recv_sem.at[slot + n], twin)
            for n, (src, rows) in enumerate(zip(source, self.pieces[stage]))
        ]

    def start(self):
        begin(self.copies(0, 1) + self.copies(0, 0))

    def early_copies(self, stage):
        def one(slot, src, dst, device):
            return remote(src, dst, self.send_sem.at[slot], self.recv_sem.at[slot], device)

        if stage == 0:
            return [
                one(2 * i + p, self.home.at[rows], self.early.at[i, p], {"mp": self.chunks[i]})
                for i in (1, 0)
                for p, rows in enumerate((self.one_a, self.one_b))
            ]
        return [one(4 + p, self.early.at[1, p], self.early.at[2, p], {"mp": self.near}) for p in range(2)]

    def own_pieces(self, sem):
        return [
            pltpu.make_async_copy(self.early.at[i, p], self.spot.at[self.chunks[i], rows], sem.at[2 * i + p])
            for i in range(3)
            for p, rows in enumerate((self.one_a, self.one_b))
        ]

    def advance(self, stage, *parts):
        for i in parts:
            arrive(self.copies(stage - 1, i))
            if stage == 1 and i == 1:
                begin(self.copies(0, 2))
            begin((self.copies(stage, i) if stage < 3 else []) + self.to_twin(stage - 1, i))

    def done(self, *parts):
        for i in parts:
            for stage in range(3):
                arrive(self.to_twin(stage, i))

    def sent(self):
        for stage in range(3):
            for i in range(3):
                if stage > 0 or self.early is None:
                    sent(self.copies(stage, i))
                sent(self.to_twin(stage, i))


GATHER_SEMS = 36
PARTS = 2


class Reduce:
    def __init__(self, at, model_size, full, base, got_half, got_a, got_b, got_a2, got_b2, last, got_z, out,
                 send_sem, recv_sem, far_first=0, direct=False):
        self.far_first, self.direct = far_first, direct
        self.at, self.full, self.base, self.got_half = at, full, base, got_half
        self.got_a, self.got_b, self.got_a2, self.got_b2 = got_a, got_b, got_a2, got_b2
        self.last, self.got_z, self.out = last, got_z, out
        self.send_sem, self.recv_sem = send_sem, recv_sem
        z = at["z"]
        self.near, self.cross = z + 1 - 2 * (z % 2), (z + 2) % model_size

    def copies(self, stage, i=0):
        at, base = self.at, self.base
        b, lo, hi = at["b"], at["lo"], at["hi"]

        def one(slot, src, dst, device):
            return remote(src, dst, self.send_sem.at[slot], self.recv_sem.at[slot], device)

        m = chunk_of(at, i)
        if stage == 0:
            return [
                one(25 + 4 * i + 2 * y + p, self.full.at[m, y, 1 - lo, p], self.got_half.at[m, y, p], at["twin"])
                for y in range(2)
                for p in range(PARTS)
            ]
        if stage == 1 and i < self.far_first:
            return [
                one(4 + 2 * i, base.at[m, :, 0, 1 - hi], self.got_a.at[m], at["far"]),
                one(5 + 2 * i, base.at[m, :, 1, 1 - hi], self.got_b.at[m], at["far"]),
            ]
        if stage == 2 and i < self.far_first:
            return [
                one(12 + 2 * i, base.at[m, 1 - b, 0, hi], self.got_a2.at[m], at["side"]),
                one(13 + 2 * i, base.at[m, 1 - b, 1, hi], self.got_b2.at[m], at["side"]),
            ]
        if stage == 1:
            return [
                one(4 + 2 * i, base.at[m, :, 0, 1 - hi], self.got_a.at[m], at["far"]),
                one(5 + 2 * i, base.at[m, 1 - b, 1], self.got_b.at[m], at["side"]),
            ]
        if stage == 2:
            return [
                one(12 + 2 * i, base.at[m, 1 - b, 0, hi], self.got_a2.at[m], at["side"]),
                one(13 + 2 * i, base.at[m, b, 1, 1 - hi], self.got_b2.at[m], at["far"]),
            ]
        if stage == 3:
            device = {"mp": self.cross if i == 2 else self.near}
            return [one(20 + i, self.last.at[m], self.got_z.at[i], device)] if i < 3 else []
        mine = self.out.at[lo, :, hi]
        if stage == 4 and self.direct:
            return [one(23 + 18 * n, mine, mine, at[peer]) for n, peer in enumerate(("far", "twin", "far_twin"))]
        if stage == 4:
            return [one(23, mine, mine, at["far"])]
        if self.direct:
            return []
        return [one(24, self.out.at[lo], self.out.at[lo], at["twin"])]

    def start(self, i):
        begin(self.copies(0, i))

    def after_core(self, i, go_on=True):
        arrive(self.copies(0, i))
        m = chunk_of(self.at, i)

        def one(n, _):
            y, p, h = n // 4, n // 2 % 2, n % 2
            self.base[m, y, p, h] = self.base[m, y, p, h] + self.got_half[m, y, p, h]
            return 0

        lax.fori_loop(0, 8, one, 0)
        if go_on:
            begin(self.copies(1, i))

    def after_one(self, i):
        arrive(self.copies(1, i))
        m, b, hi, base = chunk_of(self.at, i), self.at["b"], self.at["hi"], self.base
        for h in range(2):
            base[m, h, 0, hi] = base[m, h, 0, hi] + self.got_a[m, h]
            if i < self.far_first:
                base[m, h, 1, hi] = base[m, h, 1, hi] + self.got_b[m, h]
            else:
                base[m, b, 1, h] = base[m, b, 1, h] + self.got_b[m, h]
        begin(self.copies(2, i))

    def after_two(self, i, go_on=True):
        arrive(self.copies(2, i))
        m, b, hi, base = chunk_of(self.at, i), self.at["b"], self.at["hi"], self.base
        found = [base[m, b, 0, hi] + self.got_a2[m], base[m, b, 1, hi] + self.got_b2[m]]
        if i == 2:
            arrive(self.copies(3, 0))
        for p in range(PARTS):
            self.last[m, p] = found[p] + self.got_z[0, p] if i == 2 else found[p]
        if go_on:
            begin(self.copies(3, i))

    def total(self, p):
        z = self.at["z"]
        found = self.last[z, p].astype(F32) + self.got_z[1, p].astype(F32) + self.got_z[2, p].astype(F32)
        return found.astype(BF16)

    def after_three(self):
        arrive(self.copies(3, 1) + self.copies(3, 2))
        for p in range(PARTS):
            self.out[self.at["lo"], p, self.at["hi"]] = self.total(p)
        begin(self.copies(4))

    def hand_over(self, own_ref, hand_ref):
        arrive(self.copies(3, 1))
        own_ref[...] = self.base[self.at["z"]]
        hand_ref[0] = self.last[self.cross]
        hand_ref[1] = self.got_z[1]

    def after_four(self):
        arrive(self.copies(4))
        begin(self.copies(5))

    def done(self):
        arrive(self.copies(4) if self.direct else self.copies(5))

    def sent(self):
        for stage in range(6):
            for i in range(4 if stage < 4 else 1):
                sent(self.copies(stage, i))

    def sent_early(self):
        for stage, count in enumerate((4, 3, 3, 2)):
            for i in range(count):
                sent(self.copies(stage, i))


class Finish:
    def __init__(self, at, model_size, own, hand, got_a, got_b, got_a2, got_b2, got_z, out, send_sem, recv_sem):
        self.at, self.own, self.hand, self.out = at, own, hand, out
        self.got_a, self.got_b, self.got_a2, self.got_b2, self.got_z = got_a, got_b, got_a2, got_b2, got_z
        self.send_sem, self.recv_sem = send_sem, recv_sem
        self.cross = (at["z"] + 2) % model_size

    def copies(self, stage):
        at, own = self.at, self.own
        b, lo, hi = at["b"], at["lo"], at["hi"]

        def one(slot, src, dst, device):
            return remote(src, dst, self.send_sem.at[slot], self.recv_sem.at[slot], device)

        if stage == 0:
            return [one(0, self.hand.at[0], self.got_z, {"mp": self.cross})]
        if stage == 1:
            return [
                one(1, own.at[:, 0, 1 - hi], self.got_a, at["far"]),
                one(2, own.at[1 - b, 1], self.got_b, at["side"]),
            ]
        if stage == 2:
            return [
                one(3, self.got_a.at[1 - b], self.got_a2, at["side"]),
                one(4, self.got_b.at[1 - hi], self.got_b2, at["far"]),
            ]
        mine = self.out.at[lo, :, hi]
        return [one(5 + n, mine, mine, at[peer]) for n, peer in enumerate(("far", "twin", "far_twin"))]

    def start(self):
        begin(self.copies(1) + self.copies(0))

    def after_one(self):
        arrive(self.copies(1))
        b, hi = self.at["b"], self.at["hi"]
        for h in range(2):
            self.got_a[h] = self.got_a[h] + self.own[h, 0, hi]
            self.got_b[h] = self.got_b[h] + self.own[b, 1, h]
        begin(self.copies(2))

    def after_two(self):
        arrive(self.copies(2) + self.copies(0))
        b, lo, hi = self.at["b"], self.at["lo"], self.at["hi"]
        halves = ((self.got_a[b], self.got_a2[...]), (self.got_b[hi], self.got_b2[...]))
        for p, (held, got) in enumerate(halves):
            total = held.astype(F32) + got.astype(F32) + self.hand[1, p].astype(F32) + self.got_z[p].astype(F32)
            self.out[lo, p, hi] = total.astype(BF16)
        begin(self.copies(3))

    def done(self):
        arrive(self.copies(3))

    def sent(self):
        for stage in range(4):
            sent(self.copies(stage))


REDUCE_SEMS = 60


def chunk_of(at, i):
    high, low = at["z"] // 2, at["z"] % 2
    flip_high, flip_low = 1 - i % 2, 1 - i // 2
    return 2 * (high + flip_high - 2 * high * flip_high) + low + flip_low - 2 * low * flip_low


def reduce_scratch(model_size, piece, dim):
    low = lambda *shape: pltpu.VMEM(shape, BF16)
    return [
        low(model_size, 2, PARTS, 2, piece, dim),
        low(model_size, 2, piece, dim),
        low(model_size, 2, piece, dim),
        low(model_size, piece, dim),
        low(model_size, piece, dim),
        low(model_size, PARTS, piece, dim),
        low(3, PARTS, piece, dim),
    ]


def pack_places(dim, width):
    ends = [dim]
    for size in (width, 16, 8, 8 * dim // width, 8 * dim // width):
        ends.append(ends[-1] + size)
    return [slice(first, last) for first, last in zip(ends[:-1], ends[1:])]


def pack_rows(dim, width):
    return -(-pack_places(dim, width)[-1].stop // 128) * 128


def student_step(
    stud_ref, own_ref, query_ref, w2_ref, bmid, w3_ref, b3_ref,
    dstud_ref, gw2_ref, gw3_ref, gsmall_ref, classes, pairs,
):
    row_count, seq, width = stud_ref.shape
    head = own_ref.shape[1] - seq
    tag_cells = [
        [own_ref[r : r + 1, p : p + 1] for p in range(2 * pairs)] for r in range(row_count)
    ]
    labels = jnp.concatenate([cells[p] for cells in tag_cells for p in range(pairs)], axis=0)
    weights = jnp.concatenate([cells[pairs + p] for cells in tag_cells for p in range(pairs)], axis=0)
    half = width // 2
    lane = lax.broadcasted_iota(jnp.int32, (2 * pairs, width), 1)
    row = lax.broadcasted_iota(jnp.int32, (2 * pairs, width), 0)
    mine = (lane >= half) == (row >= pairs)
    query_rows = jnp.where(mine, query_ref[...].reshape(1, width) * half ** (-0.5), 0.0)
    pair_of = lax.rem(lax.broadcasted_iota(jnp.int32, (2 * pairs, seq), 0), pairs).astype(F32)
    members, shares_all, pooled_all = [], [], []
    for r in range(row_count):
        scores = mm_exact(query_rows, stud_ref[r], NT)
        member = own_ref[r : r + 1, head:] == pair_of
        masked = jnp.where(member, scores, NEG)
        terms = jnp.exp(masked - jnp.max(masked, axis=1, keepdims=True))
        shares = terms / jnp.sum(terms, axis=1, keepdims=True)
        pooled = jnp.where(mine, mm_exact(shares, stud_ref[r]), 0.0)
        members.append(member)
        shares_all.append(shares)
        pooled_all.append(pooled[:pairs] + pooled[pairs:])
    pooled = jnp.concatenate(pooled_all, axis=0)
    middle = jnp.tanh(mm_exact(pooled, w2_ref[...]) + bmid)
    logits = mm_exact(middle, w3_ref[...], NT) + b3_ref[...]
    class_of = lax.broadcasted_iota(jnp.int32, logits.shape, 1)
    logits = jnp.where(class_of < classes, logits, NEG)
    terms = jnp.exp(logits - jnp.max(logits, axis=1, keepdims=True))
    chance = terms / jnp.sum(terms, axis=1, keepdims=True)
    grad_logits = weights * (chance - jnp.where(class_of.astype(F32) == labels, 1.0, 0.0))
    gw3_ref[...] = mm_exact(grad_logits, middle, TN)[: gw3_ref.shape[0]]
    grad_pre = mm_exact(grad_logits, w3_ref[...]) * (1.0 - middle * middle)
    gw2_ref[...] = mm_exact(pooled, grad_pre, TN)
    grad_pooled = mm_exact(grad_pre, w2_ref[...], NT)
    grad_query = jnp.zeros((1, width), F32)
    grad_bias = jnp.zeros((1, width), F32)
    for r in range(row_count):
        part = grad_pooled[r * pairs : (r + 1) * pairs]
        grad_parts = jnp.where(mine, jnp.concatenate([part, part], axis=0), 0.0)
        shares = shares_all[r]
        grad_shares = mm_exact(grad_parts, stud_ref[r], NT)
        inner = jnp.sum(shares * grad_shares, axis=1, keepdims=True)
        grad_scores = jnp.where(members[r], shares * (grad_shares - inner), 0.0)
        grad_hidden = mm_exact(
            jnp.concatenate([shares, grad_scores], axis=0),
            jnp.concatenate([grad_parts, query_rows], axis=0),
            TN,
        )
        low = grad_hidden.astype(BF16)
        dstud_ref[r] = low
        grad_bias += column_sum(low.astype(F32))
        found = mm_exact(grad_scores, stud_ref[r]) * half ** (-0.5)
        grad_query += column_sum(jnp.where(mine, found, 0.0))
    gsmall_ref[0:1] = grad_bias
    gsmall_ref[1:2] = column_sum(grad_pre)
    gsmall_ref[2:3] = grad_query
    gsmall_ref[3:4] = column_sum(grad_logits)
    gsmall_ref[4:8] = jnp.zeros((4, width), F32)


def gelu_parts(value):
    size = jnp.abs(value)
    bell = jnp.exp(value * value * -0.5)
    base = 1.0 + (0.3275911 * 0.5 ** 0.5) * size
    t = pl.reciprocal(base, approx=True)
    t = t * (2.0 - base * t)
    terms = ((((1.061405429 * t - 1.453152027) * t + 1.421413741) * t - 0.284496736) * t + 0.254829592) * t
    tail = 0.5 * terms * bell
    return jnp.where(value < 0.0, tail, 1.0 - tail), bell * 0.3989422804014327


COLUMNS = 256


def ffn_kernel(
    classes, pairs, scatter,
    xhat1_ref, rstd1_ref, gain_ref, shift_ref, wb_hbm, wc_home, early_ref, vecs_ref, bdown_ref, cot_hbm, own_ref,
    sw1_ref, sbias_ref, query_ref, w2_in, w3_in, b3_in,
    mixed_ref, gres_ref, dwb_ref, out_ref, hand_ref, packed_ref,
    pack_ref, w2_ref, w3_ref, b3_ref, gbup_ref, gvec_ref, gsw1_ref, act_ref, slope_ref, xhat2_ref, rstd2_ref,
    stud_ref, dstud_ref, low_ref, flip_ref, wc_ref, dwc_ref, wsend, wrecv, msend, mrecv, local_sem, piece_sem, wb_ref, cot_ref, *parts,
):
    row_count, seq, dim = xhat1_ref.shape
    model_size = wb_ref.shape[0]
    inner = wb_ref.shape[2]
    per_row = seq // BLOCK
    blocks = row_count * per_row
    width = sw1_ref.shape[1]
    at = mesh_place()
    gather = Gather(at, model_size, wc_home, wc_ref, wsend, wrecv, early_ref)
    own_pieces = gather.own_pieces(piece_sem)
    own_copy = pltpu.make_async_copy(wc_home, wc_ref.at[at["z"]], local_sem.at[0])
    own_copy.start()
    loads = [
        pltpu.make_async_copy(wb_hbm, wb_ref, local_sem.at[1]),
        pltpu.make_async_copy(cot_hbm, cot_ref, local_sem.at[2]),
    ]
    begin(loads)
    for copy in own_pieces:
        copy.start()
    greet(at, 2 if scatter else 1, model_size)
    for i in (1, 0, 2):
        begin(gather.copies(1, i) + gather.to_twin(0, i))
    if scatter:
        reducer = Reduce(at, model_size, dwc_ref, dwc_ref.at[:, :, at["lo"]], *parts, None, msend, mrecv)

    w2_at, w3_at, small_at, vec_at, bup_at = pack_places(dim, width)
    sb1, bmid = sbias_ref[0:1], sbias_ref[1:2]
    w2_ref[...] = w2_in[...].astype(F32)
    w3_ref[...] = jnp.zeros_like(w3_ref)
    w3_ref[:classes] = w3_in[...].astype(F32)
    b3_ref[...] = jnp.zeros_like(b3_ref)
    b3_ref[:, :classes] = b3_in[...].reshape(1, classes)
    gain_one, gain_two = gain_ref[0:1], gain_ref[1:2]
    shift_one, shift_two = shift_ref[0:1], shift_ref[1:2]

    def live(r):
        cells = [own_ref[i : i + 1, 2 * pairs : 2 * pairs + 1] for i in range(row_count)]
        return sum(jnp.where(r == i, 1.0, 0.0) * cells[i] for i in range(row_count))

    def place(t):
        return t // per_row, pl.ds(pl.multiple_of(t % per_row * BLOCK, BLOCK), BLOCK)

    def prepare(t, _):
        r, part = place(t)
        hidden = xhat1_ref[r, part] * gain_one + shift_one
        low_ref[t] = hidden.astype(BF16)
        xhat2_ref[r, part] = hidden + bdown_ref[...].reshape(1, dim)
        return 0

    lax.fori_loop(0, blocks, prepare, 0)
    for copy in own_pieces:
        copy.wait()
    loads[0].wait()

    def during(m, table):
        for when, actions in table.items():
            @pl.when(m == when)
            def _():
                for action, *args in actions:
                    action(*args)

    def up(m, _):
        during(m, {
            1: [(gather.advance, 2, 1, 0)],
            2: [(gather.advance, 2, 2), (gather.advance, 3, 1)],
            3: [(gather.advance, 3, 0)],
        })

        def one(t, _):
            low = low_ref[t]
            for c in range(0, inner, COLUMNS):
                columns = slice(c, c + COLUMNS)
                pre = mm(low, wb_ref[m, :, columns]) + vecs_ref[m, 1:2, columns]
                cdf, pdf = gelu_parts(pre)
                act_ref[m, t, :, columns] = (pre * cdf).astype(BF16)
                slope_ref[m, t, :, columns] = (cdf + pre * pdf).astype(BF16)
            return 0

        lax.fori_loop(0, blocks, one, 0)
        return 0

    lax.fori_loop(0, model_size, up, 0)
    gather.advance(3, 2)
    own_copy.wait()

    def down(m):
        def one(t, _):
            r, part = place(t)
            xhat2_ref[r, part] = xhat2_ref[r, part] + mm(act_ref[m, t], wc_ref[m])
            return 0

        lax.fori_loop(0, blocks, one, 0)

    down(at["z"])
    for i in (1, 0, 2):
        gather.done(i)
        down(gather.chunks[i])

    def norm_two(t, _):
        r, part = place(t)
        xhat, rstd = norm_parts(xhat2_ref[r, part])
        xhat2_ref[r, part] = xhat
        rstd2_ref[r, part] = rstd
        hidden_two = xhat * gain_two + shift_two
        mixed_ref[r, part] = (hidden_two * live(r)).astype(BF16)
        stud_ref[r, part] = mm(hidden_two.astype(BF16), sw1_ref[...]) + sb1
        return 0

    lax.fori_loop(0, blocks, norm_two, 0)
    student_step(
        stud_ref, own_ref, query_ref, w2_ref, bmid, w3_ref, b3_ref,
        dstud_ref, pack_ref.at[w2_at], pack_ref.at[w3_at], pack_ref.at[small_at], classes, pairs,
    )
    gvec_ref[...] = jnp.zeros_like(gvec_ref)
    gsw1_ref[...] = jnp.zeros_like(gsw1_ref)
    gbup_ref[...] = jnp.zeros_like(gbup_ref)

    loads[1].wait()

    def norm_two_back(t, _):
        r, part = place(t)
        xhat = xhat2_ref[r, part]
        two_low = (xhat * gain_two + shift_two).astype(BF16)
        grad_low = dstud_ref[r, part]
        gsw1_ref[...] += mm(grad_low, two_low, TN)
        upstream = cot_ref[r, part].astype(F32) * live(r) + mm(grad_low, sw1_ref[...], NT)
        gvec_ref[1:2] += column_sum(upstream * xhat)
        gvec_ref[3:4] += column_sum(upstream)
        grad = norm_back(upstream, xhat, rstd2_ref[r, part], gain_two)
        low = grad.astype(BF16)
        gvec_ref[4:5] += column_sum(low.astype(F32))
        gres_ref[r, part] = grad
        low_ref[t] = low
        flip_ref[:, pl.ds(pl.multiple_of(t * BLOCK, BLOCK), BLOCK)] = low.T
        return 0

    lax.fori_loop(0, blocks, norm_two_back, 0)
    half = dim // 2

    def weight_grads(out, right_ref, m):
        def one(y, _):
            part = pl.ds(pl.multiple_of(y * half, 128), half)
            total = mm(flip_ref[part, :], right_ref[m].reshape(blocks * BLOCK, inner)).astype(BF16)
            out[m, y] = total.reshape(out.shape[2:])
            return 0

        lax.fori_loop(0, 2, one, 0)

    def first_grads(i, _):
        weight_grads(dwc_ref, act_ref, chunk_of(at, i))
        if scatter:
            during(i, {n: [(reducer.start, n)] for n in range(model_size)})
        return 0

    lax.fori_loop(0, model_size, first_grads, 0)
    def backward(m, _):
        if scatter:
            during(m, {
                1: [(reducer.after_core, 0)],
                2: [(reducer.after_core, 1), (reducer.after_one, 0)],
                3: [(reducer.after_two, 0), (reducer.after_one, 1), (reducer.after_core, 2)],
            })

        def one(t, _):
            r, part = place(t)
            grad_pre = (mm(low_ref[t], wc_ref[m], NT) * slope_ref[m, t].astype(F32)).astype(BF16)
            slope_ref[m, t] = grad_pre
            gbup_ref[m] += column_sum(grad_pre.astype(F32))
            gres_ref[r, part] = gres_ref[r, part] + mm(grad_pre, wb_ref[m], NT)
            return 0

        lax.fori_loop(0, blocks, one, 0)
        return 0

    lax.fori_loop(0, model_size, backward, 0)

    def norm_one_back(t, _):
        r, part = place(t)
        upstream = gres_ref[r, part]
        xhat = xhat1_ref[r, part]
        gvec_ref[0:1] += column_sum(upstream * xhat)
        gvec_ref[2:3] += column_sum(upstream)
        resid = norm_back(upstream, xhat, rstd1_ref[r, part], gain_one)
        gres_ref[r, part] = resid
        gvec_ref[5:6] += column_sum(resid.astype(BF16).astype(F32))
        flip_ref[:, pl.ds(pl.multiple_of(t * BLOCK, BLOCK), BLOCK)] = (xhat * gain_one + shift_one).astype(BF16).T
        return 0

    lax.fori_loop(0, blocks, norm_one_back, 0)
    def second_grads(m, _):
        if scatter:
            during(m, {
                1: [(reducer.after_two, 1), (reducer.after_one, 2)],
                3: [(reducer.after_core, 3, False), (reducer.after_two, 2, False)],
            })
        weight_grads(dwb_ref, slope_ref, m)
        return 0

    lax.fori_loop(0, model_size, second_grads, 0)
    for m in range(model_size):
        bup = gbup_ref[m]
        for j in range(dim // width):
            pack_ref[bup_at.start + j * 8 + m : bup_at.start + j * 8 + m + 1] = bup[:, j * width : (j + 1) * width]
    for j in range(dim // width):
        columns = slice(j * width, (j + 1) * width)
        pack_ref[columns] = gsw1_ref[:, columns]
        pack_ref[vec_at.start + j * 8 : vec_at.start + j * 8 + 8] = gvec_ref[:, columns]
        if model_size < 8:
            first = bup_at.start + j * 8
            pack_ref[first + model_size : first + 8] = jnp.zeros((8 - model_size, width), F32)
    pack_ref[bup_at.stop :] = jnp.zeros((pack_ref.shape[0] - bup_at.stop, width), F32)
    packed_ref[...] = pack_ref[...].astype(BF16)
    if scatter:
        reducer.hand_over(out_ref, hand_ref)
        reducer.sent_early()
    else:
        out_ref[...] = dwc_ref[...]
        hand_ref[...] = jnp.zeros_like(hand_ref)
    gather.sent()


def ffn_both(xhat1, rstd1, gain, shift, w_b, w_c, early, vecs, b_down, cot, own, pairs, scatter,
             s_w1, s_bias, s_query, s_w2, s_w3, s_b3):
    rows, seq, dim = xhat1.shape
    model_size = w_b.shape[0]
    inner = w_b.shape[2]
    width = s_w1.shape[1]
    classes = s_w3.shape[1]
    blocks = rows * seq // BLOCK
    piece = dim // 16
    grid_shape = (model_size, 2, 2, PARTS, 2, piece, inner)
    low = lambda *shape: pltpu.VMEM(shape, BF16)
    f32 = lambda *shape: pltpu.VMEM(shape, F32)
    dma = pltpu.SemaphoreType.DMA
    vmem = pl.BlockSpec(memory_space=pltpu.VMEM)
    hbm = pl.BlockSpec(memory_space=pl.ANY)
    return pl.pallas_call(
        functools.partial(ffn_kernel, classes, pairs, scatter),
        in_specs=[vmem] * 4 + [hbm] * 3 + [vmem, vmem, hbm] + [vmem] * 7,
        out_specs=[vmem] * 6,
        out_shape=(
            jax.ShapeDtypeStruct((rows, seq, dim), BF16),
            jax.ShapeDtypeStruct((rows, seq, dim), F32),
            jax.ShapeDtypeStruct(grid_shape, BF16),
            jax.ShapeDtypeStruct(grid_shape[1:2] + grid_shape[3:] if scatter else grid_shape, BF16),
            jax.ShapeDtypeStruct((2, PARTS, piece, inner), BF16),
            jax.ShapeDtypeStruct((pack_rows(dim, width), width), BF16),
        ),
        scratch_shapes=[
            f32(pack_rows(dim, width), width),
            f32(width, width),
            f32(width, width),
            f32(1, width),
            f32(model_size, 1, inner),
            f32(8, dim),
            f32(width, dim),
            low(model_size, blocks, BLOCK, inner),
            low(model_size, blocks, BLOCK, inner),
            f32(rows, seq, dim),
            f32(rows, seq, 1),
            f32(rows, seq, width),
            low(rows, seq, width),
            low(blocks, BLOCK, dim),
            low(dim, rows * seq),
            low(model_size, inner, dim),
            low(*grid_shape),
            dma((GATHER_SEMS,)),
            dma((GATHER_SEMS,)),
            dma((REDUCE_SEMS,)),
            dma((REDUCE_SEMS,)),
            dma((3,)),
            dma((6,)),
            low(model_size, dim, inner),
            low(rows, seq, dim),
            *(reduce_scratch(model_size, piece, inner) if scatter else ()),
        ],
        compiler_params=pltpu.CompilerParams(
            vmem_limit_bytes=VMEM_MOST, collective_id=1, has_side_effects=True
        ),
        name="ffn_both",
    )(
        xhat1, rstd1, gain, shift, w_b, w_c, early, vecs, b_down, cot, own,
        s_w1, s_bias, s_query, s_w2, s_w3.T, s_b3,
    )


TILE_Q = 256
TILE_BACK = 64


def backward_group(grad_ctx, ctx_of, load, store, mask, lse_of, group_dim, p_ref, s_ref):
    scale = HEAD_DIM ** (-0.5)
    for j in range(group_dim // HEAD_DIM):
        rows = slice(j * HEAD_DIM, (j + 1) * HEAD_DIM)
        k_rows = slice(group_dim + rows.start, group_dim + rows.stop)
        v_rows = slice(2 * group_dim + rows.start, 2 * group_dim + rows.stop)
        q_t = load(rows) * scale
        k_t = load(k_rows)
        v_t = load(v_rows)
        d_t = grad_ctx[rows]
        seq = q_t.shape[1]
        inner = column_sum(d_t.astype(F32) * ctx_of(rows).astype(F32))
        lse = lse_of(j)
        k_n, v_n = k_t.T, v_t.T
        probs_ref, grads_ref = p_ref.at[j % 2], s_ref.at[j % 2]
        for q0 in range(0, seq, TILE_Q):
            columns = slice(q0, q0 + TILE_Q)
            q, d = q_t[:, columns], d_t[:, columns]
            for k0 in range(0, seq, TILE_BACK):
                part = slice(k0, k0 + TILE_BACK)
                probs = jnp.exp(mm(k_n[part], q) + mask[part, columns] - lse[:, columns])
                grad_probs = mm(v_n[part], d)
                probs_ref[part, columns] = probs.astype(BF16)
                grads_ref[part, columns] = (probs * (grad_probs - inner[:, columns])).astype(BF16)
        store(rows, mm(k_t * scale, grads_ref[...]).astype(BF16))
        store(k_rows, mm(q_t, grads_ref[...], NT).astype(BF16))
        store(v_rows, mm(d_t, probs_ref[...], NT).astype(BF16))


def attn_backward_kernel(
    x_ref, gres_ref, wa_ref, qkv_ref, ctx_ref, lse_ref, own_ref, dx_ref, dwa_ref, bias_ref,
    mask_ref, acc_ref, work_ref, xflip_ref, gflip_ref, p_ref, s_ref,
):
    row_count, seq, dim = x_ref.shape
    model_size = wa_ref.shape[0]
    group_dim = ctx_ref.shape[2]
    bias_ref[...] = jnp.zeros_like(bias_ref)
    seg_rows = own_ref[:, own_ref.shape[1] - seq :]
    seg_cols = seg_rows.T
    for r in range(row_count):
        mask_ref[...] = jnp.where(seg_cols[:, r : r + 1] == seg_rows[r : r + 1], 0.0, NEG)
        acc_ref[...] = gres_ref[r]
        grad_low = gres_ref[r].astype(BF16)
        columns = slice(r * seq, (r + 1) * seq)
        gflip_ref[:, columns] = grad_low.T
        xflip_ref[:, columns] = x_ref[r].T

        def one_group(m, _):
            grad_ctx = mm(wa_ref[m, 3 * group_dim :, :], grad_low, NT).astype(BF16)

            def store(rows, value):
                work_ref[r, m, rows, :] = value

            backward_group(
                grad_ctx, lambda rows: ctx_ref[r, m, rows, :], lambda rows: qkv_ref[r, m, rows, :], store,
                mask_ref, lambda j: lse_ref[r, m, j : j + 1, :], group_dim, p_ref, s_ref,
            )
            grads = work_ref[r, m]
            bias_ref[m] += mm(jnp.ones((8, seq), BF16), grads, NT)
            acc_ref[...] += mm(grads, wa_ref[m, : 3 * group_dim, :], TN)
            return 0

        lax.fori_loop(0, model_size, one_group, 0)
        dx_ref[r] = acc_ref[...].astype(BF16)

    def weight_grads(i, _):
        m, part = i // 2, pl.ds(pl.multiple_of(i % 2 * (dim // 2), 128), dim // 2)
        left, right = 0.0, 0.0
        for r in range(row_count):
            columns = slice(r * seq, (r + 1) * seq)
            left += mm(xflip_ref[part, columns], work_ref[r, m], NT)
            right += mm(gflip_ref[part, columns], ctx_ref[r, m], NT)
        dwa_ref[m, part, : 3 * group_dim] = left.astype(BF16)
        dwa_ref[m, part, 3 * group_dim :] = right.astype(BF16)
        return 0

    lax.fori_loop(0, 2 * model_size, weight_grads, 0)


def attn_backward(x, gres, w_a, qkv, ctx, lse, own):
    rows, seq, dim = x.shape
    model_size = w_a.shape[0]
    group_dim = dim // model_size
    return pl.pallas_call(
        attn_backward_kernel,
        out_shape=(
            jax.ShapeDtypeStruct((rows, seq, dim), BF16),
            jax.ShapeDtypeStruct((model_size, dim, 4 * group_dim), BF16),
            jax.ShapeDtypeStruct((model_size, 8, 3 * group_dim), F32),
        ),
        scratch_shapes=[
            pltpu.VMEM((seq, seq), F32),
            pltpu.VMEM((seq, dim), F32),
            pltpu.VMEM((rows, model_size, 3 * group_dim, seq), BF16),
            pltpu.VMEM((dim, rows * seq), BF16),
            pltpu.VMEM((dim, rows * seq), BF16),
            pltpu.VMEM((2, seq, seq), BF16),
            pltpu.VMEM((2, seq, seq), BF16),
        ],
        compiler_params=pltpu.CompilerParams(vmem_limit_bytes=VMEM_MOST),
        name="attn_backward",
    )(x, gres, w_a, qkv, ctx, lse, own)
def slot_of_rows(exit_ref, target_ref, depth):
    count = exit_ref.shape[0]
    flat = []
    for i in range(count):
        rank = 0
        for h in range(i):
            rank = rank + jnp.where(target_ref[h] == target_ref[i], 1 - exit_ref[h], 0)
        flat.append(jnp.where(exit_ref[i] == 0, target_ref[i] * depth + rank, -1))
    return flat


def pick_of_slots(tag_ref, depth, flag_at, capacity):
    seen = jnp.zeros((1, 1), F32)
    picks = []
    for k in range(tag_ref.shape[0] * depth):
        live = tag_ref[k // depth, k % depth : k % depth + 1, flag_at : flag_at + 1]
        picks.append([jnp.where(seen == float(c), live, 0.0) for c in range(min(capacity, k + 1))])
        seen = seen + live
    return picks


def slots_of_tags(tag_ref, depth, flag_at, capacity):
    seen, slots = 0, []
    for k in range(tag_ref.shape[0] * depth):
        cell = tag_ref[k // depth, k % depth : k % depth + 1, flag_at : flag_at + 1]
        live = jnp.where(jnp.sum(cell) > 0.5, 1, 0)
        slots.append((jnp.minimum(seen, capacity - 1), live))
        seen = seen + live
    return slots


TOKENS = 32
CUTS = 3


def enter_kernel(
    depth, pairs,
    exit_ref, target_ref, rows_ref, seg_ref, lab_ref, wt_ref, wqkv_ref, wout_ref, bqv_ref, bup_ref, bout_ref,
    wb_loc, wc_loc,
    own_ref, got_tags_ref, vecs_ref, x_out, wa_out, wb_ref, early_ref,
    qkv_ref, ctx_ref, lse_ref, xhat_ref, rstd_ref,
    tags_ref, vec_ref, wa_loc, slot_ref, part_ref, x_ref, wa_ref, tag_ref, taggot_ref, taglocal_ref, vecgot_ref,
    mask_ref, acc_ref, wsend, wrecv, rsend, rrecv, local_sem, *got_refs,
):
    row_count, token_part, dim = rows_ref.shape
    own_rows, seq = x_ref.shape[:2]
    model_size = wa_ref.shape[0]
    batch_size = taggot_ref.shape[0]
    capacity = own_rows * model_size
    group_dim = wout_ref.shape[0]
    flag_at = 2 * pairs
    head = tag_ref.shape[2] - seq
    at = mesh_place()
    b, z = at["b"], at["z"]
    gathers = [
        Gather(at, model_size, home, spot, wsend.at[k], wrecv.at[k])
        for k, (home, spot) in enumerate(((wa_loc, wa_ref), (wb_loc, wb_ref)))
    ]
    first_gather, second_gather = gathers
    third_gather = Gather(at, model_size, wc_loc, None, wsend.at[2], wrecv.at[2], early_ref)
    vec_first = (CUTS + 1) * batch_size + CUTS * model_size

    def vec_copies():
        return [
            remote(vec_ref, vecgot_ref.at[z], rsend.at[vec_first + i], rrecv.at[vec_first + i],
                   {"mp": (z + i) % model_size})
            for i in range(1, model_size)
        ]

    wide = dim // CUTS

    def batch_copies(cut):
        columns = pl.ds(cut * wide, wide)
        copies = []
        for j in range(1, batch_size):
            t = (b + j) % batch_size
            n = cut * batch_size + j
            copies.append(remote(slot_ref.at[pl.ds(t * depth, depth), :, columns],
                                 got_refs[cut].at[pl.ds(b * depth, depth)],
                                 rsend.at[n], rrecv.at[n], {"batch": t}))
            if cut == 0:
                n = CUTS * batch_size + j
                copies.append(remote(tag_ref.at[t], taggot_ref.at[b], rsend.at[n], rrecv.at[n], {"batch": t}))
        return copies

    mine = pl.ds(pl.multiple_of(z * token_part, 128), token_part)

    def row_copies(cut, r):
        columns = pl.ds(cut * wide, wide)
        first = (CUTS + 1) * (batch_size + model_size) + (cut * own_rows + r) * model_size
        return [
            remote(part_ref.at[(z + i) % model_size * own_rows + r, :, columns], x_ref.at[r, mine, columns],
                   rsend.at[first + i], rrecv.at[first + i], {"mp": (z + i) % model_size})
            for i in range(1, model_size)
        ]

    def local_copies():
        return [
            pltpu.make_async_copy(gather.home, gather.spot.at[z], local_sem.at[k])
            for k, gather in enumerate(gathers)
        ]

    for j in range(3):
        wa_loc[j * group_dim : (j + 1) * group_dim, :] = wqkv_ref[j]
    wa_loc[3 * group_dim :, :] = wout_ref[...]
    vec_ref[...] = jnp.zeros_like(vec_ref)
    vec_ref[0:1, :group_dim] = bqv_ref[0:1]
    vec_ref[0:1, 2 * group_dim : 3 * group_dim] = bqv_ref[1:2]
    vec_ref[1:2] = bup_ref[...].reshape(1, dim)
    greet(at, batch_size, model_size)
    first_gather.start()
    begin(vec_copies())
    begin(local_copies())

    flat = slot_of_rows(exit_ref, target_ref, depth)
    tags_ref[...] = jnp.zeros_like(tags_ref)
    taglocal_ref[0] = jnp.zeros_like(taglocal_ref[0])
    taglocal_ref[0, :pairs, :row_count] = lab_ref[...].astype(F32)
    taglocal_ref[0, pairs : 2 * pairs, :row_count] = wt_ref[...].astype(F32)
    tags_ref[:, : 2 * pairs] = taglocal_ref[0, : 2 * pairs, :128].T[: tags_ref.shape[0]]
    tags_ref[:row_count, flag_at : flag_at + 1] = jnp.ones((row_count, 1), F32)
    tags_ref[:row_count, head:] = seg_ref[...].astype(F32)
    tag_ref[...] = jnp.zeros_like(tag_ref)

    def taken(k):
        hits = [jnp.where(flat[r] == k, 1, 0) for r in range(row_count)]
        return sum(r * hits[r] for r in range(row_count)), sum(hits).astype(F32)

    def fill(t, dst_ref, cut):
        columns = pl.ds(cut * wide, wide)
        for s in range(depth):
            row, there = taken(t * depth + s)
            found = (rows_ref[row, :, columns].astype(F32) * there).astype(BF16)
            if dst_ref is None:
                got_refs[cut][t * depth + s] = found
            else:
                dst_ref[t * depth + s, :, columns] = found

    def fill_tags(t):
        for s in range(depth):
            total = jnp.zeros((1, tags_ref.shape[1]), F32)
            for r in range(row_count):
                total += jnp.where(flat[r] == t * depth + s, 1.0, 0.0) * tags_ref[r : r + 1]
            tag_ref[t, s : s + 1] = total

    for j in range(1, batch_size):
        fill_tags((b + j) % batch_size)
    for cut in range(CUTS):
        for j in range(1, batch_size):
            fill((b + j) % batch_size, slot_ref, cut)
        if cut == 0:
            begin(batch_copies(0))
            fill_tags(b)
            taggot_ref[b] = tag_ref[b]
            fill(b, None, 0)
    for cut in range(1, CUTS):
        fill(b, None, cut)
    arrive(batch_copies(0))
    begin(batch_copies(1))

    picks = pick_of_slots(taggot_ref, depth, flag_at, capacity)

    slots = slots_of_tags(taggot_ref, depth, flag_at, capacity)

    def compact(cut):
        columns = pl.ds(cut * wide, wide)
        for c in range(capacity):
            hits = [jnp.where(place == c, live, 0) for place, live in slots]
            k = sum(n * hits[n] for n in range(c, len(slots)))
            there = sum(hits[c:]).astype(F32)
            part_ref[c, :, columns] = (got_refs[cut][k].astype(F32) * there).astype(BF16)
        begin(row_copies(cut, 0))

    compact(0)
    first_gather.advance(1, 1, 0)
    arrive(batch_copies(1))
    for cut in range(2, CUTS):
        begin(batch_copies(cut))
        compact(cut - 1)
        if cut == 2:
            first_gather.advance(1, 2)
        arrive(batch_copies(cut))
    compact(CUTS - 1)
    first_gather.advance(2, 1, 0, 2)
    second_gather.start()
    for r in range(1, own_rows):
        for cut in range(CUTS):
            begin(row_copies(cut, r))
    for c in range(capacity):
        total = jnp.zeros((1, tags_ref.shape[1]), F32)
        for k in range(c, len(picks)):
            total += picks[k][c] * taggot_ref[k // depth, k % depth : k % depth + 1]
        taglocal_ref[c, 0:1] = total
    for i in range(own_rows):
        x_ref[i, mine] = part_ref[z * own_rows + i]
    own_ref[...] = jnp.zeros_like(own_ref)
    for i in range(own_rows):
        own_ref[i : i + 1] = taglocal_ref[z * own_rows + i, 0:1]
    got_tags_ref[...] = taggot_ref[...]

    first_gather.advance(3, 1, 0, 2)
    arrive(vec_copies())
    vecgot_ref[z] = vec_ref[...]
    vecs_ref[...] = vecgot_ref[...]
    for copy in local_copies():
        copy.wait()
    keep = [
        pltpu.make_async_copy(x_ref, x_out, local_sem.at[3]),
        pltpu.make_async_copy(wa_ref, wa_out, local_sem.at[4]),
    ]

    def rows_here(r):
        for cut in range(CUTS):
            arrive(row_copies(cut, r))

    rows_here(0)
    seg_rows = own_ref[:, head:]
    seg_cols = seg_rows.T
    def forward_early():
        arrive(third_gather.early_copies(0))
        begin(third_gather.early_copies(1))

    late = {
        (0, 1): ((first_gather.done, 1),),
        (0, 2): ((first_gather.done, 0), (second_gather.advance, 1, 1, 0)),
        (0, 3): ((first_gather.done, 2), (second_gather.advance, 1, 2)),
        (1, 0): ((second_gather.advance, 2, 2),),
        (1, 1): ((second_gather.advance, 3, 1, 0),),
        (1, 2): ((second_gather.advance, 3, 2), (forward_early,)),
    }

    for r in range(own_rows):
        if r == 1:
            second_gather.advance(2, 1, 0)
            begin(third_gather.early_copies(0))
            for n in range(1, own_rows):
                rows_here(n)
            begin(keep)
        mask_ref[...] = jnp.where(seg_cols[:, r : r + 1] == seg_rows[r : r + 1], 0.0, NEG)
        acc_ref[...] = jnp.zeros_like(acc_ref)

        def one_group(i, _):
            m = chunk_of(at, model_size - 1 - i)
            for step in range(model_size):
                if (r, step) in late:
                    @pl.when(i == step)
                    def _():
                        for action, *args in late[r, step]:
                            action(*args)

            bias = vecgot_ref[m].T[: 3 * group_dim, 0:1]
            low = (mm(wa_ref[m, : 3 * group_dim, :], x_ref[r], NT) + bias).astype(BF16)
            qkv_ref[r, m] = low
            for j in range(group_dim // HEAD_DIM):
                rows = slice(j * HEAD_DIM, (j + 1) * HEAD_DIM)
                q_t = low[rows] * HEAD_DIM ** (-0.5)
                k_t = low[group_dim + rows.start : group_dim + rows.stop]
                v_t = low[2 * group_dim + rows.start : 2 * group_dim + rows.stop]
                scores = mm(k_t, q_t, TN) + mask_ref[...]
                top = jnp.max(scores, axis=0, keepdims=True)
                terms = jnp.exp(scores - top)
                total = jnp.sum(terms, axis=0, keepdims=True)
                ctx_t = mm(v_t, terms.astype(BF16)) / total
                ctx_ref[r, m, rows, :] = ctx_t.astype(BF16)
                lse_ref[r, m, j : j + 1, :] = top + jnp.log(total)
            acc_ref[...] += mm(ctx_ref[r, m], wa_ref[m, 3 * group_dim :, :], TN)
            return 0

        lax.fori_loop(0, model_size, one_group, 0)
        xhat, rstd = norm_parts(x_ref[r].astype(F32) + (acc_ref[...] + bout_ref[...].reshape(1, dim)))
        xhat_ref[r] = xhat
        rstd_ref[r] = rstd

    second_gather.done(0, 1, 2)
    arrive(third_gather.early_copies(1))
    for copy in keep:
        copy.wait()
    for gather in gathers:
        gather.sent()
    sent(third_gather.early_copies(0) + third_gather.early_copies(1))
    sent(vec_copies())
    for cut in range(CUTS):
        sent(batch_copies(cut))
        for r in range(own_rows):
            sent(row_copies(cut, r))


def enter(exit_flag, target, rows_in, seg, labels, weights, w_qkv, w_out, b_qv, b_up, b_out, w_b, w_c,
          own_rows, batch_size, model_size):
    row_count, token_part, dim = rows_in.shape
    seq = token_part * model_size
    capacity = own_rows * model_size
    depth = (capacity + batch_size - 1) // batch_size
    group_dim = dim // model_size
    pairs = labels.shape[1]
    tag_wide = 128 + seq
    smem = pl.BlockSpec(memory_space=pltpu.SMEM)
    vmem = pl.BlockSpec(memory_space=pltpu.VMEM)
    hbm = pl.BlockSpec(memory_space=pl.ANY)
    full = jax.ShapeDtypeStruct((model_size, dim, dim), BF16)
    f32 = lambda *shape: jax.ShapeDtypeStruct(shape, F32)
    low = lambda *shape: jax.ShapeDtypeStruct(shape, BF16)
    moves = (CUTS + 1) * (batch_size + model_size) + CUTS * own_rows * model_size
    return pl.pallas_call(
        functools.partial(enter_kernel, depth, pairs),
        in_specs=[smem, smem] + [vmem] * 9 + [hbm, hbm],
        out_specs=[vmem, vmem, vmem, hbm, hbm, hbm, hbm] + [vmem] * 5,
        out_shape=(
            f32(8, tag_wide),
            f32(batch_size, 8, tag_wide),
            f32(model_size, 8, dim),
            low(own_rows, seq, dim),
            full,
            full,
            low(3, 2, dim // 16, dim),
            low(own_rows, model_size, 3 * group_dim, seq),
            low(own_rows, model_size, group_dim, seq),
            f32(own_rows, model_size, group_dim // HEAD_DIM, seq),
            f32(own_rows, seq, dim),
            f32(own_rows, seq, 1),
        ),
        scratch_shapes=[
            pltpu.VMEM((-(-row_count // 8) * 8, tag_wide), F32),
            pltpu.VMEM((8, dim), F32),
            pltpu.VMEM((dim, dim), BF16),
            pltpu.VMEM((batch_size * depth, token_part, dim), BF16),
            pltpu.VMEM((capacity, token_part, dim), BF16),
            pltpu.VMEM((own_rows, seq, dim), BF16),
            pltpu.VMEM((model_size, dim, dim), BF16),
            pltpu.VMEM((batch_size, 8, tag_wide), F32),
            pltpu.VMEM((batch_size, 8, tag_wide), F32),
            pltpu.VMEM((capacity, 8, tag_wide), F32),
            pltpu.VMEM((model_size, 8, dim), F32),
            pltpu.VMEM((seq, seq), F32),
            pltpu.VMEM((seq, dim), F32),
            pltpu.SemaphoreType.DMA((3, GATHER_SEMS)),
            pltpu.SemaphoreType.DMA((3, GATHER_SEMS)),
            pltpu.SemaphoreType.DMA((moves,)),
            pltpu.SemaphoreType.DMA((moves,)),
            pltpu.SemaphoreType.DMA((5,)),
            *[pltpu.VMEM((batch_size * depth, token_part, dim // CUTS), BF16) for _ in range(CUTS)],
        ],
        compiler_params=pltpu.CompilerParams(
            vmem_limit_bytes=VMEM_MOST, collective_id=0, has_side_effects=True
        ),
        name="enter",
    )(
        exit_flag, target, rows_in, seg, labels.T, weights.T, jnp.transpose(w_qkv, (0, 2, 1)), w_out, b_qv, b_up, b_out,
        w_b, w_c,
    )


def leave_kernel(
    depth, pairs,
    tags_ref, own_ref, x_hbm, gres_hbm, wa_hbm, qkv_hbm, ctx_hbm, lse_ref,
    dwb_hbm, ownc_ref, hand_ref, pack_ref,
    back_got, mats_ref, sums_ref, bias_ref,
    x_ref, wa_ref, ctx_ref, work_ref, acc_ref, mask_ref, p_ref, s_ref, xflip_ref, gflip_ref, dx_ref, dwa_ref,
    own_half, *rest,
):
    parts_a, parts_b, parts_c, rest = rest[:7], rest[7:14], rest[14:19], rest[19:]
    (
        small_acc, small_got, small_z, bias_acc, bias_row, bias_got, bias_z, back_ref,
        msend, mrecv, ssend, srecv, bsend, brecv, rsend, rrecv, local_sem, *mine_refs,
    ) = rest
    row_count, seq, dim = x_ref.shape
    model_size = wa_ref.shape[0]
    batch_size = tags_ref.shape[0]
    group_dim = ctx_ref.shape[2]
    token_part = seq // model_size
    capacity = row_count * model_size
    others = model_size - 1
    at = mesh_place()
    b, z, lo, hi = at["b"], at["z"], at["lo"], at["hi"]
    far, twin, side = at["far"], at["twin"], at["side"]

    def shard(i):
        return {"mp": (z + i) % model_size}

    first = Reduce(at, model_size, dwb_hbm, own_half, *parts_b, mats_ref.at[1], msend.at[1], mrecv.at[1], 0, True)
    second = Reduce(at, model_size, dwa_ref, dwa_ref.at[:, :, lo], *parts_a, mats_ref.at[0], msend.at[0], mrecv.at[0], 2, True)
    third = Finish(at, model_size, ownc_ref, hand_ref, *parts_c, mats_ref.at[2], msend.at[2], mrecv.at[2])

    def small_copies(stage):
        def one(slot, src, dst, device):
            return remote(src, dst, ssend.at[slot], srecv.at[slot], device)

        if stage == 0:
            return [one(0, pack_ref.at[1 - lo], small_got.at[0], twin)]
        if stage < 3:
            return [one(stage, small_acc.at[stage - 1], small_got.at[stage], (far, side)[stage - 1])]
        if stage == 3:
            return [
                one(2 + i, small_acc.at[2, (z + i) % model_size], small_z.at[i - 1], shard(i))
                for i in range(1, model_size)
            ]
        if stage == 4:
            return [
                one(2 + others + i, sums_ref.at[lo, z], sums_ref.at[lo, z], shard(i))
                for i in range(1, model_size)
            ]
        return [one(3 + 2 * others, sums_ref.at[lo], sums_ref.at[lo], twin)]

    def bias_copies(stage):
        def one(slot, src, dst, device):
            return remote(src, dst, bsend.at[slot], brecv.at[slot], device)

        if stage < 3:
            return [one(stage, bias_row.at[stage], bias_got.at[stage], (twin, far, side)[stage])]
        return [one(2 + i, bias_row.at[3], bias_z.at[i - 1], shard(i)) for i in range(1, model_size)]

    wide = dim // CUTS

    def row_copies(r, cut):
        columns = pl.ds(cut * wide, wide)
        first = (r * CUTS + cut) * others - 1
        return [
            remote(
                dx_ref.at[r, pl.ds(pl.multiple_of((z + i) % model_size * token_part, 128), token_part), columns],
                mine_refs[cut].at[z * row_count + r],
                rsend.at[first + i], rrecv.at[first + i], shard(i),
            )
            for i in range(1, model_size)
        ]

    def batch_copies(cut):
        columns = pl.ds(cut * wide, wide)
        first = row_count * CUTS * others + cut * (batch_size - 1) - 1
        copies = []
        for j in range(1, batch_size):
            t = (b + j) % batch_size
            copies.append(remote(
                back_ref.at[pl.ds(t * depth, depth), :, columns],
                back_got.at[pl.ds(b * depth, depth), :, columns],
                rsend.at[first + j], rrecv.at[first + j], {"batch": t},
            ))
        return copies

    def local_copies():
        return [
            pltpu.make_async_copy(dwb_hbm.at[:, :, lo], own_half, local_sem.at[0]),
        ]

    def inputs():
        return [
            pltpu.make_async_copy(qkv_hbm, work_ref, local_sem.at[2]),
            pltpu.make_async_copy(gres_hbm, acc_ref, local_sem.at[3]),
            pltpu.make_async_copy(x_hbm, x_ref, local_sem.at[4]),
            pltpu.make_async_copy(wa_hbm, wa_ref, local_sem.at[5]),
            pltpu.make_async_copy(ctx_hbm, ctx_ref, local_sem.at[6]),
        ]

    def small_step(stage):
        arrive(small_copies(stage))
        if stage == 0:
            small_acc[0] = pack_ref[lo] + small_got[0]
        if stage in (1, 2):
            small_acc[stage] = small_acc[stage - 1] + small_got[stage]
        if stage == 3:
            total = small_acc[2, z].astype(F32)
            for i in range(others):
                total += small_z[i].astype(F32)
            sums_ref[lo, z] = total.astype(BF16)
        if stage < 5:
            begin(small_copies(stage + 1))

    def bias_step(stage):
        arrive(bias_copies(stage))
        if stage < 3:
            bias_row[stage + 1] = bias_row[stage] + bias_got[stage]
            begin(bias_copies(stage + 1))
        else:
            total = bias_row[3]
            for i in range(others):
                total += bias_z[i]
            own = sum(jnp.where(z == m, 1.0, 0.0) * total[m : m + 1] for m in range(model_size))
            bias_ref[...] = jnp.broadcast_to(own, bias_ref.shape)

    begin(inputs())
    begin(local_copies())
    greet(at, batch_size, model_size)
    begin(small_copies(0))
    third.start()
    for i in range(model_size):
        first.start(i)
    seg_rows = own_ref[:, own_ref.shape[1] - seq :]
    seg_cols = seg_rows.T
    for copy in inputs() + local_copies():
        copy.wait()

    steps = {
        0: [],
        1: [(small_step, 0), (third.after_one,)],
        2: [(first.after_core, 0)],
        3: [(first.after_core, 1), (small_step, 1), (third.after_two,)],
        4: [(first.after_one, 0), (small_step, 2)],
        5: [(first.after_core, 2), (first.after_one, 1), (first.after_two, 0), (small_step, 3)],
        6: [(first.after_core, 3), (first.after_two, 1), (small_step, 4)],
        7: [(first.after_one, 2), (second.after_core, 0)],
    }

    def weight_grads(i):
        m, rows_y = chunk_of(at, i), dim // 2

        def one(y, _):
            part = pl.ds(pl.multiple_of(y * rows_y, 128), rows_y)
            left, right = 0.0, 0.0
            for q in range(row_count):
                cols = slice(q * seq, (q + 1) * seq)
                left += mm(xflip_ref[part, cols], work_ref[q, m], NT)
                right += mm(gflip_ref[part, cols], ctx_ref[q, m], NT)
            shape = dwa_ref.shape[2:-1]
            dwa_ref[m, y, :, :, :, :, : 3 * group_dim] = left.astype(BF16).reshape(*shape, 3 * group_dim)
            dwa_ref[m, y, :, :, :, :, 3 * group_dim :] = right.astype(BF16).reshape(*shape, group_dim)
            return 0

        lax.fori_loop(0, 2, one, 0)

    for r in range(row_count):
        mask_ref[...] = jnp.where(seg_cols[:, r : r + 1] == seg_rows[r : r + 1], 0.0, NEG)
        grad_low = acc_ref[r].astype(BF16)
        columns = slice(r * seq, (r + 1) * seq)
        gflip_ref[:, columns] = grad_low.T
        xflip_ref[:, columns] = x_ref[r].T

        def one_group(i, _):
            if r == row_count - 1:
                @pl.when(i > 0)
                def _():
                    weight_grads(i - 1)

            for step in range(model_size):
                @pl.when(i == step)
                def _():
                    if r == row_count - 1 and step > 0:
                        second.start(step - 1)
                    for action, *args in steps[r * model_size + step]:
                        action(*args)

            m = chunk_of(at, i)
            grad_ctx = mm(wa_ref[m, 3 * group_dim :, :], grad_low, NT).astype(BF16)

            def store(rows, value):
                work_ref[r, m, rows, :] = value

            backward_group(
                grad_ctx, lambda rows: ctx_ref[r, m, rows, :], lambda rows: work_ref[r, m, rows, :], store,
                mask_ref, lambda j: lse_ref[r, m, j : j + 1, :], group_dim, p_ref, s_ref,
            )
            grads = work_ref[r, m]
            found = mm(jnp.ones((8, seq), BF16), grads, NT)
            if r == 0:
                bias_acc[m] = found
            else:
                bias_acc[m] = bias_acc[m] + found
            acc_ref[r] = acc_ref[r] + mm(grads, wa_ref[m, : 3 * group_dim, :], TN)
            return 0

        lax.fori_loop(0, model_size, one_group, 0)
        dx_ref[r] = acc_ref[r].astype(BF16)
        for cut in range(CUTS if r < row_count - 1 else 2):
            begin(row_copies(r, cut))

    weight_grads(model_size - 1)
    second.start(model_size - 1)
    for r in range(row_count):
        for cut in range(CUTS):
            part = pl.ds(pl.multiple_of(z * token_part, 128), token_part)
            mine_refs[cut][z * row_count + r] = dx_ref[r, part, cut * wide : (cut + 1) * wide]
    first.after_one(3)
    second.after_core(1)
    slots = slots_of_tags(tags_ref, depth, 2 * pairs, capacity)

    def give(cut):
        columns = pl.ds(cut * wide, wide)
        for k, (place, live) in enumerate(slots):
            found = mine_refs[cut][place].astype(F32) * live.astype(F32)
            back_ref[k, :, columns] = found.astype(BF16)
        begin(batch_copies(cut))

    def returned(cut):
        for r in range(row_count):
            arrive(row_copies(r, cut))
        if cut + 2 < CUTS:
            begin(row_copies(row_count - 1, cut + 2))
        give(cut)

    returned(0)
    first.after_two(2)
    second.after_one(0)
    second.after_core(2)
    returned(1)
    bias_row[0] = jnp.zeros_like(bias_row[0])
    for m in range(model_size):
        bias_row[0, m : m + 1] = bias_acc[m, 0:1]
    begin(bias_copies(0))
    first.after_two(3)
    second.after_core(3)
    second.after_one(1)
    returned(2)
    second.after_two(0)
    own_slots = pl.ds(b * depth, depth)
    back_got[own_slots] = back_ref[own_slots]
    second.after_two(1)
    second.after_one(2)
    bias_step(0)
    first.after_three()
    second.after_two(2)
    second.after_one(3)
    bias_step(1)
    small_step(5)
    third.done()
    second.after_two(3)
    bias_step(2)
    second.after_three()
    bias_step(3)
    for cut in range(CUTS):
        arrive(batch_copies(cut))

    for reducer in (first, second):
        reducer.done()
        reducer.sent()
    third.sent()
    for stage in range(6):
        sent(small_copies(stage))
    for stage in range(4):
        sent(bias_copies(stage))
    for cut in range(CUTS):
        for r in range(row_count):
            sent(row_copies(r, cut))
        sent(batch_copies(cut))


def leave(tags, own, x, gres, w_a, qkv, ctx, lse, d_wb, mat_c, hand, pack, batch_size, pairs):
    rows, seq, dim = x.shape
    model_size = w_a.shape[0]
    group_dim = dim // model_size
    token_part = seq // model_size
    capacity = rows * model_size
    depth = (capacity + batch_size - 1) // batch_size
    slots = batch_size * depth
    piece = dim // 16
    others = model_size - 1
    grid_shape = (model_size, 2, 2, PARTS, 2, piece, dim)
    pack_shape = (2, model_size, pack.shape[0] // (2 * model_size), pack.shape[1])
    vmem = pl.BlockSpec(memory_space=pltpu.VMEM)
    hbm = pl.BlockSpec(memory_space=pl.ANY)
    dma = pltpu.SemaphoreType.DMA
    low = lambda *shape: pltpu.VMEM(shape, BF16)
    f32 = lambda *shape: pltpu.VMEM(shape, F32)
    row_moves = CUTS * (rows * others + batch_size - 1)
    return pl.pallas_call(
        functools.partial(leave_kernel, depth, pairs),
        in_specs=[vmem, vmem, hbm, hbm, hbm, hbm, hbm, vmem, hbm, vmem, vmem, vmem],
        out_specs=[vmem, vmem, vmem, vmem],
        out_shape=(
            jax.ShapeDtypeStruct((slots, token_part, dim), BF16),
            jax.ShapeDtypeStruct((3,) + grid_shape[2:], BF16),
            jax.ShapeDtypeStruct(pack_shape, BF16),
            jax.ShapeDtypeStruct((8, 3 * group_dim), F32),
        ),
        scratch_shapes=[
            low(rows, seq, dim),
            low(model_size, dim, dim),
            low(rows, model_size, group_dim, seq),
            low(rows, model_size, 3 * group_dim, seq),
            f32(rows, seq, dim),
            f32(seq, seq),
            low(2, seq, seq),
            low(2, seq, seq),
            low(dim, rows * seq),
            low(dim, rows * seq),
            low(rows, seq, dim),
            low(*grid_shape),
            low(model_size, 2, PARTS, 2, piece, dim),
            *reduce_scratch(model_size, piece, dim),
            *reduce_scratch(model_size, piece, dim),
            low(2, piece, dim),
            low(2, piece, dim),
            low(piece, dim),
            low(piece, dim),
            low(PARTS, piece, dim),
            low(3, *pack_shape[1:]),
            low(3, *pack_shape[1:]),
            low(others, *pack_shape[2:]),
            f32(model_size, 8, 3 * group_dim),
            f32(4, 8, 3 * group_dim),
            f32(3, 8, 3 * group_dim),
            f32(others, 8, 3 * group_dim),
            low(slots, token_part, dim),
            dma((3, REDUCE_SEMS)),
            dma((3, REDUCE_SEMS)),
            dma((4 + 2 * others,)),
            dma((4 + 2 * others,)),
            dma((3 + others,)),
            dma((3 + others,)),
            dma((row_moves,)),
            dma((row_moves,)),
            dma((7,)),
            *[low(capacity, token_part, dim // CUTS) for _ in range(CUTS)],
        ],
        compiler_params=pltpu.CompilerParams(
            vmem_limit_bytes=VMEM_MOST, collective_id=2, has_side_effects=True
        ),
        name="leave",
    )(
        tags, own, x, gres, w_a, qkv, ctx, lse,
        d_wb.reshape(grid_shape), mat_c, hand, pack.reshape(pack_shape),
    )


def finish_kernel(
    classes, depth, mats_ref, low_ref, bias_ref, *rest
):
    rows_in, rest = rest[: len(rest) - 18 + (1 if depth is None else 0)], rest[len(rest) - 18 + (1 if depth is None else 0) :]
    (
        gqkv_ref, gbqv_ref, gout_ref, gbout_ref, ggain_ref, gshift_ref, gup_ref, gbup_ref, gdown_ref, gbdown_ref,
        gsw1_ref, gsbias_ref, gquery_ref, gsw2_ref, gsw3_ref, gsb3_ref, *rows_out, sums_ref,
    ) = rest
    if depth is not None:
        exit_ref, target_ref, back_ref = rows_in
        flat = slot_of_rows(exit_ref, target_ref, depth)
        for r in range(rows_out[0].shape[0]):
            k = jnp.minimum(jnp.maximum(flat[r], 0), back_ref.shape[0] - 1)
            alive = jnp.where(flat[r] >= 0, 1.0, 0.0)
            rows_out[0][r] = (back_ref[k].astype(F32) * alive).astype(BF16)
    sums_ref[...] = low_ref[...].astype(F32)
    dim, width = gsw1_ref.shape
    group_dim = gout_ref.shape[0]
    b, z = lax.axis_index("batch"), lax.axis_index("mp")
    w2_at, w3_at, small_at, vec_at, bup_at = pack_places(dim, width)
    blocks = dim // width

    def vector(first, row):
        return jnp.concatenate([sums_ref[first + j * 8 + row : first + j * 8 + row + 1] for j in range(blocks)], axis=1)

    def share(value, parts):
        size = value.shape[1] // parts
        return sum(jnp.where(b == i, 1.0, 0.0) * value[:, i * size : (i + 1) * size] for i in range(parts))

    parts = dim // gbup_ref.shape[-1]
    flipped = mats_ref[0].astype(F32).T
    for j in range(3):
        gqkv_ref[j] = flipped[j * group_dim : (j + 1) * group_dim]
    gout_ref[...] = flipped[3 * group_dim :]
    gup_ref[...] = mats_ref[1].astype(F32)
    gdown_ref[...] = mats_ref[2].astype(F32).T
    for n in range(2):
        gbqv_ref[n : n + 1] = share(bias_ref[0:1, 2 * n * group_dim : (2 * n + 1) * group_dim], parts)
    gbout_ref[...] = (vector(vec_at.start, 5)).reshape(dim)
    for n in range(2):
        ggain_ref[n : n + 1] = vector(vec_at.start, n)
        gshift_ref[n : n + 1] = vector(vec_at.start, 2 + n)
    gbdown_ref[...] = (vector(vec_at.start, 4)).reshape(dim)
    ups = [vector(bup_at.start, m) for m in range(dim // group_dim)]
    gbup_ref[...] = (share(sum(jnp.where(z == m, 1.0, 0.0) * ups[m] for m in range(len(ups))), parts)).reshape(gbup_ref.shape[0])
    for j in range(blocks):
        gsw1_ref[j * width : (j + 1) * width] = sums_ref[j * width : (j + 1) * width].T
    gsbias_ref[...] = sums_ref[small_at.start : small_at.start + 2]
    gquery_ref[...] = (sums_ref[small_at.start + 2 : small_at.start + 3]).reshape(width)
    gsb3_ref[...] = (sums_ref[small_at.start + 3 : small_at.start + 4][:, :classes]).reshape(classes)
    gsw2_ref[...] = sums_ref[w2_at]
    gsw3_ref[...] = sums_ref[w3_at][:classes]


def finish(mats, sums, bias, model_size, classes, rows, slot_depth):
    depth, dim = mats.shape[1:]
    width = sums.shape[1]
    group_dim = dim // model_size
    batch_size = dim // depth
    f32 = lambda *shape: jax.ShapeDtypeStruct(shape, F32)
    smem, vmem = pl.BlockSpec(memory_space=pltpu.SMEM), pl.BlockSpec(memory_space=pltpu.VMEM)
    row_shapes = ()
    if rows:
        row_shapes = (jax.ShapeDtypeStruct((rows[0].shape[0],) + rows[2].shape[1:], BF16),)
    return pl.pallas_call(
        functools.partial(finish_kernel, classes, slot_depth if rows else None),
        in_specs=[vmem] * 3 + ([smem, smem, vmem] if rows else []),
        out_specs=[vmem] * (16 + len(row_shapes)),
        out_shape=(
            f32(3, group_dim, depth),
            f32(2, group_dim // batch_size),
            f32(group_dim, depth),
            f32(dim),
            f32(2, dim),
            f32(2, dim),
            f32(depth, dim),
            f32(depth),
            f32(dim, depth),
            f32(dim),
            f32(dim, width),
            f32(2, width),
            f32(width),
            f32(width, width),
            f32(classes, width),
            f32(classes),
            *row_shapes,
        ),
        scratch_shapes=[pltpu.VMEM(sums.shape, F32)],
        compiler_params=pltpu.CompilerParams(vmem_limit_bytes=VMEM_MOST),
        name="finish",
    )(mats, sums, bias, *rows)


def rows_back(grad_x, exit_flag, target, live, slot_depth):
    batch_size, model_size = lax.axis_size("batch"), lax.axis_size("mp")
    own_rows, seq, dim = grad_x.shape
    row_count = exit_flag.shape[0]
    capacity, slot_count = own_rows * model_size, batch_size * slot_depth
    alive_rows = 1 - exit_flag > 0
    same_goal = (target[:, None] == target[None, :]) & alive_rows[:, None] & alive_rows[None, :]
    row_order = jnp.arange(row_count, dtype=jnp.int32)
    slot_in = jnp.sum(
        (same_goal & (row_order[None, :] < row_order[:, None])).astype(jnp.int32), axis=1
    )
    flat_slot = target * slot_depth + slot_in
    send_low = (
        (jnp.arange(slot_count, dtype=jnp.int32)[:, None] == flat_slot[None, :]) & alive_rows[None, :]
    ).astype(BF16)
    live_flat = live.reshape(-1)
    position = jnp.cumsum(live_flat.astype(jnp.int32)) - 1
    pick_low = (
        (jnp.arange(capacity, dtype=jnp.int32)[:, None] == position[None, :]) & (live_flat[None, :] > 0)
    ).astype(BF16)
    mine = lax.all_to_all(grad_x, "mp", split_axis=1, concat_axis=0, tiled=True)
    back = jnp.einsum("ck,csd->ksd", pick_low, mine, preferred_element_type=F32).astype(BF16)
    back = back.reshape((batch_size, slot_depth) + back.shape[1:])
    got = lax.all_to_all(back, "batch", split_axis=0, concat_axis=0, tiled=True)
    got = got.reshape((slot_count,) + got.shape[2:])
    return jnp.einsum("kr,ksd->rsd", send_low, got, preferred_element_type=F32).astype(BF16)


def matrix_sums(grads):
    sums = []
    for grad in grads:
        part = lax.psum_scatter(grad, "mp", scatter_dimension=0, tiled=True)[0]
        part = lax.psum_scatter(part, "batch", scatter_dimension=0, tiled=True)
        sums.append(lax.psum(part, "grp"))
    return sums


def on_device(
    rows_in, segment_ids, pair_labels, pair_mask, exit_flag, target, cot_out,
    w_qkv, b_qv, w_out, b_out, ln_gain, ln_bias, w_up, b_up, w_down, b_down,
    s_w1, s_bias, s_query, s_w2, s_w3, s_b3,
):
    batch_size = lax.axis_size("batch")
    model_size = lax.axis_size("mp")
    row_count, _, model_dim = rows_in.shape
    own_rows = cot_out.shape[0]
    capacity = own_rows * model_size
    slot_depth = (capacity + batch_size - 1) // batch_size
    pair_count = pair_labels.shape[1]
    my_mp = lax.axis_index("mp")
    own, got_tags, vecs, rows_own, w_a, w_b, early, qkv, ctx, lse, xhat_one, rstd_one = enter(
        exit_flag, target, rows_in, segment_ids, pair_labels, pair_mask, w_qkv, w_out, b_qv, b_up, b_out,
        w_up, w_down, own_rows, batch_size, model_size,
    )
    scatter = batch_size == 2
    mixed_out, grad_resid, d_wb, mat_c, hand, pack = ffn_both(
        xhat_one, rstd_one, ln_gain, ln_bias, w_b, w_down, early, vecs, b_down, cot_out, own, pair_count, scatter,
        s_w1, s_bias, s_query, s_w2, s_w3, s_b3,
    )
    if scatter:
        back, mats, sums, bias_sum = leave(
            got_tags, own, rows_own, grad_resid, w_a, qkv, ctx, lse, d_wb, mat_c, hand, pack,
            batch_size, pair_count,
        )
        mats = mats.reshape(3, model_dim // batch_size, model_dim)
        sums = sums.reshape(pack.shape)
    else:
        grad_x, d_wa, bias_part = attn_backward(rows_own, grad_resid, w_a, qkv, ctx, lse, own)
        grad_rows = rows_back(grad_x, exit_flag, target, got_tags[:, :slot_depth, 2 * pair_count], slot_depth)
        whole = (model_size, model_dim, model_dim)
        mats = matrix_sums((d_wa, d_wb.reshape(whole), mat_c.reshape(whole)))
        sums, bias_sum = lax.psum((pack.astype(F32), bias_part[:, 0]), ("grp", "batch", "mp"))
        bias_sum = lax.dynamic_index_in_dim(bias_sum, my_mp, 0)
        mats = jnp.stack(mats)

    (
        g_wqkv, g_bqv, g_wout, g_bout, g_gain, g_shift, g_wup, g_bup, g_wdown, g_bdown,
        g_sw1, g_sbias, g_query, g_sw2, g_sw3, g_sb3, *rows_found,
    ) = finish(
        mats, sums, bias_sum, model_size, s_w3.shape[1], (exit_flag, target, back) if scatter else (), slot_depth
    )
    if scatter:
        grad_rows = rows_found[0]
    return (
        mixed_out, grad_rows, jnp.transpose(g_wqkv, (0, 2, 1)), g_bqv, g_wout, g_bout, g_gain, g_shift, g_wup,
        g_bup, g_wdown, g_bdown, g_sw1, g_sbias, g_query, g_sw2, g_sw3.T, g_sb3,
    )


def solution(mesh):
    return jax.shard_map(
        on_device,
        mesh=mesh,
        in_specs=(
            P(("grp", "batch"), "mp", None),
            P(("grp", "batch"), None),
            P(("grp", "batch"), None),
            P(("grp", "batch"), None),
            P(("grp", "batch")),
            P(("grp", "batch")),
            P(("grp", "batch", "mp"), None, None),
            P(None, None, "mp"),
            P(None, "mp"),
            P("mp", None),
            P(),
            P(),
            P(),
            P(None, "mp"),
            P("mp"),
            P("mp", None),
            P(),
            P(),
            P(),
            P(),
            P(),
            P(),
            P(),
        ),
        out_specs=(
            P(("grp", "batch", "mp"), None, None),
            P(("grp", "batch"), "mp", None),
            P(None, "batch", "mp"),
            P(None, ("mp", "batch")),
            P("mp", "batch"),
            P(),
            P(),
            P(),
            P("batch", "mp"),
            P(("mp", "batch")),
            P("mp", "batch"),
            P(),
            P(),
            P(),
            P(),
            P(),
            P(),
            P(),
        ),
        check_vma=False,
    )
```

```python
import functools

import jax
import jax.numpy as jnp
from jax import lax
from jax.experimental import pallas as pl
from jax.experimental.pallas import tpu as pltpu
from jax.sharding import PartitionSpec as P

HEAD_DIM = 64
EPS = 1e-12
NEG = -1000000000.0
PRECISE = lax.Precision.HIGHEST
F32 = jnp.float32
BF16 = jnp.bfloat16
BLOCK = 512
VMEM_MOST = 62 * 1024 * 1024
NN = (((1,), (0,)), ((), ()))
NT = (((1,), (1,)), ((), ()))
TN = (((0,), (0,)), ((), ()))


def mm(left, right, dims=NN):
    return lax.dot_general(left, right, dims, preferred_element_type=F32)


def mm_exact(left, right, dims=NN):
    return lax.dot_general(left, right, dims, precision=PRECISE, preferred_element_type=F32)


def norm_parts(resid):
    center = resid - jnp.mean(resid, axis=-1, keepdims=True)
    spread = jnp.mean(center * center, axis=-1, keepdims=True)
    rstd = lax.rsqrt(spread + EPS)
    return center * rstd, rstd


def norm_back(upstream, xhat, rstd, gain):
    scaled = upstream * gain
    mean_u = jnp.mean(scaled, axis=-1, keepdims=True)
    mean_ux = jnp.mean(scaled * xhat, axis=-1, keepdims=True)
    return (scaled - mean_u - xhat * mean_ux) * rstd


def column_sum(value):
    return jnp.sum(value, axis=0, keepdims=True)


def mesh_place():
    g, b, z = lax.axis_index("grp"), lax.axis_index("batch"), lax.axis_index("mp")
    hi, lo, bit = g // 2, g % 2, b % 2
    return dict(
        g=g, b=b, z=z, hi=hi, lo=lo, bit=bit,
        far={"grp": (1 - hi) * 2 + lo}, twin={"grp": hi * 2 + 1 - lo}, side={"batch": b + 1 - 2 * bit},
        far_twin={"grp": (1 - hi) * 2 + 1 - lo},
    )


def remote(src, dst, send_sem, recv_sem, device):
    return pltpu.make_async_remote_copy(
        src_ref=src, dst_ref=dst, send_sem=send_sem, recv_sem=recv_sem,
        device_id=device, device_id_type=pl.DeviceIdType.MESH,
    )


def greet(at, batch_size, model_size):
    barrier = pltpu.get_barrier_semaphore()
    peers = [at["far"], at["twin"]]
    if batch_size > 1:
        peers += [{"batch": (at["b"] + j) % batch_size} for j in range(1, batch_size)]
    else:
        peers += [at["side"]]
    peers += [{"mp": (at["z"] + i) % model_size} for i in range(1, model_size)]
    for peer in peers:
        pl.semaphore_signal(barrier, inc=1, device_id=peer, device_id_type=pl.DeviceIdType.MESH)
    pl.semaphore_wait(barrier, len(peers))


def begin(copies):
    for copy in copies:
        copy.start()


def arrive(copies):
    for copy in copies:
        copy.wait_recv()


def sent(copies):
    for copy in copies:
        copy.wait_send()


class Gather:
    def __init__(self, at, model_size, home, spot, send_sem, recv_sem, early=None):
        self.at, self.home, self.spot, self.early = at, home, spot, early
        self.send_sem, self.recv_sem = send_sem, recv_sem
        z, lo, hi, bit = at["z"], at["lo"], at["hi"], at["bit"]
        self.near = z + 1 - 2 * (z % 2)
        self.cross = (z + 2) % model_size
        self.chunks = (self.near, self.cross, (self.near + 2) % model_size)
        piece = home.shape[0] // 16
        half = pl.multiple_of(lo * (8 * piece), 16)
        self.one_a = pl.ds(pl.multiple_of(half + bit * (2 * piece) + hi * piece, 16), piece)
        self.one_b = pl.ds(pl.multiple_of(half + 4 * piece + hi * (2 * piece) + bit * piece, 16), piece)
        self.two_a = pl.ds(pl.multiple_of(half + bit * (2 * piece), 16), 2 * piece)
        self.two_b = pl.ds(pl.multiple_of(half + 4 * piece + hi * (2 * piece), 16), 2 * piece)
        rows = lambda first, count: pl.ds(pl.multiple_of(half + first * piece, 16), count * piece)
        self.pieces = (
            (self.one_a, self.one_b),
            (rows(bit * 2 + 1 - hi, 1), rows(4 + hi * 2 + 1 - bit, 1)),
            (rows(2 - 2 * bit, 2), rows(6 - 2 * hi, 2)),
        )

    def copies(self, stage, i):
        at, home, spot = self.at, self.home, self.spot

        def one(slot, src, dst, device):
            return remote(src, dst, self.send_sem.at[slot], self.recv_sem.at[slot], device)

        def same(slot, m, rows, device):
            return one(slot, spot.at[m, rows], spot.at[m, rows], device)

        m = self.chunks[i]
        if stage == 0 and i < 2:
            return [
                one(2 * i, home.at[self.one_a], spot.at[at["z"], self.one_a], {"mp": m}),
                one(2 * i + 1, home.at[self.one_b], spot.at[at["z"], self.one_b], {"mp": m}),
            ]
        if stage == 0:
            return [
                same(4, self.cross, self.one_a, {"mp": self.near}),
                same(5, self.cross, self.one_b, {"mp": self.near}),
            ]
        if stage == 1 and self.early is not None:
            return [
                one(6 + 2 * i, self.early.at[i, 0], spot.at[m, self.one_a], at["far"]),
                one(7 + 2 * i, self.early.at[i, 1], spot.at[m, self.one_b], at["side"]),
            ]
        if stage == 1:
            return [same(6 + 2 * i, m, self.one_a, at["far"]), same(7 + 2 * i, m, self.one_b, at["side"])]
        if stage == 2:
            return [same(12 + 2 * i, m, self.two_a, at["side"]), same(13 + 2 * i, m, self.two_b, at["far"])]
        raise ValueError(stage)

    def to_twin(self, stage, i):
        m, twin = self.chunks[i], self.at["twin"]
        source = [self.spot.at[m, rows] for rows in self.pieces[stage]]
        if stage == 0 and self.early is not None:
            source = [self.early.at[i, p] for p in range(2)]
        slot = 18 + 6 * i + 2 * stage
        return [
            remote(src, self.spot.at[m, rows], self.send_sem.at[slot + n], self.recv_sem.at[slot + n], twin)
            for n, (src, rows) in enumerate(zip(source, self.pieces[stage]))
        ]

    def start(self):
        begin(self.copies(0, 1) + self.copies(0, 0))

    def early_copies(self, stage):
        def one(slot, src, dst, device):
            return remote(src, dst, self.send_sem.at[slot], self.recv_sem.at[slot], device)

        if stage == 0:
            return [
                one(2 * i + p, self.home.at[rows], self.early.at[i, p], {"mp": self.chunks[i]})
                for i in (1, 0)
                for p, rows in enumerate((self.one_a, self.one_b))
            ]
        return [one(4 + p, self.early.at[1, p], self.early.at[2, p], {"mp": self.near}) for p in range(2)]

    def own_pieces(self, sem):
        return [
            pltpu.make_async_copy(self.early.at[i, p], self.spot.at[self.chunks[i], rows], sem.at[2 * i + p])
            for i in range(3)
            for p, rows in enumerate((self.one_a, self.one_b))
        ]

    def advance(self, stage, *parts):
        for i in parts:
            arrive(self.copies(stage - 1, i))
            if stage == 1 and i == 1:
                begin(self.copies(0, 2))
            begin((self.copies(stage, i) if stage < 3 else []) + self.to_twin(stage - 1, i))

    def done(self, *parts):
        for i in parts:
            for stage in range(3):
                arrive(self.to_twin(stage, i))

    def sent(self):
        for stage in range(3):
            for i in range(3):
                if stage > 0 or self.early is None:
                    sent(self.copies(stage, i))
                sent(self.to_twin(stage, i))


GATHER_SEMS = 36
PARTS = 2


class Reduce:
    def __init__(self, at, model_size, full, base, got_half, got_a, got_b, got_a2, got_b2, last, got_z, out,
                 send_sem, recv_sem, far_first=0, direct=False):
        self.far_first, self.direct = far_first, direct
        self.at, self.full, self.base, self.got_half = at, full, base, got_half
        self.got_a, self.got_b, self.got_a2, self.got_b2 = got_a, got_b, got_a2, got_b2
        self.last, self.got_z, self.out = last, got_z, out
        self.send_sem, self.recv_sem = send_sem, recv_sem
        z = at["z"]
        self.near, self.cross = z + 1 - 2 * (z % 2), (z + 2) % model_size

    def copies(self, stage, i=0):
        at, base = self.at, self.base
        b, lo, hi = at["b"], at["lo"], at["hi"]

        def one(slot, src, dst, device):
            return remote(src, dst, self.send_sem.at[slot], self.recv_sem.at[slot], device)

        m = chunk_of(at, i)
        if stage == 0:
            return [
                one(25 + 4 * i + 2 * y + p, self.full.at[m, y, 1 - lo, p], self.got_half.at[m, y, p], at["twin"])
                for y in range(2)
                for p in range(PARTS)
            ]
        if stage == 1 and i < self.far_first:
            return [
                one(4 + 2 * i, base.at[m, :, 0, 1 - hi], self.got_a.at[m], at["far"]),
                one(5 + 2 * i, base.at[m, :, 1, 1 - hi], self.got_b.at[m], at["far"]),
            ]
        if stage == 2 and i < self.far_first:
            return [
                one(12 + 2 * i, base.at[m, 1 - b, 0, hi], self.got_a2.at[m], at["side"]),
                one(13 + 2 * i, base.at[m, 1 - b, 1, hi], self.got_b2.at[m], at["side"]),
            ]
        if stage == 1:
            return [
                one(4 + 2 * i, base.at[m, :, 0, 1 - hi], self.got_a.at[m], at["far"]),
                one(5 + 2 * i, base.at[m, 1 - b, 1], self.got_b.at[m], at["side"]),
            ]
        if stage == 2:
            return [
                one(12 + 2 * i, base.at[m, 1 - b, 0, hi], self.got_a2.at[m], at["side"]),
                one(13 + 2 * i, base.at[m, b, 1, 1 - hi], self.got_b2.at[m], at["far"]),
            ]
        if stage == 3:
            device = {"mp": self.cross if i == 2 else self.near}
            return [one(20 + i, self.last.at[m], self.got_z.at[i], device)] if i < 3 else []
        mine = self.out.at[lo, :, hi]
        if stage == 4 and self.direct:
            return [one(23 + 18 * n, mine, mine, at[peer]) for n, peer in enumerate(("far", "twin", "far_twin"))]
        if stage == 4:
            return [one(23, mine, mine, at["far"])]
        if self.direct:
            return []
        return [one(24, self.out.at[lo], self.out.at[lo], at["twin"])]

    def start(self, i):
        begin(self.copies(0, i))

    def after_core(self, i, go_on=True):
        arrive(self.copies(0, i))
        m = chunk_of(self.at, i)

        def one(n, _):
            y, p, h = n // 4, n // 2 % 2, n % 2
            self.base[m, y, p, h] = self.base[m, y, p, h] + self.got_half[m, y, p, h]
            return 0

        lax.fori_loop(0, 8, one, 0)
        if go_on:
            begin(self.copies(1, i))

    def after_one(self, i):
        arrive(self.copies(1, i))
        m, b, hi, base = chunk_of(self.at, i), self.at["b"], self.at["hi"], self.base
        for h in range(2):
            base[m, h, 0, hi] = base[m, h, 0, hi] + self.got_a[m, h]
            if i < self.far_first:
                base[m, h, 1, hi] = base[m, h, 1, hi] + self.got_b[m, h]
            else:
                base[m, b, 1, h] = base[m, b, 1, h] + self.got_b[m, h]
        begin(self.copies(2, i))

    def after_two(self, i, go_on=True):
        arrive(self.copies(2, i))
        m, b, hi, base = chunk_of(self.at, i), self.at["b"], self.at["hi"], self.base
        found = [base[m, b, 0, hi] + self.got_a2[m], base[m, b, 1, hi] + self.got_b2[m]]
        if i == 2:
            arrive(self.copies(3, 0))
        for p in range(PARTS):
            self.last[m, p] = found[p] + self.got_z[0, p] if i == 2 else found[p]
        if go_on:
            begin(self.copies(3, i))

    def total(self, p):
        z = self.at["z"]
        found = self.last[z, p].astype(F32) + self.got_z[1, p].astype(F32) + self.got_z[2, p].astype(F32)
        return found.astype(BF16)

    def after_three(self):
        arrive(self.copies(3, 1) + self.copies(3, 2))
        for p in range(PARTS):
            self.out[self.at["lo"], p, self.at["hi"]] = self.total(p)
        begin(self.copies(4))

    def hand_over(self, own_ref, hand_ref):
        arrive(self.copies(3, 1))
        own_ref[...] = self.base[self.at["z"]]
        hand_ref[0] = self.last[self.cross]
        hand_ref[1] = self.got_z[1]

    def after_four(self):
        arrive(self.copies(4))
        begin(self.copies(5))

    def done(self):
        arrive(self.copies(4) if self.direct else self.copies(5))

    def sent(self):
        for stage in range(6):
            for i in range(4 if stage < 4 else 1):
                sent(self.copies(stage, i))

    def sent_early(self):
        for stage, count in enumerate((4, 3, 3, 2)):
            for i in range(count):
                sent(self.copies(stage, i))


class Finish:
    def __init__(self, at, model_size, own, hand, got_a, got_b, got_a2, got_b2, got_z, out, send_sem, recv_sem):
        self.at, self.own, self.hand, self.out = at, own, hand, out
        self.got_a, self.got_b, self.got_a2, self.got_b2, self.got_z = got_a, got_b, got_a2, got_b2, got_z
        self.send_sem, self.recv_sem = send_sem, recv_sem
        self.cross = (at["z"] + 2) % model_size

    def copies(self, stage):
        at, own = self.at, self.own
        b, lo, hi = at["b"], at["lo"], at["hi"]

        def one(slot, src, dst, device):
            return remote(src, dst, self.send_sem.at[slot], self.recv_sem.at[slot], device)

        if stage == 0:
            return [one(0, self.hand.at[0], self.got_z, {"mp": self.cross})]
        if stage == 1:
            return [
                one(1, own.at[:, 0, 1 - hi], self.got_a, at["far"]),
                one(2, own.at[1 - b, 1], self.got_b, at["side"]),
            ]
        if stage == 2:
            return [
                one(3, self.got_a.at[1 - b], self.got_a2, at["side"]),
                one(4, self.got_b.at[1 - hi], self.got_b2, at["far"]),
            ]
        if stage == 3:
            return [one(5, self.out.at[lo, :, hi], self.out.at[lo, :, hi], at["far"])]
        return [one(6, self.out.at[lo], self.out.at[lo], at["twin"])]

    def start(self):
        begin(self.copies(1) + self.copies(0))

    def after_one(self):
        arrive(self.copies(1))
        b, hi = self.at["b"], self.at["hi"]
        for h in range(2):
            self.got_a[h] = self.got_a[h] + self.own[h, 0, hi]
            self.got_b[h] = self.got_b[h] + self.own[b, 1, h]
        begin(self.copies(2))

    def after_two(self):
        arrive(self.copies(2) + self.copies(0))
        b, lo, hi = self.at["b"], self.at["lo"], self.at["hi"]
        halves = ((self.got_a[b], self.got_a2[...]), (self.got_b[hi], self.got_b2[...]))
        for p, (held, got) in enumerate(halves):
            total = held.astype(F32) + got.astype(F32) + self.hand[1, p].astype(F32) + self.got_z[p].astype(F32)
            self.out[lo, p, hi] = total.astype(BF16)
        begin(self.copies(3))

    def after_three(self):
        arrive(self.copies(3))
        begin(self.copies(4))

    def done(self):
        arrive(self.copies(4))

    def sent(self):
        for stage in range(5):
            sent(self.copies(stage))


REDUCE_SEMS = 60


def chunk_of(at, i):
    high, low = at["z"] // 2, at["z"] % 2
    flip_high, flip_low = 1 - i % 2, 1 - i // 2
    return 2 * (high + flip_high - 2 * high * flip_high) + low + flip_low - 2 * low * flip_low


def reduce_scratch(model_size, piece, dim):
    low = lambda *shape: pltpu.VMEM(shape, BF16)
    return [
        low(model_size, 2, PARTS, 2, piece, dim),
        low(model_size, 2, piece, dim),
        low(model_size, 2, piece, dim),
        low(model_size, piece, dim),
        low(model_size, piece, dim),
        low(model_size, PARTS, piece, dim),
        low(3, PARTS, piece, dim),
    ]


def pack_places(dim, width):
    ends = [dim]
    for size in (width, 16, 8, 8 * dim // width, 8 * dim // width):
        ends.append(ends[-1] + size)
    return [slice(first, last) for first, last in zip(ends[:-1], ends[1:])]


def pack_rows(dim, width):
    return -(-pack_places(dim, width)[-1].stop // 128) * 128


def student_step(
    stud_ref, own_ref, query_ref, w2_ref, bmid, w3_ref, b3_ref,
    dstud_ref, gw2_ref, gw3_ref, gsmall_ref, classes, pairs,
):
    row_count, seq, width = stud_ref.shape
    head = own_ref.shape[1] - seq
    tag_cells = [
        [own_ref[r : r + 1, p : p + 1] for p in range(2 * pairs)] for r in range(row_count)
    ]
    labels = jnp.concatenate([cells[p] for cells in tag_cells for p in range(pairs)], axis=0)
    weights = jnp.concatenate([cells[pairs + p] for cells in tag_cells for p in range(pairs)], axis=0)
    half = width // 2
    lane = lax.broadcasted_iota(jnp.int32, (2 * pairs, width), 1)
    row = lax.broadcasted_iota(jnp.int32, (2 * pairs, width), 0)
    mine = (lane >= half) == (row >= pairs)
    query_rows = jnp.where(mine, query_ref[...].reshape(1, width) * half ** (-0.5), 0.0)
    pair_of = lax.rem(lax.broadcasted_iota(jnp.int32, (2 * pairs, seq), 0), pairs).astype(F32)
    members, shares_all, pooled_all = [], [], []
    for r in range(row_count):
        scores = mm_exact(query_rows, stud_ref[r], NT)
        member = own_ref[r : r + 1, head:] == pair_of
        masked = jnp.where(member, scores, NEG)
        terms = jnp.exp(masked - jnp.max(masked, axis=1, keepdims=True))
        shares = terms / jnp.sum(terms, axis=1, keepdims=True)
        pooled = jnp.where(mine, mm_exact(shares, stud_ref[r]), 0.0)
        members.append(member)
        shares_all.append(shares)
        pooled_all.append(pooled[:pairs] + pooled[pairs:])
    pooled = jnp.concatenate(pooled_all, axis=0)
    middle = jnp.tanh(mm_exact(pooled, w2_ref[...]) + bmid)
    logits = mm_exact(middle, w3_ref[...], NT) + b3_ref[...]
    class_of = lax.broadcasted_iota(jnp.int32, logits.shape, 1)
    logits = jnp.where(class_of < classes, logits, NEG)
    terms = jnp.exp(logits - jnp.max(logits, axis=1, keepdims=True))
    chance = terms / jnp.sum(terms, axis=1, keepdims=True)
    grad_logits = weights * (chance - jnp.where(class_of.astype(F32) == labels, 1.0, 0.0))
    gw3_ref[...] = mm_exact(grad_logits, middle, TN)[: gw3_ref.shape[0]]
    grad_pre = mm_exact(grad_logits, w3_ref[...]) * (1.0 - middle * middle)
    gw2_ref[...] = mm_exact(pooled, grad_pre, TN)
    grad_pooled = mm_exact(grad_pre, w2_ref[...], NT)
    grad_query = jnp.zeros((1, width), F32)
    grad_bias = jnp.zeros((1, width), F32)
    for r in range(row_count):
        part = grad_pooled[r * pairs : (r + 1) * pairs]
        grad_parts = jnp.where(mine, jnp.concatenate([part, part], axis=0), 0.0)
        shares = shares_all[r]
        grad_shares = mm_exact(grad_parts, stud_ref[r], NT)
        inner = jnp.sum(shares * grad_shares, axis=1, keepdims=True)
        grad_scores = jnp.where(members[r], shares * (grad_shares - inner), 0.0)
        grad_hidden = mm_exact(
            jnp.concatenate([shares, grad_scores], axis=0),
            jnp.concatenate([grad_parts, query_rows], axis=0),
            TN,
        )
        low = grad_hidden.astype(BF16)
        dstud_ref[r] = low
        grad_bias += column_sum(low.astype(F32))
        found = mm_exact(grad_scores, stud_ref[r]) * half ** (-0.5)
        grad_query += column_sum(jnp.where(mine, found, 0.0))
    gsmall_ref[0:1] = grad_bias
    gsmall_ref[1:2] = column_sum(grad_pre)
    gsmall_ref[2:3] = grad_query
    gsmall_ref[3:4] = column_sum(grad_logits)
    gsmall_ref[4:8] = jnp.zeros((4, width), F32)


def gelu_parts(value):
    size = jnp.abs(value)
    bell = jnp.exp(value * value * -0.5)
    base = 1.0 + (0.3275911 * 0.5 ** 0.5) * size
    t = pl.reciprocal(base, approx=True)
    t = t * (2.0 - base * t)
    terms = ((((1.061405429 * t - 1.453152027) * t + 1.421413741) * t - 0.284496736) * t + 0.254829592) * t
    tail = 0.5 * terms * bell
    return jnp.where(value < 0.0, tail, 1.0 - tail), bell * 0.3989422804014327


COLUMNS = 256


def ffn_kernel(
    classes, pairs, scatter,
    xhat1_ref, rstd1_ref, gain_ref, shift_ref, wb_hbm, wc_home, early_ref, vecs_ref, bdown_ref, cot_hbm, own_ref,
    sw1_ref, sbias_ref, query_ref, w2_in, w3_in, b3_in,
    mixed_ref, gres_ref, dwb_ref, out_ref, hand_ref, packed_ref,
    pack_ref, w2_ref, w3_ref, b3_ref, gbup_ref, gvec_ref, gsw1_ref, act_ref, slope_ref, xhat2_ref, rstd2_ref,
    stud_ref, dstud_ref, low_ref, flip_ref, wc_ref, dwc_ref, wsend, wrecv, msend, mrecv, local_sem, piece_sem, wb_ref, cot_ref, *parts,
):
    row_count, seq, dim = xhat1_ref.shape
    model_size = wb_ref.shape[0]
    inner = wb_ref.shape[2]
    per_row = seq // BLOCK
    blocks = row_count * per_row
    width = sw1_ref.shape[1]
    at = mesh_place()
    gather = Gather(at, model_size, wc_home, wc_ref, wsend, wrecv, early_ref)
    own_pieces = gather.own_pieces(piece_sem)
    own_copy = pltpu.make_async_copy(wc_home, wc_ref.at[at["z"]], local_sem.at[0])
    own_copy.start()
    loads = [
        pltpu.make_async_copy(wb_hbm, wb_ref, local_sem.at[1]),
        pltpu.make_async_copy(cot_hbm, cot_ref, local_sem.at[2]),
    ]
    begin(loads)
    for copy in own_pieces:
        copy.start()
    greet(at, 2 if scatter else 1, model_size)
    for i in (1, 0, 2):
        begin(gather.copies(1, i) + gather.to_twin(0, i))
    if scatter:
        reducer = Reduce(at, model_size, dwc_ref, dwc_ref.at[:, :, at["lo"]], *parts, None, msend, mrecv)

    w2_at, w3_at, small_at, vec_at, bup_at = pack_places(dim, width)
    sb1, bmid = sbias_ref[0:1], sbias_ref[1:2]
    w2_ref[...] = w2_in[...].astype(F32)
    w3_ref[...] = jnp.zeros_like(w3_ref)
    w3_ref[:classes] = w3_in[...].astype(F32)
    b3_ref[...] = jnp.zeros_like(b3_ref)
    b3_ref[:, :classes] = b3_in[...].reshape(1, classes)
    gain_one, gain_two = gain_ref[0:1], gain_ref[1:2]
    shift_one, shift_two = shift_ref[0:1], shift_ref[1:2]

    def live(r):
        cells = [own_ref[i : i + 1, 2 * pairs : 2 * pairs + 1] for i in range(row_count)]
        return sum(jnp.where(r == i, 1.0, 0.0) * cells[i] for i in range(row_count))

    def place(t):
        return t // per_row, pl.ds(pl.multiple_of(t % per_row * BLOCK, BLOCK), BLOCK)

    def prepare(t, _):
        r, part = place(t)
        hidden = xhat1_ref[r, part] * gain_one + shift_one
        low_ref[t] = hidden.astype(BF16)
        xhat2_ref[r, part] = hidden + bdown_ref[...].reshape(1, dim)
        return 0

    lax.fori_loop(0, blocks, prepare, 0)
    for copy in own_pieces:
        copy.wait()
    loads[0].wait()

    def during(m, table):
        for when, actions in table.items():
            @pl.when(m == when)
            def _():
                for action, *args in actions:
                    action(*args)

    def up(m, _):
        during(m, {
            1: [(gather.advance, 2, 1, 0)],
            2: [(gather.advance, 2, 2), (gather.advance, 3, 1)],
            3: [(gather.advance, 3, 0)],
        })

        def one(t, _):
            low = low_ref[t]
            for c in range(0, inner, COLUMNS):
                columns = slice(c, c + COLUMNS)
                pre = mm(low, wb_ref[m, :, columns]) + vecs_ref[m, 1:2, columns]
                cdf, pdf = gelu_parts(pre)
                act_ref[m, t, :, columns] = (pre * cdf).astype(BF16)
                slope_ref[m, t, :, columns] = (cdf + pre * pdf).astype(BF16)
            return 0

        lax.fori_loop(0, blocks, one, 0)
        return 0

    lax.fori_loop(0, model_size, up, 0)
    gather.advance(3, 2)
    own_copy.wait()

    def down(m):
        def one(t, _):
            r, part = place(t)
            xhat2_ref[r, part] = xhat2_ref[r, part] + mm(act_ref[m, t], wc_ref[m])
            return 0

        lax.fori_loop(0, blocks, one, 0)

    down(at["z"])
    for i in (1, 0, 2):
        gather.done(i)
        down(gather.chunks[i])

    def norm_two(t, _):
        r, part = place(t)
        xhat, rstd = norm_parts(xhat2_ref[r, part])
        xhat2_ref[r, part] = xhat
        rstd2_ref[r, part] = rstd
        hidden_two = xhat * gain_two + shift_two
        mixed_ref[r, part] = (hidden_two * live(r)).astype(BF16)
        stud_ref[r, part] = mm(hidden_two.astype(BF16), sw1_ref[...]) + sb1
        return 0

    lax.fori_loop(0, blocks, norm_two, 0)
    student_step(
        stud_ref, own_ref, query_ref, w2_ref, bmid, w3_ref, b3_ref,
        dstud_ref, pack_ref.at[w2_at], pack_ref.at[w3_at], pack_ref.at[small_at], classes, pairs,
    )
    gvec_ref[...] = jnp.zeros_like(gvec_ref)
    gsw1_ref[...] = jnp.zeros_like(gsw1_ref)
    gbup_ref[...] = jnp.zeros_like(gbup_ref)

    loads[1].wait()

    def norm_two_back(t, _):
        r, part = place(t)
        xhat = xhat2_ref[r, part]
        two_low = (xhat * gain_two + shift_two).astype(BF16)
        grad_low = dstud_ref[r, part]
        gsw1_ref[...] += mm(grad_low, two_low, TN)
        upstream = cot_ref[r, part].astype(F32) * live(r) + mm(grad_low, sw1_ref[...], NT)
        gvec_ref[1:2] += column_sum(upstream * xhat)
        gvec_ref[3:4] += column_sum(upstream)
        grad = norm_back(upstream, xhat, rstd2_ref[r, part], gain_two)
        low = grad.astype(BF16)
        gvec_ref[4:5] += column_sum(low.astype(F32))
        gres_ref[r, part] = grad
        low_ref[t] = low
        flip_ref[:, pl.ds(pl.multiple_of(t * BLOCK, BLOCK), BLOCK)] = low.T
        return 0

    lax.fori_loop(0, blocks, norm_two_back, 0)
    half = dim // 2

    def weight_grads(out, right_ref, m):
        def one(y, _):
            part = pl.ds(pl.multiple_of(y * half, 128), half)
            total = mm(flip_ref[part, :], right_ref[m].reshape(blocks * BLOCK, inner)).astype(BF16)
            out[m, y] = total.reshape(out.shape[2:])
            return 0

        lax.fori_loop(0, 2, one, 0)

    def first_grads(i, _):
        weight_grads(dwc_ref, act_ref, chunk_of(at, i))
        if scatter:
            during(i, {n: [(reducer.start, n)] for n in range(model_size)})
        return 0

    lax.fori_loop(0, model_size, first_grads, 0)
    def backward(m, _):
        if scatter:
            during(m, {
                1: [(reducer.after_core, 0)],
                2: [(reducer.after_core, 1), (reducer.after_one, 0)],
                3: [(reducer.after_two, 0), (reducer.after_one, 1), (reducer.after_core, 2)],
            })

        def one(t, _):
            r, part = place(t)
            grad_pre = (mm(low_ref[t], wc_ref[m], NT) * slope_ref[m, t].astype(F32)).astype(BF16)
            slope_ref[m, t] = grad_pre
            gbup_ref[m] += column_sum(grad_pre.astype(F32))
            gres_ref[r, part] = gres_ref[r, part] + mm(grad_pre, wb_ref[m], NT)
            return 0

        lax.fori_loop(0, blocks, one, 0)
        return 0

    lax.fori_loop(0, model_size, backward, 0)

    def norm_one_back(t, _):
        r, part = place(t)
        upstream = gres_ref[r, part]
        xhat = xhat1_ref[r, part]
        gvec_ref[0:1] += column_sum(upstream * xhat)
        gvec_ref[2:3] += column_sum(upstream)
        resid = norm_back(upstream, xhat, rstd1_ref[r, part], gain_one)
        gres_ref[r, part] = resid
        gvec_ref[5:6] += column_sum(resid.astype(BF16).astype(F32))
        flip_ref[:, pl.ds(pl.multiple_of(t * BLOCK, BLOCK), BLOCK)] = (xhat * gain_one + shift_one).astype(BF16).T
        return 0

    lax.fori_loop(0, blocks, norm_one_back, 0)
    def second_grads(m, _):
        if scatter:
            during(m, {
                1: [(reducer.after_two, 1), (reducer.after_one, 2)],
                3: [(reducer.after_core, 3, False), (reducer.after_two, 2, False)],
            })
        weight_grads(dwb_ref, slope_ref, m)
        return 0

    lax.fori_loop(0, model_size, second_grads, 0)
    for m in range(model_size):
        bup = gbup_ref[m]
        for j in range(dim // width):
            pack_ref[bup_at.start + j * 8 + m : bup_at.start + j * 8 + m + 1] = bup[:, j * width : (j + 1) * width]
    for j in range(dim // width):
        columns = slice(j * width, (j + 1) * width)
        pack_ref[columns] = gsw1_ref[:, columns]
        pack_ref[vec_at.start + j * 8 : vec_at.start + j * 8 + 8] = gvec_ref[:, columns]
        if model_size < 8:
            first = bup_at.start + j * 8
            pack_ref[first + model_size : first + 8] = jnp.zeros((8 - model_size, width), F32)
    pack_ref[bup_at.stop :] = jnp.zeros((pack_ref.shape[0] - bup_at.stop, width), F32)
    packed_ref[...] = pack_ref[...].astype(BF16)
    if scatter:
        reducer.hand_over(out_ref, hand_ref)
        reducer.sent_early()
    else:
        out_ref[...] = dwc_ref[...]
        hand_ref[...] = jnp.zeros_like(hand_ref)
    gather.sent()


def ffn_both(xhat1, rstd1, gain, shift, w_b, w_c, early, vecs, b_down, cot, own, pairs, scatter,
             s_w1, s_bias, s_query, s_w2, s_w3, s_b3):
    rows, seq, dim = xhat1.shape
    model_size = w_b.shape[0]
    inner = w_b.shape[2]
    width = s_w1.shape[1]
    classes = s_w3.shape[1]
    blocks = rows * seq // BLOCK
    piece = dim // 16
    grid_shape = (model_size, 2, 2, PARTS, 2, piece, inner)
    low = lambda *shape: pltpu.VMEM(shape, BF16)
    f32 = lambda *shape: pltpu.VMEM(shape, F32)
    dma = pltpu.SemaphoreType.DMA
    vmem = pl.BlockSpec(memory_space=pltpu.VMEM)
    hbm = pl.BlockSpec(memory_space=pl.ANY)
    return pl.pallas_call(
        functools.partial(ffn_kernel, classes, pairs, scatter),
        in_specs=[vmem] * 4 + [hbm] * 3 + [vmem, vmem, hbm] + [vmem] * 7,
        out_specs=[vmem] * 6,
        out_shape=(
            jax.ShapeDtypeStruct((rows, seq, dim), BF16),
            jax.ShapeDtypeStruct((rows, seq, dim), F32),
            jax.ShapeDtypeStruct(grid_shape, BF16),
            jax.ShapeDtypeStruct(grid_shape[1:2] + grid_shape[3:] if scatter else grid_shape, BF16),
            jax.ShapeDtypeStruct((2, PARTS, piece, inner), BF16),
            jax.ShapeDtypeStruct((pack_rows(dim, width), width), BF16),
        ),
        scratch_shapes=[
            f32(pack_rows(dim, width), width),
            f32(width, width),
            f32(width, width),
            f32(1, width),
            f32(model_size, 1, inner),
            f32(8, dim),
            f32(width, dim),
            low(model_size, blocks, BLOCK, inner),
            low(model_size, blocks, BLOCK, inner),
            f32(rows, seq, dim),
            f32(rows, seq, 1),
            f32(rows, seq, width),
            low(rows, seq, width),
            low(blocks, BLOCK, dim),
            low(dim, rows * seq),
            low(model_size, inner, dim),
            low(*grid_shape),
            dma((GATHER_SEMS,)),
            dma((GATHER_SEMS,)),
            dma((REDUCE_SEMS,)),
            dma((REDUCE_SEMS,)),
            dma((3,)),
            dma((6,)),
            low(model_size, dim, inner),
            low(rows, seq, dim),
            *(reduce_scratch(model_size, piece, inner) if scatter else ()),
        ],
        compiler_params=pltpu.CompilerParams(
            vmem_limit_bytes=VMEM_MOST, collective_id=1, has_side_effects=True
        ),
        name="ffn_both",
    )(
        xhat1, rstd1, gain, shift, w_b, w_c, early, vecs, b_down, cot, own,
        s_w1, s_bias, s_query, s_w2, s_w3.T, s_b3,
    )


TILE_Q = 256
TILE_BACK = 128


def backward_group(grad_ctx, ctx_of, load, store, mask, lse_of, group_dim, p_ref, s_ref):
    scale = HEAD_DIM ** (-0.5)
    for j in range(group_dim // HEAD_DIM):
        rows = slice(j * HEAD_DIM, (j + 1) * HEAD_DIM)
        k_rows = slice(group_dim + rows.start, group_dim + rows.stop)
        v_rows = slice(2 * group_dim + rows.start, 2 * group_dim + rows.stop)
        q_t = load(rows) * scale
        k_t = load(k_rows)
        v_t = load(v_rows)
        d_t = grad_ctx[rows]
        seq = q_t.shape[1]
        inner = column_sum(d_t.astype(F32) * ctx_of(rows).astype(F32))
        lse = lse_of(j)
        k_n, v_n = k_t.T, v_t.T
        probs_ref, grads_ref = p_ref.at[j % 2], s_ref.at[j % 2]
        for q0 in range(0, seq, TILE_Q):
            columns = slice(q0, q0 + TILE_Q)
            q, d = q_t[:, columns], d_t[:, columns]
            for k0 in range(0, seq, TILE_BACK):
                part = slice(k0, k0 + TILE_BACK)
                probs = jnp.exp(mm(k_n[part], q) + mask[part, columns] - lse[:, columns])
                grad_probs = mm(v_n[part], d)
                probs_ref[part, columns] = probs.astype(BF16)
                grads_ref[part, columns] = (probs * (grad_probs - inner[:, columns])).astype(BF16)
        store(rows, mm(k_t * scale, grads_ref[...]).astype(BF16))
        store(k_rows, mm(q_t, grads_ref[...], NT).astype(BF16))
        store(v_rows, mm(d_t, probs_ref[...], NT).astype(BF16))


def attn_backward_kernel(
    x_ref, gres_ref, wa_ref, qkv_ref, ctx_ref, lse_ref, own_ref, dx_ref, dwa_ref, bias_ref,
    mask_ref, acc_ref, work_ref, xflip_ref, gflip_ref, p_ref, s_ref,
):
    row_count, seq, dim = x_ref.shape
    model_size = wa_ref.shape[0]
    group_dim = ctx_ref.shape[2]
    bias_ref[...] = jnp.zeros_like(bias_ref)
    seg_rows = own_ref[:, own_ref.shape[1] - seq :]
    seg_cols = seg_rows.T
    for r in range(row_count):
        mask_ref[...] = jnp.where(seg_cols[:, r : r + 1] == seg_rows[r : r + 1], 0.0, NEG)
        acc_ref[...] = gres_ref[r]
        grad_low = gres_ref[r].astype(BF16)
        columns = slice(r * seq, (r + 1) * seq)
        gflip_ref[:, columns] = grad_low.T
        xflip_ref[:, columns] = x_ref[r].T

        def one_group(m, _):
            grad_ctx = mm(wa_ref[m, 3 * group_dim :, :], grad_low, NT).astype(BF16)

            def store(rows, value):
                work_ref[r, m, rows, :] = value

            backward_group(
                grad_ctx, lambda rows: ctx_ref[r, m, rows, :], lambda rows: qkv_ref[r, m, rows, :], store,
                mask_ref, lambda j: lse_ref[r, m, j : j + 1, :], group_dim, p_ref, s_ref,
            )
            grads = work_ref[r, m]
            bias_ref[m] += mm(jnp.ones((8, seq), BF16), grads, NT)
            acc_ref[...] += mm(grads, wa_ref[m, : 3 * group_dim, :], TN)
            return 0

        lax.fori_loop(0, model_size, one_group, 0)
        dx_ref[r] = acc_ref[...].astype(BF16)

    def weight_grads(i, _):
        m, part = i // 2, pl.ds(pl.multiple_of(i % 2 * (dim // 2), 128), dim // 2)
        left, right = 0.0, 0.0
        for r in range(row_count):
            columns = slice(r * seq, (r + 1) * seq)
            left += mm(xflip_ref[part, columns], work_ref[r, m], NT)
            right += mm(gflip_ref[part, columns], ctx_ref[r, m], NT)
        dwa_ref[m, part, : 3 * group_dim] = left.astype(BF16)
        dwa_ref[m, part, 3 * group_dim :] = right.astype(BF16)
        return 0

    lax.fori_loop(0, 2 * model_size, weight_grads, 0)


def attn_backward(x, gres, w_a, qkv, ctx, lse, own):
    rows, seq, dim = x.shape
    model_size = w_a.shape[0]
    group_dim = dim // model_size
    return pl.pallas_call(
        attn_backward_kernel,
        out_shape=(
            jax.ShapeDtypeStruct((rows, seq, dim), BF16),
            jax.ShapeDtypeStruct((model_size, dim, 4 * group_dim), BF16),
            jax.ShapeDtypeStruct((model_size, 8, 3 * group_dim), F32),
        ),
        scratch_shapes=[
            pltpu.VMEM((seq, seq), F32),
            pltpu.VMEM((seq, dim), F32),
            pltpu.VMEM((rows, model_size, 3 * group_dim, seq), BF16),
            pltpu.VMEM((dim, rows * seq), BF16),
            pltpu.VMEM((dim, rows * seq), BF16),
            pltpu.VMEM((2, seq, seq), BF16),
            pltpu.VMEM((2, seq, seq), BF16),
        ],
        compiler_params=pltpu.CompilerParams(vmem_limit_bytes=VMEM_MOST),
        name="attn_backward",
    )(x, gres, w_a, qkv, ctx, lse, own)
def slot_of_rows(exit_ref, target_ref, depth):
    count = exit_ref.shape[0]
    flat = []
    for i in range(count):
        rank = 0
        for h in range(i):
            rank = rank + jnp.where(target_ref[h] == target_ref[i], 1 - exit_ref[h], 0)
        flat.append(jnp.where(exit_ref[i] == 0, target_ref[i] * depth + rank, -1))
    return flat


def pick_of_slots(tag_ref, depth, flag_at, capacity):
    seen = jnp.zeros((1, 1), F32)
    picks = []
    for k in range(tag_ref.shape[0] * depth):
        live = tag_ref[k // depth, k % depth : k % depth + 1, flag_at : flag_at + 1]
        picks.append([jnp.where(seen == float(c), live, 0.0) for c in range(min(capacity, k + 1))])
        seen = seen + live
    return picks


def slots_of_tags(tag_ref, depth, flag_at, capacity):
    seen, slots = 0, []
    for k in range(tag_ref.shape[0] * depth):
        cell = tag_ref[k // depth, k % depth : k % depth + 1, flag_at : flag_at + 1]
        live = jnp.where(jnp.sum(cell) > 0.5, 1, 0)
        slots.append((jnp.minimum(seen, capacity - 1), live))
        seen = seen + live
    return slots


TOKENS = 32
CUTS = 3


def enter_kernel(
    depth, pairs,
    exit_ref, target_ref, rows_ref, seg_ref, lab_ref, wt_ref, wqkv_ref, wout_ref, bqv_ref, bup_ref, bout_ref,
    wb_loc, wc_loc,
    own_ref, got_tags_ref, vecs_ref, x_out, wa_out, wb_ref, early_ref,
    qkv_ref, ctx_ref, lse_ref, xhat_ref, rstd_ref,
    tags_ref, vec_ref, wa_loc, slot_ref, part_ref, x_ref, wa_ref, tag_ref, taggot_ref, taglocal_ref, vecgot_ref,
    mask_ref, acc_ref, wsend, wrecv, rsend, rrecv, local_sem, *got_refs,
):
    row_count, token_part, dim = rows_ref.shape
    own_rows, seq = x_ref.shape[:2]
    model_size = wa_ref.shape[0]
    batch_size = taggot_ref.shape[0]
    capacity = own_rows * model_size
    group_dim = wout_ref.shape[0]
    flag_at = 2 * pairs
    head = tag_ref.shape[2] - seq
    at = mesh_place()
    b, z = at["b"], at["z"]
    gathers = [
        Gather(at, model_size, home, spot, wsend.at[k], wrecv.at[k])
        for k, (home, spot) in enumerate(((wa_loc, wa_ref), (wb_loc, wb_ref)))
    ]
    first_gather, second_gather = gathers
    third_gather = Gather(at, model_size, wc_loc, None, wsend.at[2], wrecv.at[2], early_ref)
    vec_first = (CUTS + 1) * batch_size + CUTS * model_size

    def vec_copies():
        return [
            remote(vec_ref, vecgot_ref.at[z], rsend.at[vec_first + i], rrecv.at[vec_first + i],
                   {"mp": (z + i) % model_size})
            for i in range(1, model_size)
        ]

    wide = dim // CUTS

    def batch_copies(cut):
        columns = pl.ds(cut * wide, wide)
        copies = []
        for j in range(1, batch_size):
            t = (b + j) % batch_size
            n = cut * batch_size + j
            copies.append(remote(slot_ref.at[pl.ds(t * depth, depth), :, columns],
                                 got_refs[cut].at[pl.ds(b * depth, depth)],
                                 rsend.at[n], rrecv.at[n], {"batch": t}))
            if cut == 0:
                n = CUTS * batch_size + j
                copies.append(remote(tag_ref.at[t], taggot_ref.at[b], rsend.at[n], rrecv.at[n], {"batch": t}))
        return copies

    mine = pl.ds(pl.multiple_of(z * token_part, 128), token_part)

    def row_copies(cut, r):
        columns = pl.ds(cut * wide, wide)
        first = (CUTS + 1) * (batch_size + model_size) + (cut * own_rows + r) * model_size
        return [
            remote(part_ref.at[(z + i) % model_size * own_rows + r, :, columns], x_ref.at[r, mine, columns],
                   rsend.at[first + i], rrecv.at[first + i], {"mp": (z + i) % model_size})
            for i in range(1, model_size)
        ]

    def local_copies():
        return [
            pltpu.make_async_copy(gather.home, gather.spot.at[z], local_sem.at[k])
            for k, gather in enumerate(gathers)
        ]

    for j in range(3):
        wa_loc[j * group_dim : (j + 1) * group_dim, :] = wqkv_ref[j]
    wa_loc[3 * group_dim :, :] = wout_ref[...]
    vec_ref[...] = jnp.zeros_like(vec_ref)
    vec_ref[0:1, :group_dim] = bqv_ref[0:1]
    vec_ref[0:1, 2 * group_dim : 3 * group_dim] = bqv_ref[1:2]
    vec_ref[1:2] = bup_ref[...].reshape(1, dim)
    greet(at, batch_size, model_size)
    first_gather.start()
    begin(vec_copies())
    begin(local_copies())

    flat = slot_of_rows(exit_ref, target_ref, depth)
    tags_ref[...] = jnp.zeros_like(tags_ref)
    taglocal_ref[0] = jnp.zeros_like(taglocal_ref[0])
    taglocal_ref[0, :pairs, :row_count] = lab_ref[...].astype(F32)
    taglocal_ref[0, pairs : 2 * pairs, :row_count] = wt_ref[...].astype(F32)
    tags_ref[:, : 2 * pairs] = taglocal_ref[0, : 2 * pairs, :128].T[: tags_ref.shape[0]]
    tags_ref[:row_count, flag_at : flag_at + 1] = jnp.ones((row_count, 1), F32)
    tags_ref[:row_count, head:] = seg_ref[...].astype(F32)
    tag_ref[...] = jnp.zeros_like(tag_ref)

    def taken(k):
        hits = [jnp.where(flat[r] == k, 1, 0) for r in range(row_count)]
        return sum(r * hits[r] for r in range(row_count)), sum(hits).astype(F32)

    def fill(t, dst_ref, cut):
        columns = pl.ds(cut * wide, wide)
        for s in range(depth):
            row, there = taken(t * depth + s)
            found = (rows_ref[row, :, columns].astype(F32) * there).astype(BF16)
            if dst_ref is None:
                got_refs[cut][t * depth + s] = found
            else:
                dst_ref[t * depth + s, :, columns] = found

    def fill_tags(t):
        for s in range(depth):
            total = jnp.zeros((1, tags_ref.shape[1]), F32)
            for r in range(row_count):
                total += jnp.where(flat[r] == t * depth + s, 1.0, 0.0) * tags_ref[r : r + 1]
            tag_ref[t, s : s + 1] = total

    for j in range(1, batch_size):
        fill_tags((b + j) % batch_size)
    for cut in range(CUTS):
        for j in range(1, batch_size):
            fill((b + j) % batch_size, slot_ref, cut)
        if cut == 0:
            begin(batch_copies(0))
            fill_tags(b)
            taggot_ref[b] = tag_ref[b]
            fill(b, None, 0)
    for cut in range(1, CUTS):
        fill(b, None, cut)
    arrive(batch_copies(0))
    begin(batch_copies(1))

    picks = pick_of_slots(taggot_ref, depth, flag_at, capacity)

    slots = slots_of_tags(taggot_ref, depth, flag_at, capacity)

    def compact(cut):
        columns = pl.ds(cut * wide, wide)
        for c in range(capacity):
            hits = [jnp.where(place == c, live, 0) for place, live in slots]
            k = sum(n * hits[n] for n in range(c, len(slots)))
            there = sum(hits[c:]).astype(F32)
            part_ref[c, :, columns] = (got_refs[cut][k].astype(F32) * there).astype(BF16)
        begin(row_copies(cut, 0))

    compact(0)
    first_gather.advance(1, 1, 0)
    arrive(batch_copies(1))
    for cut in range(2, CUTS):
        begin(batch_copies(cut))
        compact(cut - 1)
        if cut == 2:
            first_gather.advance(1, 2)
        arrive(batch_copies(cut))
    compact(CUTS - 1)
    first_gather.advance(2, 1, 0, 2)
    second_gather.start()
    for r in range(1, own_rows):
        for cut in range(CUTS):
            begin(row_copies(cut, r))
    for c in range(capacity):
        total = jnp.zeros((1, tags_ref.shape[1]), F32)
        for k in range(c, len(picks)):
            total += picks[k][c] * taggot_ref[k // depth, k % depth : k % depth + 1]
        taglocal_ref[c, 0:1] = total
    for i in range(own_rows):
        x_ref[i, mine] = part_ref[z * own_rows + i]
    own_ref[...] = jnp.zeros_like(own_ref)
    for i in range(own_rows):
        own_ref[i : i + 1] = taglocal_ref[z * own_rows + i, 0:1]
    got_tags_ref[...] = taggot_ref[...]

    first_gather.advance(3, 1, 0, 2)
    arrive(vec_copies())
    vecgot_ref[z] = vec_ref[...]
    vecs_ref[...] = vecgot_ref[...]
    for copy in local_copies():
        copy.wait()
    keep = [
        pltpu.make_async_copy(x_ref, x_out, local_sem.at[3]),
        pltpu.make_async_copy(wa_ref, wa_out, local_sem.at[4]),
    ]

    def rows_here(r):
        for cut in range(CUTS):
            arrive(row_copies(cut, r))

    rows_here(0)
    seg_rows = own_ref[:, head:]
    seg_cols = seg_rows.T
    def forward_early():
        arrive(third_gather.early_copies(0))
        begin(third_gather.early_copies(1))

    late = {
        (0, 1): ((first_gather.done, 1),),
        (0, 2): ((first_gather.done, 0), (second_gather.advance, 1, 1, 0)),
        (0, 3): ((first_gather.done, 2), (second_gather.advance, 1, 2)),
        (1, 0): ((second_gather.advance, 2, 2),),
        (1, 1): ((second_gather.advance, 3, 1, 0),),
        (1, 2): ((second_gather.advance, 3, 2), (forward_early,)),
    }

    for r in range(own_rows):
        if r == 1:
            second_gather.advance(2, 1, 0)
            begin(third_gather.early_copies(0))
            for n in range(1, own_rows):
                rows_here(n)
            begin(keep)
        mask_ref[...] = jnp.where(seg_cols[:, r : r + 1] == seg_rows[r : r + 1], 0.0, NEG)
        acc_ref[...] = jnp.zeros_like(acc_ref)

        def one_group(i, _):
            m = chunk_of(at, model_size - 1 - i)
            for step in range(model_size):
                if (r, step) in late:
                    @pl.when(i == step)
                    def _():
                        for action, *args in late[r, step]:
                            action(*args)

            bias = vecgot_ref[m].T[: 3 * group_dim, 0:1]
            low = (mm(wa_ref[m, : 3 * group_dim, :], x_ref[r], NT) + bias).astype(BF16)
            qkv_ref[r, m] = low
            for j in range(group_dim // HEAD_DIM):
                rows = slice(j * HEAD_DIM, (j + 1) * HEAD_DIM)
                q_t = low[rows] * HEAD_DIM ** (-0.5)
                k_t = low[group_dim + rows.start : group_dim + rows.stop]
                v_t = low[2 * group_dim + rows.start : 2 * group_dim + rows.stop]
                scores = mm(k_t, q_t, TN) + mask_ref[...]
                top = jnp.max(scores, axis=0, keepdims=True)
                terms = jnp.exp(scores - top)
                total = jnp.sum(terms, axis=0, keepdims=True)
                ctx_t = mm(v_t, terms.astype(BF16)) / total
                ctx_ref[r, m, rows, :] = ctx_t.astype(BF16)
                lse_ref[r, m, j : j + 1, :] = top + jnp.log(total)
            acc_ref[...] += mm(ctx_ref[r, m], wa_ref[m, 3 * group_dim :, :], TN)
            return 0

        lax.fori_loop(0, model_size, one_group, 0)
        xhat, rstd = norm_parts(x_ref[r].astype(F32) + (acc_ref[...] + bout_ref[...].reshape(1, dim)))
        xhat_ref[r] = xhat
        rstd_ref[r] = rstd

    second_gather.done(0, 1, 2)
    arrive(third_gather.early_copies(1))
    for copy in keep:
        copy.wait()
    for gather in gathers:
        gather.sent()
    sent(third_gather.early_copies(0) + third_gather.early_copies(1))
    sent(vec_copies())
    for cut in range(CUTS):
        sent(batch_copies(cut))
        for r in range(own_rows):
            sent(row_copies(cut, r))


def enter(exit_flag, target, rows_in, seg, labels, weights, w_qkv, w_out, b_qv, b_up, b_out, w_b, w_c,
          own_rows, batch_size, model_size):
    row_count, token_part, dim = rows_in.shape
    seq = token_part * model_size
    capacity = own_rows * model_size
    depth = (capacity + batch_size - 1) // batch_size
    group_dim = dim // model_size
    pairs = labels.shape[1]
    tag_wide = 128 + seq
    smem = pl.BlockSpec(memory_space=pltpu.SMEM)
    vmem = pl.BlockSpec(memory_space=pltpu.VMEM)
    hbm = pl.BlockSpec(memory_space=pl.ANY)
    full = jax.ShapeDtypeStruct((model_size, dim, dim), BF16)
    f32 = lambda *shape: jax.ShapeDtypeStruct(shape, F32)
    low = lambda *shape: jax.ShapeDtypeStruct(shape, BF16)
    moves = (CUTS + 1) * (batch_size + model_size) + CUTS * own_rows * model_size
    return pl.pallas_call(
        functools.partial(enter_kernel, depth, pairs),
        in_specs=[smem, smem] + [vmem] * 9 + [hbm, hbm],
        out_specs=[vmem, vmem, vmem, hbm, hbm, hbm, hbm] + [vmem] * 5,
        out_shape=(
            f32(8, tag_wide),
            f32(batch_size, 8, tag_wide),
            f32(model_size, 8, dim),
            low(own_rows, seq, dim),
            full,
            full,
            low(3, 2, dim // 16, dim),
            low(own_rows, model_size, 3 * group_dim, seq),
            low(own_rows, model_size, group_dim, seq),
            f32(own_rows, model_size, group_dim // HEAD_DIM, seq),
            f32(own_rows, seq, dim),
            f32(own_rows, seq, 1),
        ),
        scratch_shapes=[
            pltpu.VMEM((-(-row_count // 8) * 8, tag_wide), F32),
            pltpu.VMEM((8, dim), F32),
            pltpu.VMEM((dim, dim), BF16),
            pltpu.VMEM((batch_size * depth, token_part, dim), BF16),
            pltpu.VMEM((capacity, token_part, dim), BF16),
            pltpu.VMEM((own_rows, seq, dim), BF16),
            pltpu.VMEM((model_size, dim, dim), BF16),
            pltpu.VMEM((batch_size, 8, tag_wide), F32),
            pltpu.VMEM((batch_size, 8, tag_wide), F32),
            pltpu.VMEM((capacity, 8, tag_wide), F32),
            pltpu.VMEM((model_size, 8, dim), F32),
            pltpu.VMEM((seq, seq), F32),
            pltpu.VMEM((seq, dim), F32),
            pltpu.SemaphoreType.DMA((3, GATHER_SEMS)),
            pltpu.SemaphoreType.DMA((3, GATHER_SEMS)),
            pltpu.SemaphoreType.DMA((moves,)),
            pltpu.SemaphoreType.DMA((moves,)),
            pltpu.SemaphoreType.DMA((5,)),
            *[pltpu.VMEM((batch_size * depth, token_part, dim // CUTS), BF16) for _ in range(CUTS)],
        ],
        compiler_params=pltpu.CompilerParams(
            vmem_limit_bytes=VMEM_MOST, collective_id=0, has_side_effects=True
        ),
        name="enter",
    )(
        exit_flag, target, rows_in, seg, labels.T, weights.T, jnp.transpose(w_qkv, (0, 2, 1)), w_out, b_qv, b_up, b_out,
        w_b, w_c,
    )


def leave_kernel(
    depth, pairs,
    tags_ref, own_ref, x_hbm, gres_hbm, wa_hbm, qkv_hbm, ctx_hbm, lse_ref,
    dwb_hbm, ownc_ref, hand_ref, pack_ref,
    back_got, mats_ref, sums_ref, bias_ref,
    x_ref, wa_ref, ctx_ref, work_ref, acc_ref, mask_ref, p_ref, s_ref, xflip_ref, gflip_ref, dx_ref, dwa_ref,
    own_half, *rest,
):
    parts_a, parts_b, parts_c, rest = rest[:7], rest[7:14], rest[14:19], rest[19:]
    (
        small_acc, small_got, small_z, bias_acc, bias_row, bias_got, bias_z, back_ref,
        msend, mrecv, ssend, srecv, bsend, brecv, rsend, rrecv, local_sem, *mine_refs,
    ) = rest
    row_count, seq, dim = x_ref.shape
    model_size = wa_ref.shape[0]
    batch_size = tags_ref.shape[0]
    group_dim = ctx_ref.shape[2]
    token_part = seq // model_size
    capacity = row_count * model_size
    others = model_size - 1
    at = mesh_place()
    b, z, lo, hi = at["b"], at["z"], at["lo"], at["hi"]
    far, twin, side = at["far"], at["twin"], at["side"]

    def shard(i):
        return {"mp": (z + i) % model_size}

    first = Reduce(at, model_size, dwb_hbm, own_half, *parts_b, mats_ref.at[1], msend.at[1], mrecv.at[1], 0, True)
    second = Reduce(at, model_size, dwa_ref, dwa_ref.at[:, :, lo], *parts_a, mats_ref.at[0], msend.at[0], mrecv.at[0], 3, True)
    third = Finish(at, model_size, ownc_ref, hand_ref, *parts_c, mats_ref.at[2], msend.at[2], mrecv.at[2])

    def small_copies(stage):
        def one(slot, src, dst, device):
            return remote(src, dst, ssend.at[slot], srecv.at[slot], device)

        if stage == 0:
            return [one(0, pack_ref.at[1 - lo], small_got.at[0], twin)]
        if stage < 3:
            return [one(stage, small_acc.at[stage - 1], small_got.at[stage], (far, side)[stage - 1])]
        if stage == 3:
            return [
                one(2 + i, small_acc.at[2, (z + i) % model_size], small_z.at[i - 1], shard(i))
                for i in range(1, model_size)
            ]
        if stage == 4:
            return [
                one(2 + others + i, sums_ref.at[lo, z], sums_ref.at[lo, z], shard(i))
                for i in range(1, model_size)
            ]
        return [one(3 + 2 * others, sums_ref.at[lo], sums_ref.at[lo], twin)]

    def bias_copies(stage):
        def one(slot, src, dst, device):
            return remote(src, dst, bsend.at[slot], brecv.at[slot], device)

        if stage < 3:
            return [one(stage, bias_row.at[stage], bias_got.at[stage], (twin, far, side)[stage])]
        return [one(2 + i, bias_row.at[3], bias_z.at[i - 1], shard(i)) for i in range(1, model_size)]

    wide = dim // CUTS

    def row_copies(r, cut):
        columns = pl.ds(cut * wide, wide)
        first = (r * CUTS + cut) * others - 1
        return [
            remote(
                dx_ref.at[r, pl.ds(pl.multiple_of((z + i) % model_size * token_part, 128), token_part), columns],
                mine_refs[cut].at[z * row_count + r],
                rsend.at[first + i], rrecv.at[first + i], shard(i),
            )
            for i in range(1, model_size)
        ]

    def batch_copies(cut):
        columns = pl.ds(cut * wide, wide)
        first = row_count * CUTS * others + cut * (batch_size - 1) - 1
        copies = []
        for j in range(1, batch_size):
            t = (b + j) % batch_size
            copies.append(remote(
                back_ref.at[pl.ds(t * depth, depth), :, columns],
                back_got.at[pl.ds(b * depth, depth), :, columns],
                rsend.at[first + j], rrecv.at[first + j], {"batch": t},
            ))
        return copies

    def local_copies():
        return [
            pltpu.make_async_copy(dwb_hbm.at[:, :, lo], own_half, local_sem.at[0]),
        ]

    def inputs():
        return [
            pltpu.make_async_copy(qkv_hbm, work_ref, local_sem.at[2]),
            pltpu.make_async_copy(gres_hbm, acc_ref, local_sem.at[3]),
            pltpu.make_async_copy(x_hbm, x_ref, local_sem.at[4]),
            pltpu.make_async_copy(wa_hbm, wa_ref, local_sem.at[5]),
            pltpu.make_async_copy(ctx_hbm, ctx_ref, local_sem.at[6]),
        ]

    def small_step(stage):
        arrive(small_copies(stage))
        if stage == 0:
            small_acc[0] = pack_ref[lo] + small_got[0]
        if stage in (1, 2):
            small_acc[stage] = small_acc[stage - 1] + small_got[stage]
        if stage == 3:
            total = small_acc[2, z].astype(F32)
            for i in range(others):
                total += small_z[i].astype(F32)
            sums_ref[lo, z] = total.astype(BF16)
        if stage < 5:
            begin(small_copies(stage + 1))

    def bias_step(stage):
        arrive(bias_copies(stage))
        if stage < 3:
            bias_row[stage + 1] = bias_row[stage] + bias_got[stage]
            begin(bias_copies(stage + 1))
        else:
            total = bias_row[3]
            for i in range(others):
                total += bias_z[i]
            own = sum(jnp.where(z == m, 1.0, 0.0) * total[m : m + 1] for m in range(model_size))
            bias_ref[...] = jnp.broadcast_to(own, bias_ref.shape)

    begin(inputs())
    begin(local_copies())
    greet(at, batch_size, model_size)
    begin(small_copies(0))
    third.start()
    for i in range(model_size):
        first.start(i)
    seg_rows = own_ref[:, own_ref.shape[1] - seq :]
    seg_cols = seg_rows.T
    for copy in inputs() + local_copies():
        copy.wait()

    steps = {
        0: [],
        1: [(small_step, 0), (third.after_one,)],
        2: [(first.after_core, 0)],
        3: [(first.after_core, 1), (small_step, 1), (third.after_two,)],
        4: [(first.after_one, 0), (small_step, 2)],
        5: [(first.after_core, 2), (first.after_one, 1), (first.after_two, 0), (small_step, 3), (third.after_three,)],
        6: [(first.after_core, 3), (first.after_two, 1), (small_step, 4)],
        7: [(first.after_one, 2), (second.after_core, 0)],
    }

    def weight_grads(i):
        m, rows_y = chunk_of(at, i), dim // 2

        def one(y, _):
            part = pl.ds(pl.multiple_of(y * rows_y, 128), rows_y)
            left, right = 0.0, 0.0
            for q in range(row_count):
                cols = slice(q * seq, (q + 1) * seq)
                left += mm(xflip_ref[part, cols], work_ref[q, m], NT)
                right += mm(gflip_ref[part, cols], ctx_ref[q, m], NT)
            shape = dwa_ref.shape[2:-1]
            dwa_ref[m, y, :, :, :, :, : 3 * group_dim] = left.astype(BF16).reshape(*shape, 3 * group_dim)
            dwa_ref[m, y, :, :, :, :, 3 * group_dim :] = right.astype(BF16).reshape(*shape, group_dim)
            return 0

        lax.fori_loop(0, 2, one, 0)

    for r in range(row_count):
        mask_ref[...] = jnp.where(seg_cols[:, r : r + 1] == seg_rows[r : r + 1], 0.0, NEG)
        grad_low = acc_ref[r].astype(BF16)
        columns = slice(r * seq, (r + 1) * seq)
        gflip_ref[:, columns] = grad_low.T
        xflip_ref[:, columns] = x_ref[r].T

        def one_group(i, _):
            if r == row_count - 1:
                @pl.when(i > 0)
                def _():
                    weight_grads(i - 1)

            for step in range(model_size):
                @pl.when(i == step)
                def _():
                    if r == row_count - 1 and step > 0:
                        second.start(step - 1)
                    for action, *args in steps[r * model_size + step]:
                        action(*args)

            m = chunk_of(at, i)
            grad_ctx = mm(wa_ref[m, 3 * group_dim :, :], grad_low, NT).astype(BF16)

            def store(rows, value):
                work_ref[r, m, rows, :] = value

            backward_group(
                grad_ctx, lambda rows: ctx_ref[r, m, rows, :], lambda rows: work_ref[r, m, rows, :], store,
                mask_ref, lambda j: lse_ref[r, m, j : j + 1, :], group_dim, p_ref, s_ref,
            )
            grads = work_ref[r, m]
            found = mm(jnp.ones((8, seq), BF16), grads, NT)
            if r == 0:
                bias_acc[m] = found
            else:
                bias_acc[m] = bias_acc[m] + found
            acc_ref[r] = acc_ref[r] + mm(grads, wa_ref[m, : 3 * group_dim, :], TN)
            return 0

        lax.fori_loop(0, model_size, one_group, 0)
        dx_ref[r] = acc_ref[r].astype(BF16)
        for cut in range(CUTS if r < row_count - 1 else 2):
            begin(row_copies(r, cut))

    weight_grads(model_size - 1)
    second.start(model_size - 1)
    for r in range(row_count):
        for cut in range(CUTS):
            part = pl.ds(pl.multiple_of(z * token_part, 128), token_part)
            mine_refs[cut][z * row_count + r] = dx_ref[r, part, cut * wide : (cut + 1) * wide]
    first.after_one(3)
    second.after_core(1)
    slots = slots_of_tags(tags_ref, depth, 2 * pairs, capacity)

    def give(cut):
        columns = pl.ds(cut * wide, wide)
        for k, (place, live) in enumerate(slots):
            found = mine_refs[cut][place].astype(F32) * live.astype(F32)
            back_ref[k, :, columns] = found.astype(BF16)
        begin(batch_copies(cut))

    def returned(cut):
        for r in range(row_count):
            arrive(row_copies(r, cut))
        if cut + 2 < CUTS:
            begin(row_copies(row_count - 1, cut + 2))
        give(cut)

    returned(0)
    first.after_two(2)
    second.after_one(0)
    second.after_core(2)
    returned(1)
    bias_row[0] = jnp.zeros_like(bias_row[0])
    for m in range(model_size):
        bias_row[0, m : m + 1] = bias_acc[m, 0:1]
    begin(bias_copies(0))
    first.after_two(3)
    second.after_core(3)
    second.after_one(1)
    returned(2)
    second.after_two(0)
    own_slots = pl.ds(b * depth, depth)
    back_got[own_slots] = back_ref[own_slots]
    second.after_two(1)
    second.after_one(2)
    bias_step(0)
    first.after_three()
    second.after_two(2)
    second.after_one(3)
    bias_step(1)
    small_step(5)
    third.done()
    second.after_two(3)
    bias_step(2)
    second.after_three()
    bias_step(3)
    for cut in range(CUTS):
        arrive(batch_copies(cut))

    for reducer in (first, second):
        reducer.done()
        reducer.sent()
    third.sent()
    for stage in range(6):
        sent(small_copies(stage))
    for stage in range(4):
        sent(bias_copies(stage))
    for cut in range(CUTS):
        for r in range(row_count):
            sent(row_copies(r, cut))
        sent(batch_copies(cut))


def leave(tags, own, x, gres, w_a, qkv, ctx, lse, d_wb, mat_c, hand, pack, batch_size, pairs):
    rows, seq, dim = x.shape
    model_size = w_a.shape[0]
    group_dim = dim // model_size
    token_part = seq // model_size
    capacity = rows * model_size
    depth = (capacity + batch_size - 1) // batch_size
    slots = batch_size * depth
    piece = dim // 16
    others = model_size - 1
    grid_shape = (model_size, 2, 2, PARTS, 2, piece, dim)
    pack_shape = (2, model_size, pack.shape[0] // (2 * model_size), pack.shape[1])
    vmem = pl.BlockSpec(memory_space=pltpu.VMEM)
    hbm = pl.BlockSpec(memory_space=pl.ANY)
    dma = pltpu.SemaphoreType.DMA
    low = lambda *shape: pltpu.VMEM(shape, BF16)
    f32 = lambda *shape: pltpu.VMEM(shape, F32)
    row_moves = CUTS * (rows * others + batch_size - 1)
    return pl.pallas_call(
        functools.partial(leave_kernel, depth, pairs),
        in_specs=[vmem, vmem, hbm, hbm, hbm, hbm, hbm, vmem, hbm, vmem, vmem, vmem],
        out_specs=[vmem, vmem, vmem, vmem],
        out_shape=(
            jax.ShapeDtypeStruct((slots, token_part, dim), BF16),
            jax.ShapeDtypeStruct((3,) + grid_shape[2:], BF16),
            jax.ShapeDtypeStruct(pack_shape, BF16),
            jax.ShapeDtypeStruct((8, 3 * group_dim), F32),
        ),
        scratch_shapes=[
            low(rows, seq, dim),
            low(model_size, dim, dim),
            low(rows, model_size, group_dim, seq),
            low(rows, model_size, 3 * group_dim, seq),
            f32(rows, seq, dim),
            f32(seq, seq),
            low(2, seq, seq),
            low(2, seq, seq),
            low(dim, rows * seq),
            low(dim, rows * seq),
            low(rows, seq, dim),
            low(*grid_shape),
            low(model_size, 2, PARTS, 2, piece, dim),
            *reduce_scratch(model_size, piece, dim),
            *reduce_scratch(model_size, piece, dim),
            low(2, piece, dim),
            low(2, piece, dim),
            low(piece, dim),
            low(piece, dim),
            low(PARTS, piece, dim),
            low(3, *pack_shape[1:]),
            low(3, *pack_shape[1:]),
            low(others, *pack_shape[2:]),
            f32(model_size, 8, 3 * group_dim),
            f32(4, 8, 3 * group_dim),
            f32(3, 8, 3 * group_dim),
            f32(others, 8, 3 * group_dim),
            low(slots, token_part, dim),
            dma((3, REDUCE_SEMS)),
            dma((3, REDUCE_SEMS)),
            dma((4 + 2 * others,)),
            dma((4 + 2 * others,)),
            dma((3 + others,)),
            dma((3 + others,)),
            dma((row_moves,)),
            dma((row_moves,)),
            dma((7,)),
            *[low(capacity, token_part, dim // CUTS) for _ in range(CUTS)],
        ],
        compiler_params=pltpu.CompilerParams(
            vmem_limit_bytes=VMEM_MOST, collective_id=2, has_side_effects=True
        ),
        name="leave",
    )(
        tags, own, x, gres, w_a, qkv, ctx, lse,
        d_wb.reshape(grid_shape), mat_c, hand, pack.reshape(pack_shape),
    )


def finish_kernel(
    classes, depth, mats_ref, low_ref, bias_ref, *rest
):
    rows_in, rest = rest[: len(rest) - 18 + (1 if depth is None else 0)], rest[len(rest) - 18 + (1 if depth is None else 0) :]
    (
        gqkv_ref, gbqv_ref, gout_ref, gbout_ref, ggain_ref, gshift_ref, gup_ref, gbup_ref, gdown_ref, gbdown_ref,
        gsw1_ref, gsbias_ref, gquery_ref, gsw2_ref, gsw3_ref, gsb3_ref, *rows_out, sums_ref,
    ) = rest
    if depth is not None:
        exit_ref, target_ref, back_ref = rows_in
        flat = slot_of_rows(exit_ref, target_ref, depth)
        for r in range(rows_out[0].shape[0]):
            k = jnp.minimum(jnp.maximum(flat[r], 0), back_ref.shape[0] - 1)
            alive = jnp.where(flat[r] >= 0, 1.0, 0.0)
            rows_out[0][r] = (back_ref[k].astype(F32) * alive).astype(BF16)
    sums_ref[...] = low_ref[...].astype(F32)
    dim, width = gsw1_ref.shape
    group_dim = gout_ref.shape[0]
    b, z = lax.axis_index("batch"), lax.axis_index("mp")
    w2_at, w3_at, small_at, vec_at, bup_at = pack_places(dim, width)
    blocks = dim // width

    def vector(first, row):
        return jnp.concatenate([sums_ref[first + j * 8 + row : first + j * 8 + row + 1] for j in range(blocks)], axis=1)

    def share(value, parts):
        size = value.shape[1] // parts
        return sum(jnp.where(b == i, 1.0, 0.0) * value[:, i * size : (i + 1) * size] for i in range(parts))

    parts = dim // gbup_ref.shape[-1]
    flipped = mats_ref[0].astype(F32).T
    for j in range(3):
        gqkv_ref[j] = flipped[j * group_dim : (j + 1) * group_dim]
    gout_ref[...] = flipped[3 * group_dim :]
    gup_ref[...] = mats_ref[1].astype(F32)
    gdown_ref[...] = mats_ref[2].astype(F32).T
    for n in range(2):
        gbqv_ref[n : n + 1] = share(bias_ref[0:1, 2 * n * group_dim : (2 * n + 1) * group_dim], parts)
    gbout_ref[...] = (vector(vec_at.start, 5)).reshape(dim)
    for n in range(2):
        ggain_ref[n : n + 1] = vector(vec_at.start, n)
        gshift_ref[n : n + 1] = vector(vec_at.start, 2 + n)
    gbdown_ref[...] = (vector(vec_at.start, 4)).reshape(dim)
    ups = [vector(bup_at.start, m) for m in range(dim // group_dim)]
    gbup_ref[...] = (share(sum(jnp.where(z == m, 1.0, 0.0) * ups[m] for m in range(len(ups))), parts)).reshape(gbup_ref.shape[0])
    for j in range(blocks):
        gsw1_ref[j * width : (j + 1) * width] = sums_ref[j * width : (j + 1) * width].T
    gsbias_ref[...] = sums_ref[small_at.start : small_at.start + 2]
    gquery_ref[...] = (sums_ref[small_at.start + 2 : small_at.start + 3]).reshape(width)
    gsb3_ref[...] = (sums_ref[small_at.start + 3 : small_at.start + 4][:, :classes]).reshape(classes)
    gsw2_ref[...] = sums_ref[w2_at]
    gsw3_ref[...] = sums_ref[w3_at][:classes]


def finish(mats, sums, bias, model_size, classes, rows, slot_depth):
    depth, dim = mats.shape[1:]
    width = sums.shape[1]
    group_dim = dim // model_size
    batch_size = dim // depth
    f32 = lambda *shape: jax.ShapeDtypeStruct(shape, F32)
    smem, vmem = pl.BlockSpec(memory_space=pltpu.SMEM), pl.BlockSpec(memory_space=pltpu.VMEM)
    row_shapes = ()
    if rows:
        row_shapes = (jax.ShapeDtypeStruct((rows[0].shape[0],) + rows[2].shape[1:], BF16),)
    return pl.pallas_call(
        functools.partial(finish_kernel, classes, slot_depth if rows else None),
        in_specs=[vmem] * 3 + ([smem, smem, vmem] if rows else []),
        out_specs=[vmem] * (16 + len(row_shapes)),
        out_shape=(
            f32(3, group_dim, depth),
            f32(2, group_dim // batch_size),
            f32(group_dim, depth),
            f32(dim),
            f32(2, dim),
            f32(2, dim),
            f32(depth, dim),
            f32(depth),
            f32(dim, depth),
            f32(dim),
            f32(dim, width),
            f32(2, width),
            f32(width),
            f32(width, width),
            f32(classes, width),
            f32(classes),
            *row_shapes,
        ),
        scratch_shapes=[pltpu.VMEM(sums.shape, F32)],
        compiler_params=pltpu.CompilerParams(vmem_limit_bytes=VMEM_MOST),
        name="finish",
    )(mats, sums, bias, *rows)


def rows_back(grad_x, exit_flag, target, live, slot_depth):
    batch_size, model_size = lax.axis_size("batch"), lax.axis_size("mp")
    own_rows, seq, dim = grad_x.shape
    row_count = exit_flag.shape[0]
    capacity, slot_count = own_rows * model_size, batch_size * slot_depth
    alive_rows = 1 - exit_flag > 0
    same_goal = (target[:, None] == target[None, :]) & alive_rows[:, None] & alive_rows[None, :]
    row_order = jnp.arange(row_count, dtype=jnp.int32)
    slot_in = jnp.sum(
        (same_goal & (row_order[None, :] < row_order[:, None])).astype(jnp.int32), axis=1
    )
    flat_slot = target * slot_depth + slot_in
    send_low = (
        (jnp.arange(slot_count, dtype=jnp.int32)[:, None] == flat_slot[None, :]) & alive_rows[None, :]
    ).astype(BF16)
    live_flat = live.reshape(-1)
    position = jnp.cumsum(live_flat.astype(jnp.int32)) - 1
    pick_low = (
        (jnp.arange(capacity, dtype=jnp.int32)[:, None] == position[None, :]) & (live_flat[None, :] > 0)
    ).astype(BF16)
    mine = lax.all_to_all(grad_x, "mp", split_axis=1, concat_axis=0, tiled=True)
    back = jnp.einsum("ck,csd->ksd", pick_low, mine, preferred_element_type=F32).astype(BF16)
    back = back.reshape((batch_size, slot_depth) + back.shape[1:])
    got = lax.all_to_all(back, "batch", split_axis=0, concat_axis=0, tiled=True)
    got = got.reshape((slot_count,) + got.shape[2:])
    return jnp.einsum("kr,ksd->rsd", send_low, got, preferred_element_type=F32).astype(BF16)


def matrix_sums(grads):
    sums = []
    for grad in grads:
        part = lax.psum_scatter(grad, "mp", scatter_dimension=0, tiled=True)[0]
        part = lax.psum_scatter(part, "batch", scatter_dimension=0, tiled=True)
        sums.append(lax.psum(part, "grp"))
    return sums


def on_device(
    rows_in, segment_ids, pair_labels, pair_mask, exit_flag, target, cot_out,
    w_qkv, b_qv, w_out, b_out, ln_gain, ln_bias, w_up, b_up, w_down, b_down,
    s_w1, s_bias, s_query, s_w2, s_w3, s_b3,
):
    batch_size = lax.axis_size("batch")
    model_size = lax.axis_size("mp")
    row_count, _, model_dim = rows_in.shape
    own_rows = cot_out.shape[0]
    capacity = own_rows * model_size
    slot_depth = (capacity + batch_size - 1) // batch_size
    pair_count = pair_labels.shape[1]
    my_mp = lax.axis_index("mp")
    own, got_tags, vecs, rows_own, w_a, w_b, early, qkv, ctx, lse, xhat_one, rstd_one = enter(
        exit_flag, target, rows_in, segment_ids, pair_labels, pair_mask, w_qkv, w_out, b_qv, b_up, b_out,
        w_up, w_down, own_rows, batch_size, model_size,
    )
    scatter = batch_size == 2
    mixed_out, grad_resid, d_wb, mat_c, hand, pack = ffn_both(
        xhat_one, rstd_one, ln_gain, ln_bias, w_b, w_down, early, vecs, b_down, cot_out, own, pair_count, scatter,
        s_w1, s_bias, s_query, s_w2, s_w3, s_b3,
    )
    if scatter:
        back, mats, sums, bias_sum = leave(
            got_tags, own, rows_own, grad_resid, w_a, qkv, ctx, lse, d_wb, mat_c, hand, pack,
            batch_size, pair_count,
        )
        mats = mats.reshape(3, model_dim // batch_size, model_dim)
        sums = sums.reshape(pack.shape)
    else:
        grad_x, d_wa, bias_part = attn_backward(rows_own, grad_resid, w_a, qkv, ctx, lse, own)
        grad_rows = rows_back(grad_x, exit_flag, target, got_tags[:, :slot_depth, 2 * pair_count], slot_depth)
        whole = (model_size, model_dim, model_dim)
        mats = matrix_sums((d_wa, d_wb.reshape(whole), mat_c.reshape(whole)))
        sums, bias_sum = lax.psum((pack.astype(F32), bias_part[:, 0]), ("grp", "batch", "mp"))
        bias_sum = lax.dynamic_index_in_dim(bias_sum, my_mp, 0)
        mats = jnp.stack(mats)

    (
        g_wqkv, g_bqv, g_wout, g_bout, g_gain, g_shift, g_wup, g_bup, g_wdown, g_bdown,
        g_sw1, g_sbias, g_query, g_sw2, g_sw3, g_sb3, *rows_found,
    ) = finish(
        mats, sums, bias_sum, model_size, s_w3.shape[1], (exit_flag, target, back) if scatter else (), slot_depth
    )
    if scatter:
        grad_rows = rows_found[0]
    return (
        mixed_out, grad_rows, jnp.transpose(g_wqkv, (0, 2, 1)), g_bqv, g_wout, g_bout, g_gain, g_shift, g_wup,
        g_bup, g_wdown, g_bdown, g_sw1, g_sbias, g_query, g_sw2, g_sw3.T, g_sb3,
    )


def solution(mesh):
    return jax.shard_map(
        on_device,
        mesh=mesh,
        in_specs=(
            P(("grp", "batch"), "mp", None),
            P(("grp", "batch"), None),
            P(("grp", "batch"), None),
            P(("grp", "batch"), None),
            P(("grp", "batch")),
            P(("grp", "batch")),
            P(("grp", "batch", "mp"), None, None),
            P(None, None, "mp"),
            P(None, "mp"),
            P("mp", None),
            P(),
            P(),
            P(),
            P(None, "mp"),
            P("mp"),
            P("mp", None),
            P(),
            P(),
            P(),
            P(),
            P(),
            P(),
            P(),
        ),
        out_specs=(
            P(("grp", "batch", "mp"), None, None),
            P(("grp", "batch"), "mp", None),
            P(None, "batch", "mp"),
            P(None, ("mp", "batch")),
            P("mp", "batch"),
            P(),
            P(),
            P(),
            P("batch", "mp"),
            P(("mp", "batch")),
            P("mp", "batch"),
            P(),
            P(),
            P(),
            P(),
            P(),
            P(),
            P(),
        ),
        check_vma=False,
    )
```
